32 devices in a mesh: ens: 2 (over y), space: 4 (over z), tm: 4 (over x, core).
Axes of the slice: x: 2, y: 2, z: 4, core: 2. Of those that a mesh axis runs over, the one named last changes fastest.
Arguments:
- right_side: float32 [8, 4, 16, 8, 720], P(('ens', 'tm'), None, None, 'space'), parts along dimension 0, may hold values from -8 to 8
- error_precision: float32 [4, 4, 16, 8, 720], P('tm', None, None, 'space'), may hold values from 0.5 to 4
- obs_count: int32 [4, 4, 16, 8, 720], P('tm', None, None, 'space'), may hold values from 0 to 3
- background_wind: float32 [2, 16, 8, 720], P(None, None, 'space'), may hold values from -0.4 to 0.4
- wave_speed: float32 [16], replicated, may hold values from 0.3 to 1.2
- tracer_coupling: float32 [16], replicated, may hold values from 0.2 to 1
Outputs:
- solution_field: float32 [8, 4, 16, 8, 720], P(('ens', 'tm'), None, None, 'space'), parts along dimension 0
- residual: float32 [8, 4, 16, 8, 720], P(('ens', 'tm'), None, None, 'space'), parts along dimension 0
The draws below stay inside these ranges and needn't reach their ends.
There are 2 independent parts, one for each index of `ens`. The reference program is written for one: setup_inputs(seed, part) draws one part's arguments, and reference() takes and returns one part's arrays. A program takes and returns all parts, laid end to end along the dimension named above; an argument that names none is the same for every part. Nothing has to cross between parts.
All inputs are finite; a program needn't handle non-finite values.
Results may differ from the reference program's by a relative error of at most 0.0001.
Values sent between devices are 32-bit elements; how exact they have to be, the bound alone decides.
No kernel may reach another device: no remote copies, remote signals or barrier semaphores. Data moves between devices by JAX's collectives and lax.ppermute only.
A program may use at most 64 MiB of HBM per device.

```python
import math
import jax
import jax.numpy as jnp
from jax import lax

NLON = 720
LEV = 16
STEPS = 2
ITERS = 2
NLAT = 8
SUBWIN = 4


def plant(array, key, least, high):
    index_at = [jax.random.randint(jax.random.fold_in(key, axis), (), 0, length) for axis, length in enumerate(array.shape)]
    longest = array.shape.index(max(array.shape))
    beside = index_at[:longest] + [(index_at[longest] + 1) % array.shape[longest]] + index_at[longest + 1:]
    return array.at[tuple(index_at)].set(least).at[tuple(beside)].set(high)


def block_levels(stream_key, shape, shards, smallest, largest):
    gain, own = 1.0, jax.random.fold_in(stream_key, 6)
    for axis_at, parts in shards:
        heights = jnp.exp(jax.random.uniform(jax.random.fold_in(own, axis_at), (parts,), jnp.float32, smallest / len(shards), largest / len(shards)))
        gain = gain * jnp.repeat(heights, shape[axis_at] // parts).reshape([-1 if axis == axis_at else 1 for axis in range(len(shape))])
    return gain


def bell_draw(rng, dims, scale, most, cuts=(), dtype=jnp.bfloat16):
    result = jax.random.normal(rng, dims, jnp.float32) * scale
    if len(cuts) > 0:
        result = block_levels(rng, dims, cuts, -0.22, 0.18) * result
    return jnp.clip(result, min=-most, max=most).astype(dtype)


def setup_inputs(seed: int = 0, part: int = 0) -> dict:
    keys = jax.random.split(jax.random.key(seed), 7)
    part_splits = jax.random.split(jax.random.fold_in(keys[6], part), 7)
    right_side = bell_draw(part_splits[0], (SUBWIN, 4, LEV, NLAT, NLON), 1.0, 8.0, ((0, 4), (3, 4)), jnp.float32)
    error_precision = jnp.clip(jnp.exp(math.log(4.0) - 2.0794415 * jax.random.uniform(keys[1], (SUBWIN, 4, LEV, NLAT, NLON), jnp.float32) ** block_levels(keys[1], (SUBWIN, 4, LEV, NLAT, NLON), ((0, 4), (3, 4)), -0.2, 0.2)), 0.5, 4.0)
    obs_count = plant(jax.random.randint(keys[2], (SUBWIN, 4, LEV, NLAT, NLON), 0, 4), jax.random.fold_in(keys[2], 1), 0, 3).astype(jnp.int32)
    background_wind = jnp.clip(jax.random.uniform(keys[3], (2, LEV, NLAT, NLON), jnp.float32, -0.4, 0.4) * block_levels(keys[3], (2, LEV, NLAT, NLON), ((2, 4),), -0.4, 0.0), -0.4, 0.4)
    wave_speed = jnp.clip(jax.random.uniform(keys[4], (LEV,), jnp.float32, 0.3, 1.2), 0.3, 1.2)
    tracer_coupling = jnp.clip(jax.random.uniform(keys[5], (LEV,), jnp.float32, 0.2, 1.0), 0.2, 1.0)
    return {"right_side": right_side, "error_precision": error_precision, "obs_count": obs_count, "background_wind": background_wind, "wave_speed": wave_speed, "tracer_coupling": tracer_coupling}


diffusion = 0.1


def along_x(field):
    return 0.5 * (jnp.roll(field, -1, axis=-1) - jnp.roll(field, 1, axis=-1))


def padded_rows(field):
    widths = [(0, 0)] * (field.ndim - 2) + [(1, 1), (0, 0)]
    return jnp.pad(field, widths)


def along_y(field):
    padded = padded_rows(field)
    return 0.5 * (padded[..., 2:, :] - padded[..., :-2, :])


def laplace(field):
    padded = padded_rows(field)
    return (jnp.roll(field, -1, axis=-1) + jnp.roll(field, 1, axis=-1)
            + padded[..., 2:, :] + padded[..., :-2, :] - 4.0 * field)


def tangent_step(state, speed_col, couple_col, wind_east, wind_north):
    height, east, north, tracer = state[0], state[1], state[2], state[3]
    east_new = east - speed_col * along_x(height)
    north_new = north - speed_col * along_y(height)
    height_new = height - speed_col * (along_x(east_new) + along_y(north_new))
    tracer_new = (tracer - wind_east * along_x(tracer) - wind_north * along_y(tracer)
                  + diffusion * laplace(tracer) + couple_col * height_new)
    return jnp.stack([height_new, east_new, north_new, tracer_new], axis=0)


def adjoint_step(state, speed_col, couple_col, wind_east, wind_north):
    height, east, north, tracer = state[0], state[1], state[2], state[3]
    height_mix = height + couple_col * tracer
    east_new = east + speed_col * along_x(height_mix)
    north_new = north + speed_col * along_y(height_mix)
    height_new = height_mix + speed_col * (along_x(east_new) + along_y(north_new))
    tracer_new = (tracer + along_x(wind_east * tracer) + along_y(wind_north * tracer)
                  + diffusion * laplace(tracer))
    return jnp.stack([height_new, east_new, north_new, tracer_new], axis=0)


def propagate(fields, step_fn, speed_col, couple_col, wind_east, wind_north):
    def single(state):
        def advance(index, current):
            return step_fn(current, speed_col, couple_col, wind_east, wind_north)
        return lax.fori_loop(0, STEPS, advance, state)
    return lax.map(single, fields)


def operate(direction, error_precision, observed, speed_col, couple_col, wind_east, wind_north):
    moved = propagate(direction, tangent_step, speed_col, couple_col, wind_east, wind_north)
    previous = jnp.concatenate([jnp.zeros_like(moved[:1]), moved[:-1]], axis=0)
    weighted = error_precision * (direction - previous)
    back = propagate(weighted, adjoint_step, speed_col, couple_col, wind_east, wind_north)
    following = jnp.concatenate([back[1:], jnp.zeros_like(back[:1])], axis=0)
    return weighted - following + observed * direction


def reference(right_side, error_precision, obs_count, background_wind, wave_speed, tracer_coupling):
    speed_col = wave_speed[:, None, None]
    couple_col = tracer_coupling[:, None, None]
    wind_east = background_wind[0]
    wind_north = background_wind[1]
    observed = obs_count.astype(jnp.float32)
    solution_field = jnp.zeros_like(right_side)
    residual, direction = right_side, right_side
    norm_now = jnp.sum(residual * residual)
    for step in range(ITERS):
        image = operate(direction, error_precision, observed, speed_col, couple_col, wind_east, wind_north)
        alpha = norm_now / jnp.sum(direction * image)
        solution_field = solution_field + alpha * direction
        residual = residual - alpha * image
        norm_next = jnp.sum(residual * residual)
        direction = residual + (norm_next / norm_now) * direction
        norm_now = norm_next
    return solution_field, residual
```

```python
import jax
import jax.numpy as jnp
from jax import lax
from jax.experimental import pallas as pl
from jax.experimental.pallas import tpu as pltpu
from jax.sharding import PartitionSpec as P

STEPS = 2
ITERS = 2


diffusion = 0.1


LANES = 128
ROWS = 8
HALO = 24


def tiles_of(lon):
    return -(-lon // LANES)


def pack_kernel(lon, b_ref, e_ref, o_ref, w_ref, out_ref):
    fields, levels, share, _ = b_ref.shape
    full = lon // LANES
    rest = lon - full * LANES
    over = LANES - rest
    half = out_ref.shape[0] // levels // share
    group = 3 * full + 2
    spare = fields * group
    mine = lax.axis_index("tm")
    lower = lax.rem(mine, 2) == 0
    for level in range(levels):
        base = level * half * share

        def put(row, value, lo, hi):
            out_ref[pl.ds(base + row, share, stride=half), lo:hi] = value

        for f in range(fields):
            parts = [b_ref[f, level], e_ref[f, level], o_ref[f, level].astype(jnp.float32)]
            for a, part in enumerate(parts):
                for c in range(full):
                    put(f * group + a * full + c, part[:, c * LANES : (c + 1) * LANES], 0, LANES)
            tails = [part[:, full * LANES :] for part in parts]
            put(f * group + 3 * full, jnp.concatenate([tails[0], tails[2][:, :over]], axis=1), 0, LANES)
            put(f * group + 3 * full + 1, jnp.concatenate([tails[1], tails[2][:, over:]], axis=1), 0, 2 * rest - over)
        wind = w_ref[mine // 2, level]
        wind = jnp.where(lower, wind[0:1], wind[1:2])
        for c in range(full + 1):
            row = base + (c // 4) * half + spare + c % 4
            if c < full:
                out_ref[pl.ds(row, 1), :] = wind[:, c * LANES : (c + 1) * LANES]
            else:
                out_ref[pl.ds(row, 1), 0:rest] = wind[:, c * LANES :]


def layer_kernel(lon, subwins, in_ref, speed_ref, couple_ref, out_ref, wind_ref):
    fields = 4
    full = lon // LANES
    rest = lon - full * LANES
    over = LANES - rest
    tiles = full + 1
    half = in_ref.shape[0] // (subwins * ROWS)
    half_out = out_ref.shape[0] // (subwins * ROWS)
    group = 3 * full + 2
    spare = fields * group
    layer = lax.axis_index("tm") * lax.axis_size("space") + lax.axis_index("space")
    speed = 0.5 * speed_ref[layer]
    couple = couple_ref[layer]
    lane = lax.broadcasted_iota(jnp.int32, (ROWS, LANES), 1)
    row = lax.broadcasted_iota(jnp.int32, (ROWS, LANES), 0)

    def load(t, k):
        return in_ref[pl.ds(t * ROWS * half + k, ROWS, stride=half), :]

    def back(x, by):
        return [
            jnp.where(lane < by, before, here)
            for before, here in _pairs([pltpu.roll(v, by, 1) for v in x], -1)
        ]

    def ahead(x, by):
        return [
            jnp.where(lane >= LANES - by, after, here)
            for after, here in _pairs([pltpu.roll(v, LANES - by, 1) for v in x], 1)
        ]

    def up(x, by):
        return [pltpu.roll(v, ROWS - by, 0) for v in x]

    def down(x, by):
        return [pltpu.roll(v, by, 0) for v in x]

    def wrapped(x):
        first, last = x[0], x[-1]
        tail = jnp.where(lane < rest + HALO, pltpu.roll(first, rest, 1), pltpu.roll(last, LANES - rest, 1))
        return x[:-1] + [jnp.where(lane < rest, last, tail)]

    def staggered(f, x):
        if f == 1:
            return ahead(x, 1)
        if f == 2:
            return up(x, 1)
        return x

    def aligned(f, x):
        if f == 1:
            return back(x, 1)
        if f == 2:
            return down(x, 1)
        return x

    def fetch(t):
        got = [[], [], []]
        for f in range(fields):
            at = f * group
            one = load(t, at + 3 * full)
            two = load(t, at + 3 * full + 1)
            three = jnp.where(lane < over, pltpu.roll(one, over, 1), pltpu.roll(two, 2 * over, 1))
            for a, tail in enumerate((one, two, three)):
                x = [load(t, at + a * full + c) for c in range(full)] + [tail]
                got[a].append(staggered(f, wrapped(x)))
        return got

    for comp in range(2):
        for r in range(2):
            for c in range(tiles):
                at = (2 * comp + r) * ROWS * half + (c // 4) * half + spare + c % 4
                wind_ref[comp, c, pl.ds(r, ROWS // 2, stride=2), :] = in_ref[
                    pl.ds(at, ROWS // 2, stride=2 * half), :
                ]
    east = wrapped([wind_ref[0, c] for c in range(tiles)])
    north = wrapped([wind_ref[1, c] for c in range(tiles)])
    east_m = [diffusion - 0.5 * v for v in east]
    east_p = [diffusion + 0.5 * v for v in east]
    north_m = [jnp.where(row == ROWS - 1, 0.0, diffusion - 0.5 * v) for v in north]
    north_p = [jnp.where(row == 0, 0.0, diffusion + 0.5 * v) for v in north]
    stay = 1.0 - 4.0 * diffusion
    grad_p = jnp.where(row == ROWS - 2, 0.0, speed)
    grad_m = jnp.where(row == ROWS - 1, 0.0, speed)
    div_p = jnp.where(row == ROWS - 1, 0.0, speed)
    div_m = jnp.where(row == 0, 0.0, speed)

    def tangent(state):
        h, u, v, q = state
        u = [a - speed * (n - m) for a, n, m in zip(u, ahead(h, 2), h)]
        v = [a - (grad_p * n - grad_m * m) for a, n, m in zip(v, up(h, 2), h)]
        h = [
            a - (speed * (p - m) + (div_p * n - div_m * s))
            for a, p, m, n, s in zip(h, u, back(u, 2), v, down(v, 2))
        ]
        q = [
            stay * a + (em * e + ep * w) + (nm * n + np * s) + couple * p
            for a, em, e, ep, w, nm, n, np, s, p in zip(
                q, east_m, ahead(q, 1), east_p, back(q, 1), north_m, up(q, 1), north_p, down(q, 1), h
            )
        ]
        return [h, u, v, q]

    def adjoint(state):
        h, u, v, q = state
        h = [a + couple * b for a, b in zip(h, q)]
        u = [a + speed * (n - m) for a, n, m in zip(u, ahead(h, 2), h)]
        v = [a + (grad_p * n - grad_m * m) for a, n, m in zip(v, up(h, 2), h)]
        h = [
            a + (speed * (p - m) + (div_p * n - div_m * s))
            for a, p, m, n, s in zip(h, u, back(u, 2), v, down(v, 2))
        ]
        e = ahead([a * b for a, b in zip(east_p, q)], 1)
        w = back([a * b for a, b in zip(east_m, q)], 1)
        n = up([a * b for a, b in zip(north_p, q)], 1)
        s = down([a * b for a, b in zip(north_m, q)], 1)
        q = [stay * a + (b + c) + (d + f) for a, b, c, d, f in zip(q, e, w, n, s)]
        return [h, u, v, q]

    def each(fn, *states):
        return [[fn(*vals) for vals in zip(*xs)] for xs in zip(*states)]

    def operate(p, precision, observed):
        weighted = []
        for t in range(subwins):
            change = p[t]
            if t > 0:
                moved = p[t - 1]
                for _ in range(STEPS):
                    moved = tangent(moved)
                change = each(lambda a, b: a - b, change, moved)
            weighted.append(each(lambda a, b: a * b, precision[t], change))
        image = []
        for t in range(subwins):
            out = each(lambda w, o, d: w + o * d, weighted[t], observed[t], p[t])
            if t + 1 < subwins:
                moved = weighted[t + 1]
                for _ in range(STEPS):
                    moved = adjoint(moved)
                out = each(lambda a, b: a - b, out, moved)
            image.append(out)
        return image

    got = [fetch(t) for t in range(subwins)]
    b = [g[0] for g in got]
    precision = [g[1] for g in got]
    observed = [g[2] for g in got]
    one = operate(b, precision, observed)
    two = operate(one, precision, observed)

    def flat(x):
        return [(c, v) for state in x for field in state for c, v in enumerate(field)]

    fb, f1, f2 = flat(b), flat(one), flat(two)

    def total(terms):
        inner, edge = None, None
        for c, v in terms:
            if c < full:
                inner = v if inner is None else inner + v
            else:
                edge = v if edge is None else edge + v
        both = inner + jnp.where(lane < rest, edge, 0.0)
        return jnp.sum(both, axis=(0, 1), keepdims=True)

    def dot(x, y):
        return total([(c, v * w) for (c, v), (_, w) in zip(x, y)])

    bb, b1, s11, s12 = dot(fb, fb), dot(fb, f1), dot(f1, f1), dot(f1, f2)
    step = jnp.where(b1 > 0.0, bb / jnp.where(b1 > 0.0, b1, 1.0), 0.0)
    grow = jnp.where(bb > 0.0, step * step * s11 / jnp.where(bb > 0.0, bb, 1.0) - 1.0, 0.0)
    step_t = jnp.broadcast_to(step, (ROWS, LANES))
    grow_t = jnp.broadcast_to(grow, (ROWS, LANES))
    res = [(c, v - step_t * w) for (c, v), (_, w) in zip(fb, f1)]
    mov = [(c, v + grow_t * w) for (c, v), (_, w) in zip(res, fb)]
    img = [(c, (v - step_t * w) + grow_t * v) for (c, v), (_, w) in zip(f1, f2)]
    sums = [step, grow, bb, b1, s11, s12, dot(res, res), dot(res, f1), dot(mov, img), dot(mov, f2), dot(mov, f1)]
    for t in range(subwins):
        for a, x in enumerate((one, two)):
            for f in range(fields):
                y = aligned(f, x[t][f])
                for c in range(tiles):
                    at = (a * fields + f) * tiles + c
                    v = y[c]
                    if c == full:
                        i = a * fields + f
                        even = sums[i]
                        odd = sums[i + 8] if i + 8 < len(sums) else jnp.zeros_like(even)
                        v = jnp.where(lane < rest, v, jnp.where(row % 2 == 0, even, odd))
                    out_ref[pl.ds(t * ROWS * half_out + at, ROWS, stride=half_out), :] = v


def _pairs(x, by):
    n = len(x)
    return [(x[(i + by) % n], x[i]) for i in range(n)]


def finish_kernel(lon, b_ref, in_ref, x_ref, r_ref):
    fields, levels, share, _ = b_ref.shape
    full = lon // LANES
    rest = lon - full * LANES
    tiles = full + 1
    half = in_ref.shape[0] // (levels * share)

    def sums(i):
        at = (i // 8) * half + (i % 8) * tiles + full
        return in_ref[pl.ds(at, levels, stride=half * share), :]

    step, grow, bb, b1, s11, s12, rr, r1, mi, m2, m1 = [sums(i) for i in range(11)]

    def total(x):
        return jnp.sum(x, axis=0, keepdims=True)

    norm_0 = total(bb)
    alpha_0 = norm_0 / total(b1)
    d = step - alpha_0
    norm_1 = total(rr + d * (2.0 * r1 + d * s11))
    beta = norm_1 / norm_0
    g = beta - grow
    curve = total(mi + 2.0 * (d * m2 + g * m1) + d * (d * s12 + 2.0 * g * s11) + g * g * b1)
    alpha_1 = norm_1 / curve
    first = alpha_0 + alpha_1 * (1.0 + beta)
    second = alpha_0 * alpha_1
    first = jnp.broadcast_to(first[:, rest : rest + 1], (share, LANES))
    second = jnp.broadcast_to(second[:, rest : rest + 1], (share, LANES))
    for level in range(levels):
        base = level * half * share
        for f in range(fields):
            b = b_ref[f, level]
            for c in range(tiles):
                width = LANES if c < full else rest
                cols = pl.ds(c * LANES, width)
                one = in_ref[pl.ds(base + f * tiles + c, share, stride=half), :][:, :width]
                two = in_ref[pl.ds(base + (fields + f) * tiles + c, share, stride=half), :][:, :width]
                part = b[:, c * LANES : c * LANES + width]
                x_ref[f, level, :, cols] = first[:, :width] * part - second[:, :width] * one
                r_ref[f, level, :, cols] = (part - first[:, :width] * one) + second[:, :width] * two


def by_layer(right_side, error_precision, obs_count, background_wind, wave_speed, tracer_coupling):
    _, fields, levels, share, lon = right_side.shape
    subwins = lax.axis_size("tm")
    full = lon // LANES
    half = fields * (3 * full + 2) + 4
    half_out = 2 * fields * (full + 1)
    vmem = pl.BlockSpec(memory_space=pltpu.VMEM)
    smem = pl.BlockSpec(memory_space=pltpu.SMEM)
    params = pltpu.CompilerParams(vmem_limit_bytes=48 * 1024 * 1024)
    state = (fields, levels, share, lon)

    def exchange(x):
        x = x.reshape(levels, -1, LANES)
        return lax.all_to_all(x, ("tm", "space"), 0, 0, tiled=True).reshape(-1, LANES)

    b = right_side.reshape(state)
    with jax.named_scope("pack"):
        packed = pl.pallas_call(
            lambda *refs: pack_kernel(lon, *refs),
            out_shape=jax.ShapeDtypeStruct((levels * share * half, LANES), jnp.float32),
            in_specs=[vmem] * 4,
            out_specs=vmem,
            compiler_params=params,
        )(b, error_precision.reshape(state), obs_count.reshape(state), background_wind)
    packed = exchange(packed)
    with jax.named_scope("layer"):
        images = pl.pallas_call(
            lambda *refs: layer_kernel(lon, subwins, *refs),
            out_shape=jax.ShapeDtypeStruct((levels * share * half_out, LANES), jnp.float32),
            in_specs=[vmem, smem, smem],
            out_specs=vmem,
            scratch_shapes=[pltpu.VMEM((2, full + 1, ROWS, LANES), jnp.float32)],
            compiler_params=params,
        )(packed, wave_speed, tracer_coupling)
    images = exchange(images)
    with jax.named_scope("finish"):
        x, r = pl.pallas_call(
            lambda *refs: finish_kernel(lon, *refs),
            out_shape=[jax.ShapeDtypeStruct(state, jnp.float32)] * 2,
            in_specs=[vmem] * 2,
            out_specs=[vmem] * 2,
            compiler_params=params,
        )(b, images)
    return x.reshape(right_side.shape), r.reshape(right_side.shape)


def fits_by_layer(mesh, shape):
    space, tm = mesh.shape["space"], mesh.shape["tm"]
    subwins, fields, levels, lats, lon = shape
    rest = lon % LANES
    return (
        subwins == mesh.shape["ens"] * tm
        and (tm, space, fields, lats) == (4, 4, 4, ROWS)
        and levels == space * tm
        and lon >= 2 * LANES
        and 2 * (LANES - rest) <= LANES
        and LANES - rest >= 2 * HALO
        and lon // LANES <= 7
    )


def extended_2(cells, sides, width):
    for axis, dim in sides:
        count = lax.axis_size(axis)
        ends = count - 1
        head = lax.slice_in_dim(cells, 0, width, axis=dim)
        tail = lax.slice_in_dim(cells, cells.shape[dim] - width, cells.shape[dim], axis=dim)
        cells = jnp.concatenate(
            [
                lax.ppermute(tail, axis, [(i, (i + 1) % count) for i in range(ends)]),
                cells,
                lax.ppermute(head, axis, [((i + 1) % count, i) for i in range(ends)]),
            ],
            axis=dim,
        )
    return cells


def shifted(value, axis, by):
    peers = lax.axis_size(axis)
    pairs = [(i, i + by) for i in range(peers) if 0 <= i + by < peers]
    return lax.ppermute(value, axis, pairs)


def along_x(field):
    return 0.5 * (jnp.roll(field, -1, axis=-1) - jnp.roll(field, 1, axis=-1))


def second_x(field):
    return jnp.roll(field, -1, axis=-1) + jnp.roll(field, 1, axis=-1) - 2.0 * field


def along_y(extended):
    return 0.5 * (extended[..., 2:, :] - extended[..., :-2, :])


def trimmed(field, count):
    if count == 0:
        return field
    return field[..., count : field.shape[-2] - count, :]


def row_valid(lat_rows):
    first_row = lax.axis_index("space") * lat_rows - 4
    row_total = lat_rows * lax.axis_size("space")
    global_rows = first_row + jnp.arange(lat_rows + 8, dtype=jnp.int32)
    inside = jnp.logical_and(global_rows >= 0, global_rows < row_total)
    return inside.astype(jnp.float32)[:, None]


def tangent_core(state, margin, coefs):
    speed_col, couple_col, winds, have, valid = coefs
    height, east, north, tracer = (state[:, 0], state[:, 1], state[:, 2], state[:, 3])
    east_mid = east - speed_col * along_x(height)
    north_mid = (trimmed(north, 1) - speed_col * along_y(height)) * trimmed(valid, 5 - margin)
    height_new = trimmed(height, 2) - speed_col * (
        along_x(trimmed(east_mid, 2)) + along_y(north_mid)
    )
    tracer_one = trimmed(tracer, 1)
    inner = trimmed(tracer, 2)
    tracer_lap = second_x(inner) + tracer_one[..., 2:, :] + tracer_one[..., :-2, :] - 2.0 * inner
    wind_east = trimmed(winds[0], have - margin + 2)
    wind_north = trimmed(winds[1], have - margin + 2)
    tracer_new = (
        inner
        - wind_east * along_x(inner)
        - wind_north * along_y(tracer_one)
        + diffusion * tracer_lap
        + couple_col * height_new
    )
    result = jnp.stack(
        [height_new, trimmed(east_mid, 2), trimmed(north_mid, 1), tracer_new], axis=1
    )
    return result * trimmed(valid, 6 - margin)


def adjoint_core(state, margin, coefs):
    speed_col, couple_col, winds, have, valid = coefs
    height, east, north, tracer = (state[:, 0], state[:, 1], state[:, 2], state[:, 3])
    height_mix = height + couple_col * tracer
    east_mid = east + speed_col * along_x(height_mix)
    north_mid = (trimmed(north, 1) + speed_col * along_y(height_mix)) * trimmed(valid, 5 - margin)
    height_new = trimmed(height_mix, 2) + speed_col * (
        along_x(trimmed(east_mid, 2)) + along_y(north_mid)
    )
    tracer_one = trimmed(tracer, 1)
    inner = trimmed(tracer, 2)
    tracer_lap = second_x(inner) + tracer_one[..., 2:, :] + tracer_one[..., :-2, :] - 2.0 * inner
    wind_east = trimmed(winds[0], have - margin + 2)
    wind_north = trimmed(winds[1], have - margin + 1)
    tracer_new = (
        inner
        + along_x(wind_east * inner)
        + along_y(wind_north * tracer_one)
        + diffusion * tracer_lap
    )
    result = jnp.stack(
        [height_new, trimmed(east_mid, 2), trimmed(north_mid, 1), tracer_new], axis=1
    )
    return result * trimmed(valid, 6 - margin)


def rebuild(state, sent):
    widths = [(0, 0)] * (state.ndim - 3) + [(2, 2), (0, 0)]
    east_wide = jnp.pad(state[:, 1], widths)
    return jnp.stack([sent[:, 0], east_wide, sent[:, 1], sent[:, 2]], axis=1)


def tangent_near(state):
    picked = jnp.stack([state[:, 0], state[:, 2], state[:, 3]], axis=1)
    sent = extended_2(picked, (("space", 3),), 2)
    return rebuild(state, sent)


def adjoint_near(state):
    picked = jnp.stack([state[:, 0], state[:, 2], state[:, 3]], axis=1)
    sent = extended_2(picked, (("space", 3),), 2)
    return rebuild(state, sent)


def propagate(fields, step_core, near_fn, coefs):
    current = fields
    for step in range(STEPS):
        current = step_core(near_fn(current), 2, coefs)
    return current


def operate(direction, error_precision, observed, coefs):
    moved = propagate(direction, tangent_core, tangent_near, coefs)
    incoming = shifted(moved, "tm", 1)
    previous = jnp.concatenate([incoming, moved[:-1]], axis=0)
    weighted = error_precision * (direction - previous)
    back = propagate(weighted, adjoint_core, adjoint_near, coefs)
    arriving = shifted(back, "tm", -1)
    following = jnp.concatenate([back[1:], arriving], axis=0)
    return weighted - following + observed * direction


def squares(residual):
    return lax.psum(jnp.sum(residual * residual), ("space", "tm"))


def on_device(right_side, error_precision, obs_count, background_wind, wave_speed, tracer_coupling):
    lat_rows = right_side.shape[3]
    valid = row_valid(lat_rows)
    winds = extended_2(background_wind, (("space", 2),), 1)
    have = 1
    coefs = (wave_speed[:, None, None], tracer_coupling[:, None, None], winds, have, valid)
    observed = obs_count.astype(jnp.float32)
    solution_field = jnp.zeros_like(right_side)
    residual = right_side
    direction = right_side
    norm_now = squares(residual)
    for step in range(ITERS):
        image = operate(direction, error_precision, observed, coefs)
        alpha = norm_now / lax.psum(jnp.sum(direction * image), ("space", "tm"))
        solution_field = solution_field + alpha * direction
        residual = residual - alpha * image
        norm_next = squares(residual)
        direction = residual + norm_next / norm_now * direction
        norm_now = norm_next
    return (solution_field, residual)


def solution(mesh):
    def run(right_side, *others):
        body = by_layer if fits_by_layer(mesh, right_side.shape) else on_device
        return jax.shard_map(
            body,
            mesh=mesh,
            in_specs=(
                P(("ens", "tm"), None, None, "space", None),
                P("tm", None, None, "space", None),
                P("tm", None, None, "space", None),
                P(None, None, "space", None),
                P(),
                P(),
            ),
            out_specs=(
                P(("ens", "tm"), None, None, "space", None),
                P(("ens", "tm"), None, None, "space", None),
            ),
            check_vma=False,
        )(right_side, *others)

    return run
```

```python
import jax
import jax.numpy as jnp
from jax import lax
from jax.experimental import pallas as pl
from jax.experimental.pallas import tpu as pltpu
from jax.sharding import PartitionSpec as P

STEPS = 2
ITERS = 2


diffusion = 0.1


LANES = 128
ROWS = 8
TILES = 3
REACH = 4
FIELDS = 4
ROWS_IN = FIELDS * TILES * 2 + 2
ROWS_OUT = FIELDS * TILES * 2


def merge_lanes(lon):
    core = lon // 2
    return (core + 3 * REACH) % LANES, (core - 3 * REACH) % LANES


def pack_kernel(lon, merges, b_hbm, e_hbm, o_hbm, w_hbm, out_ref, b_ref, e_ref, o_ref, w_ref, sems):
    _, levels, share, _ = b_ref.shape
    copies = [
        pltpu.make_async_copy(src, dst, sems.at[i])
        for i, (src, dst) in enumerate(((w_hbm, w_ref), (b_hbm, b_ref), (e_hbm, e_ref), (o_hbm, o_ref)))
    ]
    for copy in copies:
        copy.start()
    full = lon // LANES
    rest = lon - full * LANES
    member = lax.axis_index("ens")
    first_member = member == 0
    turn = lax.axis_index("tm") * 2 + member
    lane = lax.broadcasted_iota(jnp.int32, (share, LANES), 1)

    def put(half, level, row, value):
        base = (half * levels + level) * share * ROWS_IN
        out_ref[pl.ds(base + row, share, stride=ROWS_IN), :] = value

    def windows(x):
        tiles = [x[:, c * LANES : (c + 1) * LANES] for c in range(full)]
        tail = jnp.concatenate([x[:, full * LANES :], x[:, : LANES - rest]], axis=1)
        ahead = x[:, lon - LANES :]
        ends = ((tiles[2], ahead), (tail, tiles[2]))
        halves = []
        for half, ((last, before), merge) in enumerate(zip(ends, merges)):
            merged = jnp.where(lane < merge, last, before)
            extra = jnp.where(lane < merge, before, last)
            halves.append((tiles[3 * half], tiles[3 * half + 1], merged, extra))
        return halves

    copies[0].wait()
    for level in range(levels):
        east, north = windows(w_ref[0, level]), windows(w_ref[1, level])
        for half in range(2):
            picks = list(east[half][:3]) + list(north[half][:3]) + [east[half][3], north[half][3]]
            value = picks[0]
            for i in range(1, len(picks)):
                value = jnp.where(turn == i, picks[i], value)
            put(half, level, ROWS_IN - 1, value)
    copies[1].wait()
    for level in range(levels):
        extras = [None, None]
        for f in range(FIELDS):
            for half, got in enumerate(windows(b_ref[f, level])):
                for c in range(TILES):
                    put(half, level, f * TILES + c, got[c])
                moved = got[3] if f == 0 else pltpu.roll(got[3], LANES - 2 * REACH * f, 1)
                edge = merges[half] + REACH - 2 * REACH * f
                extras[half] = moved if f == 0 else jnp.where(lane < edge, moved, extras[half])
        for half in range(2):
            put(half, level, ROWS_IN - 2, extras[half])
    copies[2].wait()
    copies[3].wait()
    for level in range(levels):
        for f in range(FIELDS):
            shared = jnp.where(first_member, e_ref[f, level], o_ref[f, level].astype(jnp.float32))
            for half, got in enumerate(windows(shared)):
                for c in range(TILES):
                    put(half, level, (FIELDS + f) * TILES + c, got[c])


def layer_kernel(lon, merges, subwins, in_ref, speed_ref, couple_ref, out_ref):
    layer = lax.axis_index("tm") * lax.axis_size("space") + lax.axis_index("space")
    half = lax.axis_index("ens")
    speed = 0.5 * speed_ref[layer]
    couple = couple_ref[layer]
    lane = lax.broadcasted_iota(jnp.int32, (ROWS, LANES), 1)
    row = lax.broadcasted_iota(jnp.int32, (ROWS, LANES), 0)
    below = lane < jnp.where(half == 0, merges[0], merges[1])
    free_lo = jnp.where(half == 0, merges[0] - 3 * REACH, merges[1] - 3 * REACH)
    free = jnp.logical_and(lane >= free_lo, lane < free_lo + 6 * REACH)

    def load(member, t, k):
        return in_ref[pl.ds((member * subwins + t) * ROWS * ROWS_IN + k, ROWS, stride=ROWS_IN), :]

    def back(x, by):
        moved = [pltpu.roll(v, by, 1) for v in x]
        return [jnp.where(lane < by, moved[i - 1], v) for i, v in enumerate(moved)]

    def ahead(x, by):
        moved = [pltpu.roll(v, LANES - by, 1) for v in x]
        return [jnp.where(lane >= LANES - by, moved[(i + 1) % len(x)], v) for i, v in enumerate(moved)]

    def up(x, by):
        return [pltpu.roll(v, ROWS - by, 0) for v in x]

    def down(x, by):
        return [pltpu.roll(v, by, 0) for v in x]

    def staggered(f, x):
        if f == 1:
            return ahead(x, 1)
        if f == 2:
            return up(x, 1)
        return x

    def aligned(f, x):
        if f == 1:
            return back(x, 1)
        if f == 2:
            return down(x, 1)
        return x

    def widened(x, extra):
        return x[:2] + [jnp.where(below, x[2], extra), jnp.where(below, extra, x[2])]

    def narrowed(x):
        return x[:2] + [jnp.where(below, x[2], x[3])]

    def fields_of(member, t, at):
        return [[load(member, t, (at + f) * TILES + c) for c in range(TILES)] for f in range(FIELDS)]

    def extras_of(member, t):
        packed = load(member, t, ROWS_IN - 2)
        return [packed] + [pltpu.roll(packed, 2 * REACH * f, 1) for f in range(1, FIELDS)]

    def stag(state):
        return [staggered(f, x) for f, x in enumerate(state)]

    def wind(turn):
        return load(turn % 2, turn // 2, ROWS_IN - 1)

    stay = 1.0 - 4.0 * diffusion
    grad_p = jnp.where(row == ROWS - 2, 0.0, speed)
    grad_m = jnp.where(row == ROWS - 1, 0.0, speed)
    div_p = jnp.where(row == ROWS - 1, 0.0, speed)
    div_m = jnp.where(row == 0, 0.0, speed)

    def coefficients(east, north):
        return (
            [diffusion - 0.5 * v for v in east],
            [diffusion + 0.5 * v for v in east],
            [jnp.where(row == ROWS - 1, 0.0, diffusion - 0.5 * v) for v in north],
            [jnp.where(row == 0, 0.0, diffusion + 0.5 * v) for v in north],
        )

    east, north = [wind(i) for i in range(3)], [wind(3 + i) for i in range(3)]
    narrow = coefficients(east, north)
    wide = coefficients(widened(east, wind(6)), widened(north, wind(7)))

    def tangent(state, coefs):
        h, u, v, q = state
        u = [a - speed * (n - m) for a, n, m in zip(u, ahead(h, 2), h)]
        v = [a - (grad_p * n - grad_m * m) for a, n, m in zip(v, up(h, 2), h)]
        h = [
            a - (speed * (p - m) + (div_p * n - div_m * s))
            for a, p, m, n, s in zip(h, u, back(u, 2), v, down(v, 2))
        ]
        q = [
            stay * a + (em * e + ep * w) + (nm * n + np * s) + couple * p
            for a, em, e, ep, w, nm, n, np, s, p in zip(
                q, coefs[0], ahead(q, 1), coefs[1], back(q, 1), coefs[2], up(q, 1), coefs[3], down(q, 1), h
            )
        ]
        return [h, u, v, q]

    def adjoint(state, coefs):
        h, u, v, q = state
        h = [a + couple * b for a, b in zip(h, q)]
        u = [a + speed * (n - m) for a, n, m in zip(u, ahead(h, 2), h)]
        v = [a + (grad_p * n - grad_m * m) for a, n, m in zip(v, up(h, 2), h)]
        h = [
            a + (speed * (p - m) + (div_p * n - div_m * s))
            for a, p, m, n, s in zip(h, u, back(u, 2), v, down(v, 2))
        ]
        e = ahead([a * b for a, b in zip(coefs[1], q)], 1)
        w = back([a * b for a, b in zip(coefs[0], q)], 1)
        n = up([a * b for a, b in zip(coefs[3], q)], 1)
        s = down([a * b for a, b in zip(coefs[2], q)], 1)
        q = [stay * a + (b + c) + (d + f) for a, b, c, d, f in zip(q, e, w, n, s)]
        return [h, u, v, q]

    def each(fn, *states):
        return [[fn(*vals) for vals in zip(*xs)] for xs in zip(*states)]

    def operate(p, p_wide, precision, observed):
        weighted = []
        for t in range(subwins):
            change = p[t]
            if t > 0:
                moved, coefs = (p[t - 1], narrow) if p_wide is None else (p_wide[t - 1], wide)
                for _ in range(STEPS):
                    moved = tangent(moved, coefs)
                if p_wide is not None:
                    moved = [narrowed(x) for x in moved]
                change = each(lambda a, b: a - b, change, moved)
            weighted.append(each(lambda a, b: a * b, precision[t], change))
        image = []
        for t in range(subwins):
            out = each(lambda w, o, d: w + o * d, weighted[t], observed[t], p[t])
            if t + 1 < subwins:
                moved = weighted[t + 1]
                for _ in range(STEPS):
                    moved = adjoint(moved, narrow)
                out = each(lambda a, b: a - b, out, moved)
            image.append(out)
        return image

    def flat(x):
        return [(c, v) for state in x for field in state for c, v in enumerate(field)]

    def total(terms):
        inner, edge = None, None
        for c, v in terms:
            if c < TILES - 1:
                inner = v if inner is None else inner + v
            else:
                edge = v if edge is None else edge + v
        both = inner + jnp.where(free, 0.0, edge)
        return jnp.sum(both, axis=(0, 1), keepdims=True)

    def dot(x, y):
        return total([(c, v * w) for (c, v), (_, w) in zip(x, y)])

    precision = [stag(fields_of(0, t, FIELDS)) for t in range(subwins)]
    observed = [stag(fields_of(1, t, FIELDS)) for t in range(subwins)]
    for member in range(2):
        plain = [fields_of(member, t, 0) for t in range(subwins)]
        b = [stag(x) for x in plain]
        b_wide = [
            stag([widened(x, e) for x, e in zip(plain[t], extras_of(member, t))]) for t in range(subwins - 1)
        ]
        one = operate(b, b_wide, precision, observed)
        two = operate(one, None, precision, observed)
        one, two = [[[aligned(f, x) for f, x in enumerate(state)] for state in y] for y in (one, two)]
        f0, f1, f2 = flat(plain), flat(one), flat(two)
        bb, b1, s11, s12 = dot(f0, f0), dot(f0, f1), dot(f1, f1), dot(f1, f2)
        step = jnp.where(b1 > 0.0, bb / jnp.where(b1 > 0.0, b1, 1.0), 0.0)
        grow = jnp.where(bb > 0.0, step * step * s11 / jnp.where(bb > 0.0, bb, 1.0) - 1.0, 0.0)
        step_t = jnp.broadcast_to(step, (ROWS, LANES))
        grow_t = jnp.broadcast_to(grow, (ROWS, LANES))
        res = [(c, v - step_t * w) for (c, v), (_, w) in zip(f0, f1)]
        mov = [(c, v + grow_t * w) for (c, v), (_, w) in zip(res, f0)]
        img = [(c, (v - step_t * w) + grow_t * v) for (c, v), (_, w) in zip(f1, f2)]
        sums = [step, grow, bb, b1, s11, s12, dot(res, res), dot(res, f1), dot(mov, img), dot(mov, f2), dot(mov, f1)]
        for t in range(subwins):
            for a, x in enumerate((one, two)):
                for f in range(FIELDS):
                    for c in range(TILES):
                        v = x[t][f][c]
                        at = (a * FIELDS + f) * TILES + c
                        if c == TILES - 1:
                            i = a * FIELDS + f
                            even = sums[i]
                            odd = sums[i + 8] if i + 8 < len(sums) else jnp.zeros_like(even)
                            v = jnp.where(free, jnp.where(row % 2 == 0, even, odd), v)
                        start = (member * subwins + t) * ROWS * ROWS_OUT + at
                        out_ref[pl.ds(start, ROWS, stride=ROWS_OUT), :] = v


def finish_kernel(lon, merges, b_ref, in_ref, x_ref, r_ref):
    _, levels, share, _ = b_ref.shape
    full = lon // LANES
    rest = lon - full * LANES
    size = share * ROWS_OUT
    apart = merges[0] - merges[1]
    at_lane = merges[0] - 3 * REACH

    def sums(i):
        at = (i // 8) * ROWS_OUT + (i % 8) * TILES + TILES - 1
        halves = [in_ref[pl.ds(half * levels * size + at, levels, stride=size), :] for half in range(2)]
        return jnp.concatenate([halves[0], pltpu.roll(halves[1], apart, 1)], axis=0)

    step, grow, bb, b1, s11, s12, rr, r1, mi, m2, m1 = [sums(i) for i in range(11)]

    def total(x):
        return jnp.sum(x, axis=0, keepdims=True)

    norm_0 = total(bb)
    alpha_0 = norm_0 / total(b1)
    d = step - alpha_0
    norm_1 = total(rr + d * (2.0 * r1 + d * s11))
    beta = norm_1 / norm_0
    g = beta - grow
    curve = total(mi + 2.0 * (d * m2 + g * m1) + d * (d * s12 + 2.0 * g * s11) + g * g * b1)
    alpha_1 = norm_1 / curve
    first = alpha_0 + alpha_1 * (1.0 + beta)
    second = alpha_0 * alpha_1
    first = jnp.broadcast_to(first[:, at_lane : at_lane + 1], (share, LANES))
    second = jnp.broadcast_to(second[:, at_lane : at_lane + 1], (share, LANES))
    lane = lax.broadcasted_iota(jnp.int32, (share, LANES), 1)

    def image(level, k):
        got = [
            [
                in_ref[pl.ds((half * levels + level) * size + k * TILES + c, share, stride=ROWS_OUT), :]
                for c in range(TILES)
            ]
            for half in range(2)
        ]
        middle = jnp.where(lane < at_lane, got[0][2], got[1][2])
        return got[0][:2] + [middle] + got[1]

    for level in range(levels):
        for f in range(FIELDS):
            b = b_ref[f, level]
            ones, twos = image(level, f), image(level, FIELDS + f)
            for c, (one, two) in enumerate(zip(ones, twos)):
                width = LANES if c < full else rest
                cols = pl.ds(c * LANES, width)
                one, two = one[:, :width], two[:, :width]
                part = b[:, c * LANES : c * LANES + width]
                x_ref[f, level, :, cols] = first[:, :width] * part - second[:, :width] * one
                r_ref[f, level, :, cols] = (part - first[:, :width] * one) + second[:, :width] * two


def by_layer(right_side, error_precision, obs_count, background_wind, wave_speed, tracer_coupling):
    _, fields, levels, share, lon = right_side.shape
    subwins = lax.axis_size("tm")
    merges = merge_lanes(lon)
    vmem = pl.BlockSpec(memory_space=pltpu.VMEM)
    smem = pl.BlockSpec(memory_space=pltpu.SMEM)
    hbm = pl.BlockSpec(memory_space=pltpu.HBM)
    params = pltpu.CompilerParams(vmem_limit_bytes=48 * 1024 * 1024)
    state = (fields, levels, share, lon)

    def exchange(x):
        x = x.reshape(2 * levels, -1, 1, LANES)
        return lax.all_to_all(x, ("ens", "tm", "space"), 0, 0, tiled=True).reshape(-1, LANES)

    b = right_side.reshape(state)
    with jax.named_scope("pack"):
        packed = pl.pallas_call(
            lambda *refs: pack_kernel(lon, merges, *refs),
            out_shape=jax.ShapeDtypeStruct((2 * levels * share * ROWS_IN, LANES), jnp.float32),
            in_specs=[hbm] * 4,
            out_specs=vmem,
            scratch_shapes=[
                pltpu.VMEM(state, jnp.float32),
                pltpu.VMEM(state, jnp.float32),
                pltpu.VMEM(state, jnp.int32),
                pltpu.VMEM(background_wind.shape, jnp.float32),
                pltpu.SemaphoreType.DMA((4,)),
            ],
            compiler_params=params,
        )(b, error_precision.reshape(state), obs_count.reshape(state), background_wind)
    packed = exchange(packed)
    with jax.named_scope("layer"):
        images = pl.pallas_call(
            lambda *refs: layer_kernel(lon, merges, subwins, *refs),
            out_shape=jax.ShapeDtypeStruct((2 * levels * share * ROWS_OUT, LANES), jnp.float32),
            in_specs=[vmem, smem, smem],
            out_specs=vmem,
            compiler_params=params,
        )(packed, wave_speed, tracer_coupling)
    images = exchange(images)
    with jax.named_scope("finish"):
        x, r = pl.pallas_call(
            lambda *refs: finish_kernel(lon, merges, *refs),
            out_shape=[jax.ShapeDtypeStruct(state, jnp.float32)] * 2,
            in_specs=[vmem] * 2,
            out_specs=[vmem] * 2,
            compiler_params=params,
        )(b, images)
    return x.reshape(right_side.shape), r.reshape(right_side.shape)


def fits_by_layer(mesh, shape):
    space, tm, ens = mesh.shape["space"], mesh.shape["tm"], mesh.shape["ens"]
    subwins, fields, levels, lats, lon = shape
    return (
        (ens, tm, space, fields, lats) == (2, 4, 4, FIELDS, ROWS)
        and subwins == ens * tm
        and levels == space * tm
        and lon == 720
    )


def extended_2(cells, sides, width):
    for axis, dim in sides:
        count = lax.axis_size(axis)
        ends = count - 1
        head = lax.slice_in_dim(cells, 0, width, axis=dim)
        tail = lax.slice_in_dim(cells, cells.shape[dim] - width, cells.shape[dim], axis=dim)
        cells = jnp.concatenate(
            [
                lax.ppermute(tail, axis, [(i, (i + 1) % count) for i in range(ends)]),
                cells,
                lax.ppermute(head, axis, [((i + 1) % count, i) for i in range(ends)]),
            ],
            axis=dim,
        )
    return cells


def shifted(value, axis, by):
    peers = lax.axis_size(axis)
    pairs = [(i, i + by) for i in range(peers) if 0 <= i + by < peers]
    return lax.ppermute(value, axis, pairs)


def along_x(field):
    return 0.5 * (jnp.roll(field, -1, axis=-1) - jnp.roll(field, 1, axis=-1))


def second_x(field):
    return jnp.roll(field, -1, axis=-1) + jnp.roll(field, 1, axis=-1) - 2.0 * field


def along_y(extended):
    return 0.5 * (extended[..., 2:, :] - extended[..., :-2, :])


def trimmed(field, count):
    if count == 0:
        return field
    return field[..., count : field.shape[-2] - count, :]


def row_valid(lat_rows):
    first_row = lax.axis_index("space") * lat_rows - 4
    row_total = lat_rows * lax.axis_size("space")
    global_rows = first_row + jnp.arange(lat_rows + 8, dtype=jnp.int32)
    inside = jnp.logical_and(global_rows >= 0, global_rows < row_total)
    return inside.astype(jnp.float32)[:, None]


def tangent_core(state, margin, coefs):
    speed_col, couple_col, winds, have, valid = coefs
    height, east, north, tracer = (state[:, 0], state[:, 1], state[:, 2], state[:, 3])
    east_mid = east - speed_col * along_x(height)
    north_mid = (trimmed(north, 1) - speed_col * along_y(height)) * trimmed(valid, 5 - margin)
    height_new = trimmed(height, 2) - speed_col * (
        along_x(trimmed(east_mid, 2)) + along_y(north_mid)
    )
    tracer_one = trimmed(tracer, 1)
    inner = trimmed(tracer, 2)
    tracer_lap = second_x(inner) + tracer_one[..., 2:, :] + tracer_one[..., :-2, :] - 2.0 * inner
    wind_east = trimmed(winds[0], have - margin + 2)
    wind_north = trimmed(winds[1], have - margin + 2)
    tracer_new = (
        inner
        - wind_east * along_x(inner)
        - wind_north * along_y(tracer_one)
        + diffusion * tracer_lap
        + couple_col * height_new
    )
    result = jnp.stack(
        [height_new, trimmed(east_mid, 2), trimmed(north_mid, 1), tracer_new], axis=1
    )
    return result * trimmed(valid, 6 - margin)


def adjoint_core(state, margin, coefs):
    speed_col, couple_col, winds, have, valid = coefs
    height, east, north, tracer = (state[:, 0], state[:, 1], state[:, 2], state[:, 3])
    height_mix = height + couple_col * tracer
    east_mid = east + speed_col * along_x(height_mix)
    north_mid = (trimmed(north, 1) + speed_col * along_y(height_mix)) * trimmed(valid, 5 - margin)
    height_new = trimmed(height_mix, 2) + speed_col * (
        along_x(trimmed(east_mid, 2)) + along_y(north_mid)
    )
    tracer_one = trimmed(tracer, 1)
    inner = trimmed(tracer, 2)
    tracer_lap = second_x(inner) + tracer_one[..., 2:, :] + tracer_one[..., :-2, :] - 2.0 * inner
    wind_east = trimmed(winds[0], have - margin + 2)
    wind_north = trimmed(winds[1], have - margin + 1)
    tracer_new = (
        inner
        + along_x(wind_east * inner)
        + along_y(wind_north * tracer_one)
        + diffusion * tracer_lap
    )
    result = jnp.stack(
        [height_new, trimmed(east_mid, 2), trimmed(north_mid, 1), tracer_new], axis=1
    )
    return result * trimmed(valid, 6 - margin)


def rebuild(state, sent):
    widths = [(0, 0)] * (state.ndim - 3) + [(2, 2), (0, 0)]
    east_wide = jnp.pad(state[:, 1], widths)
    return jnp.stack([sent[:, 0], east_wide, sent[:, 1], sent[:, 2]], axis=1)


def tangent_near(state):
    picked = jnp.stack([state[:, 0], state[:, 2], state[:, 3]], axis=1)
    sent = extended_2(picked, (("space", 3),), 2)
    return rebuild(state, sent)


def adjoint_near(state):
    picked = jnp.stack([state[:, 0], state[:, 2], state[:, 3]], axis=1)
    sent = extended_2(picked, (("space", 3),), 2)
    return rebuild(state, sent)


def propagate(fields, step_core, near_fn, coefs):
    current = fields
    for step in range(STEPS):
        current = step_core(near_fn(current), 2, coefs)
    return current


def operate(direction, error_precision, observed, coefs):
    moved = propagate(direction, tangent_core, tangent_near, coefs)
    incoming = shifted(moved, "tm", 1)
    previous = jnp.concatenate([incoming, moved[:-1]], axis=0)
    weighted = error_precision * (direction - previous)
    back = propagate(weighted, adjoint_core, adjoint_near, coefs)
    arriving = shifted(back, "tm", -1)
    following = jnp.concatenate([back[1:], arriving], axis=0)
    return weighted - following + observed * direction


def squares(residual):
    return lax.psum(jnp.sum(residual * residual), ("space", "tm"))


def on_device(right_side, error_precision, obs_count, background_wind, wave_speed, tracer_coupling):
    lat_rows = right_side.shape[3]
    valid = row_valid(lat_rows)
    winds = extended_2(background_wind, (("space", 2),), 1)
    have = 1
    coefs = (wave_speed[:, None, None], tracer_coupling[:, None, None], winds, have, valid)
    observed = obs_count.astype(jnp.float32)
    solution_field = jnp.zeros_like(right_side)
    residual = right_side
    direction = right_side
    norm_now = squares(residual)
    for step in range(ITERS):
        image = operate(direction, error_precision, observed, coefs)
        alpha = norm_now / lax.psum(jnp.sum(direction * image), ("space", "tm"))
        solution_field = solution_field + alpha * direction
        residual = residual - alpha * image
        norm_next = squares(residual)
        direction = residual + norm_next / norm_now * direction
        norm_now = norm_next
    return (solution_field, residual)


def solution(mesh):
    def run(right_side, *others):
        body = by_layer if fits_by_layer(mesh, right_side.shape) else on_device
        return jax.shard_map(
            body,
            mesh=mesh,
            in_specs=(
                P(("ens", "tm"), None, None, "space", None),
                P("tm", None, None, "space", None),
                P("tm", None, None, "space", None),
                P(None, None, "space", None),
                P(),
                P(),
            ),
            out_specs=(
                P(("ens", "tm"), None, None, "space", None),
                P(("ens", "tm"), None, None, "space", None),
            ),
            check_vma=False,
        )(right_side, *others)

    return run
```

```python
import jax
import jax.numpy as jnp
from jax import lax
from jax.experimental import pallas as pl
from jax.experimental.pallas import tpu as pltpu
from jax.sharding import PartitionSpec as P

STEPS = 2
ITERS = 2


diffusion = 0.1


LANES = 128
ROWS = 8
TILES = 3
REACH = 4
FIELDS = 4
ROWS_IN = FIELDS * TILES * 2 + 2
ROWS_OUT = FIELDS * TILES * 2


def merge_lanes(lon):
    core = lon // 2
    return (core + 3 * REACH) % LANES, (core - 3 * REACH) % LANES


def pack_kernel(
    lon, merges, b_hbm, e_hbm, o_hbm, w_hbm, speed_hbm, couple_hbm, out_ref,
    b_ref, e_ref, o_ref, w_ref, speed_ref, couple_ref, sems,
):
    _, levels, share, _ = b_ref.shape
    pairs = (
        (b_hbm, b_ref), (w_hbm, w_ref), (speed_hbm, speed_ref), (couple_hbm, couple_ref),
        (e_hbm, e_ref), (o_hbm, o_ref),
    )
    copies = [pltpu.make_async_copy(src, dst, sems.at[i]) for i, (src, dst) in enumerate(pairs)]
    for copy in copies:
        copy.start()
    full = lon // LANES
    rest = lon - full * LANES
    member = lax.axis_index("ens")
    first_member = member == 0
    turn = lax.axis_index("tm") * 2 + member
    lane = lax.broadcasted_iota(jnp.int32, (share, LANES), 1)

    def put(half, level, row, value):
        base = (half * levels + level) * share * ROWS_IN
        out_ref[pl.ds(base + row, share, stride=ROWS_IN), :] = value

    def windows(x):
        tiles = [x[:, c * LANES : (c + 1) * LANES] for c in range(full)]
        tail = jnp.concatenate([x[:, full * LANES :], x[:, : LANES - rest]], axis=1)
        ahead = pltpu.roll(tail, LANES - rest, 1)
        ends = ((tiles[2], ahead), (tail, tiles[2]))
        halves = []
        for half, ((last, before), merge) in enumerate(zip(ends, merges)):
            merged = jnp.where(lane < merge, last, before)
            extra = jnp.where(lane < merge, before, last)
            halves.append((tiles[3 * half], tiles[3 * half + 1], merged, extra))
        return halves

    for copy in copies[:4]:
        copy.wait()
    for level in range(levels):
        extras = [None, None]
        for f in range(FIELDS):
            for half, got in enumerate(windows(b_ref[f, level])):
                for c in range(TILES):
                    put(half, level, f * TILES + c, got[c])
                moved = got[3] if f == 0 else pltpu.roll(got[3], LANES - 2 * REACH * f, 1)
                edge = merges[half] + REACH - 2 * REACH * f
                extras[half] = moved if f == 0 else jnp.where(lane < edge, moved, extras[half])
        speeds = jnp.where(lane < LANES // 4, speed_ref[level], couple_ref[level])
        for half in range(2):
            put(half, level, ROWS_IN - 2, jnp.where(lane < LANES // 2, speeds, extras[half]))
        for half, got in enumerate(windows(w_ref[jnp.where(turn < 2 * TILES, turn // TILES, turn - 2 * TILES), level])):
            value = got[3]
            for c in range(TILES):
                value = jnp.where(jnp.logical_or(turn == c, turn == TILES + c), got[c], value)
            put(half, level, ROWS_IN - 1, value)
    copies[4].wait()
    copies[5].wait()
    for level in range(levels):
        for f in range(FIELDS):
            shared = jnp.where(first_member, e_ref[f, level], o_ref[f, level].astype(jnp.float32))
            for half, got in enumerate(windows(shared)):
                for c in range(TILES):
                    put(half, level, (FIELDS + f) * TILES + c, got[c])


def layer_kernel(lon, merges, subwins, in_ref, out_ref):
    half = lax.axis_index("ens")
    lane = lax.broadcasted_iota(jnp.int32, (ROWS, LANES), 1)
    row = lax.broadcasted_iota(jnp.int32, (ROWS, LANES), 0)
    below = lane < jnp.where(half == 0, merges[0], merges[1])
    free_lo = jnp.where(half == 0, merges[0] - 3 * REACH, merges[1] - 3 * REACH)
    free = jnp.logical_and(lane >= free_lo, lane < free_lo + 6 * REACH)

    def load(member, t, k):
        return in_ref[pl.ds((member * subwins + t) * ROWS * ROWS_IN + k, ROWS, stride=ROWS_IN), :]

    given = load(0, 0, ROWS_IN - 2)
    speed = 0.5 * jnp.broadcast_to(given[:, :1], (ROWS, LANES))
    couple = jnp.broadcast_to(given[:, LANES // 4 : LANES // 4 + 1], (ROWS, LANES))

    def back(x, by):
        moved = [pltpu.roll(v, by, 1) for v in x]
        return [jnp.where(lane < by, moved[i - 1], v) for i, v in enumerate(moved)]

    def ahead(x, by):
        moved = [pltpu.roll(v, LANES - by, 1) for v in x]
        return [jnp.where(lane >= LANES - by, moved[(i + 1) % len(x)], v) for i, v in enumerate(moved)]

    def up(x, by):
        return [pltpu.roll(v, ROWS - by, 0) for v in x]

    def down(x, by):
        return [pltpu.roll(v, by, 0) for v in x]

    def staggered(f, x):
        if f == 1:
            return ahead(x, 1)
        if f == 2:
            return up(x, 1)
        return x

    def aligned(f, x):
        if f == 1:
            return back(x, 1)
        if f == 2:
            return down(x, 1)
        return x

    def widened(x, extra):
        return x[:2] + [jnp.where(below, x[2], extra), jnp.where(below, extra, x[2])]

    def narrowed(x):
        return x[:2] + [jnp.where(below, x[2], x[3])]

    def fields_of(member, t, at):
        return [[load(member, t, (at + f) * TILES + c) for c in range(TILES)] for f in range(FIELDS)]

    def extras_of(member, t):
        packed = load(member, t, ROWS_IN - 2)
        return [packed] + [pltpu.roll(packed, 2 * REACH * f, 1) for f in range(1, FIELDS)]

    def stag(state):
        return [staggered(f, x) for f, x in enumerate(state)]

    def wind(turn):
        return load(turn % 2, turn // 2, ROWS_IN - 1)

    stay = 1.0 - 4.0 * diffusion
    grad_p = jnp.where(row == ROWS - 2, 0.0, speed)
    grad_m = jnp.where(row == ROWS - 1, 0.0, speed)
    div_p = jnp.where(row == ROWS - 1, 0.0, speed)
    div_m = jnp.where(row == 0, 0.0, speed)

    def coefficients(east, north):
        return (
            [diffusion - 0.5 * v for v in east],
            [diffusion + 0.5 * v for v in east],
            [jnp.where(row == ROWS - 1, 0.0, diffusion - 0.5 * v) for v in north],
            [jnp.where(row == 0, 0.0, diffusion + 0.5 * v) for v in north],
        )

    east, north = [wind(i) for i in range(3)], [wind(3 + i) for i in range(3)]
    narrow = coefficients(east, north)
    wide = coefficients(widened(east, wind(6)), widened(north, wind(7)))

    def tangent(state, coefs):
        h, u, v, q = state
        u = [a - speed * (n - m) for a, n, m in zip(u, ahead(h, 2), h)]
        v = [a - (grad_p * n - grad_m * m) for a, n, m in zip(v, up(h, 2), h)]
        h = [
            a - (speed * (p - m) + (div_p * n - div_m * s))
            for a, p, m, n, s in zip(h, u, back(u, 2), v, down(v, 2))
        ]
        q = [
            stay * a + (em * e + ep * w) + (nm * n + np * s) + couple * p
            for a, em, e, ep, w, nm, n, np, s, p in zip(
                q, coefs[0], ahead(q, 1), coefs[1], back(q, 1), coefs[2], up(q, 1), coefs[3], down(q, 1), h
            )
        ]
        return [h, u, v, q]

    def adjoint(state, coefs):
        h, u, v, q = state
        h = [a + couple * b for a, b in zip(h, q)]
        u = [a + speed * (n - m) for a, n, m in zip(u, ahead(h, 2), h)]
        v = [a + (grad_p * n - grad_m * m) for a, n, m in zip(v, up(h, 2), h)]
        h = [
            a + (speed * (p - m) + (div_p * n - div_m * s))
            for a, p, m, n, s in zip(h, u, back(u, 2), v, down(v, 2))
        ]
        e = ahead([a * b for a, b in zip(coefs[1], q)], 1)
        w = back([a * b for a, b in zip(coefs[0], q)], 1)
        n = up([a * b for a, b in zip(coefs[3], q)], 1)
        s = down([a * b for a, b in zip(coefs[2], q)], 1)
        q = [stay * a + (b + c) + (d + f) for a, b, c, d, f in zip(q, e, w, n, s)]
        return [h, u, v, q]

    def each(fn, *states):
        return [[fn(*vals) for vals in zip(*xs)] for xs in zip(*states)]

    def operate(p, p_wide, precision, observed):
        weighted = []
        for t in range(subwins):
            change = p[t]
            if t > 0:
                moved, coefs = (p[t - 1], narrow) if p_wide is None else (p_wide[t - 1], wide)
                for _ in range(STEPS):
                    moved = tangent(moved, coefs)
                if p_wide is not None:
                    moved = [narrowed(x) for x in moved]
                change = each(lambda a, b: a - b, change, moved)
            weighted.append(each(lambda a, b: a * b, precision[t], change))
        image = []
        for t in range(subwins):
            out = each(lambda w, o, d: w + o * d, weighted[t], observed[t], p[t])
            if t + 1 < subwins:
                moved = weighted[t + 1]
                for _ in range(STEPS):
                    moved = adjoint(moved, narrow)
                out = each(lambda a, b: a - b, out, moved)
            image.append(out)
        return image

    def flat(x):
        return [(c, v) for state in x for field in state for c, v in enumerate(field)]

    def total(terms):
        inner, edge = None, None
        for c, v in terms:
            if c < TILES - 1:
                inner = v if inner is None else inner + v
            else:
                edge = v if edge is None else edge + v
        both = inner + jnp.where(free, 0.0, edge)
        return jnp.sum(both, axis=(0, 1), keepdims=True)

    def dot(x, y):
        return total([(c, v * w) for (c, v), (_, w) in zip(x, y)])

    precision = [stag(fields_of(0, t, FIELDS)) for t in range(subwins)]
    observed = [stag(fields_of(1, t, FIELDS)) for t in range(subwins)]
    for member in range(2):
        plain = [fields_of(member, t, 0) for t in range(subwins)]
        b = [stag(x) for x in plain]
        b_wide = [
            stag([widened(x, e) for x, e in zip(plain[t], extras_of(member, t))]) for t in range(subwins - 1)
        ]
        one = operate(b, b_wide, precision, observed)
        two = operate(one, None, precision, observed)
        one, two = [[[aligned(f, x) for f, x in enumerate(state)] for state in y] for y in (one, two)]
        f0, f1, f2 = flat(plain), flat(one), flat(two)
        s00, s01, s11, s02, s12 = dot(f0, f0), dot(f0, f1), dot(f1, f1), dot(f0, f2), dot(f1, f2)
        step = jnp.where(s01 > 0.0, s00 / jnp.where(s01 > 0.0, s01, 1.0), 0.0)
        more = jnp.where(s00 > 0.0, step * step * s11 / jnp.where(s00 > 0.0, s00, 1.0), 1.0)
        step_t = jnp.broadcast_to(step, (ROWS, LANES))
        more_t = jnp.broadcast_to(more, (ROWS, LANES))
        res = [(c, v - step_t * w) for (c, v), (_, w) in zip(f0, f1)]
        mov = [(c, more_t * v - step_t * w) for (c, v), (_, w) in zip(f0, f1)]
        img = [(c, more_t * v - step_t * w) for (c, v), (_, w) in zip(f1, f2)]
        sums = [step, more, s00, s01, s11, s02, s12, dot(res, res), dot(mov, img)]
        for t in range(subwins):
            for a, x in enumerate((one, two)):
                for f in range(FIELDS):
                    for c in range(TILES):
                        v = x[t][f][c]
                        at = (a * FIELDS + f) * TILES + c
                        if c == TILES - 1:
                            i = a * FIELDS + f
                            even = sums[i]
                            odd = sums[i + 8] if i + 8 < len(sums) else jnp.zeros_like(even)
                            v = jnp.where(free, jnp.where(row % 2 == 0, even, odd), v)
                        start = (member * subwins + t) * ROWS * ROWS_OUT + at
                        out_ref[pl.ds(start, ROWS, stride=ROWS_OUT), :] = v


def finish_kernel(lon, merges, b_ref, in_ref, x_hbm, r_hbm, x_ref, r_ref, sems):
    _, levels, share, _ = b_ref.shape
    full = lon // LANES
    rest = lon - full * LANES
    size = share * ROWS_OUT
    apart = merges[0] - merges[1]
    at_lane = merges[0] - 3 * REACH

    def sums(i):
        at = (i // 8) * ROWS_OUT + (i % 8) * TILES + TILES - 1
        halves = [in_ref[pl.ds(half * levels * size + at, levels, stride=size), :] for half in range(2)]
        return jnp.concatenate([halves[0], pltpu.roll(halves[1], apart, 1)], axis=0)

    step, more, s00, s01, s11, s02, s12, rr, mi = [sums(i) for i in range(9)]

    def total(x):
        return jnp.sum(x, axis=0, keepdims=True)

    norm_0 = total(s00)
    alpha_0 = norm_0 / total(s01)
    d = step - alpha_0
    norm_1 = total(rr + d * (2.0 * (s01 - step * s11) + d * s11))
    beta = norm_1 / norm_0
    g = (1.0 + beta) - more
    cross_d = more * (s02 + s11) - 2.0 * step * s12
    cross_g = 2.0 * more * s01 - step * (s11 + s02)
    curve = total(mi + d * (cross_d + d * s12 + g * (s11 + s02)) + g * (cross_g + g * s01))
    alpha_1 = norm_1 / curve
    first = alpha_0 + alpha_1 * (1.0 + beta)
    second = alpha_0 * alpha_1
    first = jnp.broadcast_to(first[:, at_lane : at_lane + 1], (share, LANES))
    second = jnp.broadcast_to(second[:, at_lane : at_lane + 1], (share, LANES))
    lane = lax.broadcasted_iota(jnp.int32, (share, LANES), 1)

    def image(level, k):
        got = [
            [
                in_ref[pl.ds((half * levels + level) * size + k * TILES + c, share, stride=ROWS_OUT), :]
                for c in range(TILES)
            ]
            for half in range(2)
        ]
        middle = jnp.where(lane < at_lane, got[0][2], got[1][2])
        return got[0][:2] + [middle] + got[1]

    copies = []
    for f in range(FIELDS):
        for level in range(levels):
            b = b_ref[f, level]
            ones, twos = image(level, f), image(level, FIELDS + f)
            for c, (one, two) in enumerate(zip(ones, twos)):
                width = LANES if c < full else rest
                cols = pl.ds(c * LANES, width)
                one, two = one[:, :width], two[:, :width]
                part = b[:, c * LANES : c * LANES + width]
                x_ref[f, level, :, cols] = first[:, :width] * part - second[:, :width] * one
                r_ref[f, level, :, cols] = (part - first[:, :width] * one) + second[:, :width] * two
        for i, (src, dst) in enumerate(((x_ref, x_hbm), (r_ref, r_hbm))):
            copies.append(pltpu.make_async_copy(src.at[f], dst.at[f], sems.at[i, f]))
            copies[-1].start()
    for copy in copies:
        copy.wait()


def by_layer(right_side, error_precision, obs_count, background_wind, wave_speed, tracer_coupling):
    _, fields, levels, share, lon = right_side.shape
    subwins = lax.axis_size("tm")
    merges = merge_lanes(lon)
    vmem = pl.BlockSpec(memory_space=pltpu.VMEM)
    hbm = pl.BlockSpec(memory_space=pltpu.HBM)
    params = pltpu.CompilerParams(vmem_limit_bytes=48 * 1024 * 1024)
    state = (fields, levels, share, lon)

    def exchange(x):
        x = x.reshape(2 * levels, -1, 1, LANES)
        return lax.all_to_all(x, ("ens", "tm", "space"), 0, 0, tiled=True).reshape(-1, LANES)

    b = right_side.reshape(state)
    given = (b, error_precision.reshape(state), obs_count.reshape(state), background_wind, wave_speed, tracer_coupling)
    with jax.named_scope("pack"):
        packed = pl.pallas_call(
            lambda *refs: pack_kernel(lon, merges, *refs),
            out_shape=jax.ShapeDtypeStruct((2 * levels * share * ROWS_IN, LANES), jnp.float32),
            in_specs=[hbm] * len(given),
            out_specs=vmem,
            scratch_shapes=[
                pltpu.VMEM(state, jnp.float32),
                pltpu.VMEM(state, jnp.float32),
                pltpu.VMEM(state, jnp.int32),
                pltpu.VMEM(background_wind.shape, jnp.float32),
                pltpu.SMEM(wave_speed.shape, jnp.float32),
                pltpu.SMEM(tracer_coupling.shape, jnp.float32),
                pltpu.SemaphoreType.DMA((len(given),)),
            ],
            compiler_params=params,
        )(*[pltpu.with_memory_space_constraint(x, pltpu.HBM) for x in given])
    packed = exchange(packed)
    with jax.named_scope("layer"):
        images = pl.pallas_call(
            lambda *refs: layer_kernel(lon, merges, subwins, *refs),
            out_shape=jax.ShapeDtypeStruct((2 * levels * share * ROWS_OUT, LANES), jnp.float32),
            in_specs=[vmem],
            out_specs=vmem,
            compiler_params=params,
        )(packed)
    images = exchange(images)
    with jax.named_scope("finish"):
        x, r = pl.pallas_call(
            lambda *refs: finish_kernel(lon, merges, *refs),
            out_shape=[jax.ShapeDtypeStruct(state, jnp.float32)] * 2,
            in_specs=[vmem] * 2,
            out_specs=[hbm] * 2,
            scratch_shapes=[pltpu.VMEM(state, jnp.float32)] * 2 + [pltpu.SemaphoreType.DMA((2, FIELDS))],
            compiler_params=params,
        )(b, images)
    return x.reshape(right_side.shape), r.reshape(right_side.shape)


def fits_by_layer(mesh, shape):
    space, tm, ens = mesh.shape["space"], mesh.shape["tm"], mesh.shape["ens"]
    subwins, fields, levels, lats, lon = shape
    return (
        (ens, tm, space, fields, lats) == (2, 4, 4, FIELDS, ROWS)
        and subwins == ens * tm
        and levels == space * tm
        and lon == 720
    )


def extended_2(cells, sides, width):
    for axis, dim in sides:
        count = lax.axis_size(axis)
        ends = count - 1
        head = lax.slice_in_dim(cells, 0, width, axis=dim)
        tail = lax.slice_in_dim(cells, cells.shape[dim] - width, cells.shape[dim], axis=dim)
        cells = jnp.concatenate(
            [
                lax.ppermute(tail, axis, [(i, (i + 1) % count) for i in range(ends)]),
                cells,
                lax.ppermute(head, axis, [((i + 1) % count, i) for i in range(ends)]),
            ],
            axis=dim,
        )
    return cells


def shifted(value, axis, by):
    peers = lax.axis_size(axis)
    pairs = [(i, i + by) for i in range(peers) if 0 <= i + by < peers]
    return lax.ppermute(value, axis, pairs)


def along_x(field):
    return 0.5 * (jnp.roll(field, -1, axis=-1) - jnp.roll(field, 1, axis=-1))


def second_x(field):
    return jnp.roll(field, -1, axis=-1) + jnp.roll(field, 1, axis=-1) - 2.0 * field


def along_y(extended):
    return 0.5 * (extended[..., 2:, :] - extended[..., :-2, :])


def trimmed(field, count):
    if count == 0:
        return field
    return field[..., count : field.shape[-2] - count, :]


def row_valid(lat_rows):
    first_row = lax.axis_index("space") * lat_rows - 4
    row_total = lat_rows * lax.axis_size("space")
    global_rows = first_row + jnp.arange(lat_rows + 8, dtype=jnp.int32)
    inside = jnp.logical_and(global_rows >= 0, global_rows < row_total)
    return inside.astype(jnp.float32)[:, None]


def tangent_core(state, margin, coefs):
    speed_col, couple_col, winds, have, valid = coefs
    height, east, north, tracer = (state[:, 0], state[:, 1], state[:, 2], state[:, 3])
    east_mid = east - speed_col * along_x(height)
    north_mid = (trimmed(north, 1) - speed_col * along_y(height)) * trimmed(valid, 5 - margin)
    height_new = trimmed(height, 2) - speed_col * (
        along_x(trimmed(east_mid, 2)) + along_y(north_mid)
    )
    tracer_one = trimmed(tracer, 1)
    inner = trimmed(tracer, 2)
    tracer_lap = second_x(inner) + tracer_one[..., 2:, :] + tracer_one[..., :-2, :] - 2.0 * inner
    wind_east = trimmed(winds[0], have - margin + 2)
    wind_north = trimmed(winds[1], have - margin + 2)
    tracer_new = (
        inner
        - wind_east * along_x(inner)
        - wind_north * along_y(tracer_one)
        + diffusion * tracer_lap
        + couple_col * height_new
    )
    result = jnp.stack(
        [height_new, trimmed(east_mid, 2), trimmed(north_mid, 1), tracer_new], axis=1
    )
    return result * trimmed(valid, 6 - margin)


def adjoint_core(state, margin, coefs):
    speed_col, couple_col, winds, have, valid = coefs
    height, east, north, tracer = (state[:, 0], state[:, 1], state[:, 2], state[:, 3])
    height_mix = height + couple_col * tracer
    east_mid = east + speed_col * along_x(height_mix)
    north_mid = (trimmed(north, 1) + speed_col * along_y(height_mix)) * trimmed(valid, 5 - margin)
    height_new = trimmed(height_mix, 2) + speed_col * (
        along_x(trimmed(east_mid, 2)) + along_y(north_mid)
    )
    tracer_one = trimmed(tracer, 1)
    inner = trimmed(tracer, 2)
    tracer_lap = second_x(inner) + tracer_one[..., 2:, :] + tracer_one[..., :-2, :] - 2.0 * inner
    wind_east = trimmed(winds[0], have - margin + 2)
    wind_north = trimmed(winds[1], have - margin + 1)
    tracer_new = (
        inner
        + along_x(wind_east * inner)
        + along_y(wind_north * tracer_one)
        + diffusion * tracer_lap
    )
    result = jnp.stack(
        [height_new, trimmed(east_mid, 2), trimmed(north_mid, 1), tracer_new], axis=1
    )
    return result * trimmed(valid, 6 - margin)


def rebuild(state, sent):
    widths = [(0, 0)] * (state.ndim - 3) + [(2, 2), (0, 0)]
    east_wide = jnp.pad(state[:, 1], widths)
    return jnp.stack([sent[:, 0], east_wide, sent[:, 1], sent[:, 2]], axis=1)


def tangent_near(state):
    picked = jnp.stack([state[:, 0], state[:, 2], state[:, 3]], axis=1)
    sent = extended_2(picked, (("space", 3),), 2)
    return rebuild(state, sent)


def adjoint_near(state):
    picked = jnp.stack([state[:, 0], state[:, 2], state[:, 3]], axis=1)
    sent = extended_2(picked, (("space", 3),), 2)
    return rebuild(state, sent)


def propagate(fields, step_core, near_fn, coefs):
    current = fields
    for step in range(STEPS):
        current = step_core(near_fn(current), 2, coefs)
    return current


def operate(direction, error_precision, observed, coefs):
    moved = propagate(direction, tangent_core, tangent_near, coefs)
    incoming = shifted(moved, "tm", 1)
    previous = jnp.concatenate([incoming, moved[:-1]], axis=0)
    weighted = error_precision * (direction - previous)
    back = propagate(weighted, adjoint_core, adjoint_near, coefs)
    arriving = shifted(back, "tm", -1)
    following = jnp.concatenate([back[1:], arriving], axis=0)
    return weighted - following + observed * direction


def squares(residual):
    return lax.psum(jnp.sum(residual * residual), ("space", "tm"))


def on_device(right_side, error_precision, obs_count, background_wind, wave_speed, tracer_coupling):
    lat_rows = right_side.shape[3]
    valid = row_valid(lat_rows)
    winds = extended_2(background_wind, (("space", 2),), 1)
    have = 1
    coefs = (wave_speed[:, None, None], tracer_coupling[:, None, None], winds, have, valid)
    observed = obs_count.astype(jnp.float32)
    solution_field = jnp.zeros_like(right_side)
    residual = right_side
    direction = right_side
    norm_now = squares(residual)
    for step in range(ITERS):
        image = operate(direction, error_precision, observed, coefs)
        alpha = norm_now / lax.psum(jnp.sum(direction * image), ("space", "tm"))
        solution_field = solution_field + alpha * direction
        residual = residual - alpha * image
        norm_next = squares(residual)
        direction = residual + norm_next / norm_now * direction
        norm_now = norm_next
    return (solution_field, residual)


def solution(mesh):
    def run(right_side, *others):
        body = by_layer if fits_by_layer(mesh, right_side.shape) else on_device
        return jax.shard_map(
            body,
            mesh=mesh,
            in_specs=(
                P(("ens", "tm"), None, None, "space", None),
                P("tm", None, None, "space", None),
                P("tm", None, None, "space", None),
                P(None, None, "space", None),
                P(),
                P(),
            ),
            out_specs=(
                P(("ens", "tm"), None, None, "space", None),
                P(("ens", "tm"), None, None, "space", None),
            ),
            check_vma=False,
        )(right_side, *others)

    return run
```

```python
import jax
import jax.numpy as jnp
from jax import lax
from jax.experimental import pallas as pl
from jax.experimental.pallas import tpu as pltpu
from jax.sharding import PartitionSpec as P

STEPS = 2
ITERS = 2


diffusion = 0.1


LANES = 128
ROWS = 8
TILES = 3
REACH = 4
FIELDS = 4
SLOT = 2 * REACH
WINDS = LANES - FIELDS * SLOT
FREE = 6 * REACH
MIXED = 2 * FIELDS * TILES
ROWS_IN = MIXED + 1
THIRDS = 4 * FIELDS
ROWS_OUT = THIRDS + 2 * FIELDS - 1


def merge_lanes(lon):
    core = lon // 2
    return (core + 3 * REACH) % LANES, (core - 3 * REACH) % LANES


def pack_kernel(
    lon, merges, b_hbm, e_hbm, o_hbm, w_hbm, speed_hbm, couple_hbm, out_ref,
    b_ref, e_ref, o_ref, w_ref, speed_ref, couple_ref, stage_ref, sems,
):
    _, levels, share, _ = b_ref.shape
    full = lon // LANES
    rest = lon - full * LANES
    member = lax.axis_index("ens")
    turn = lax.axis_index("tm") * 2 + member
    comp = jnp.where(turn < 2 * TILES, turn // TILES, turn - 2 * TILES)
    copy_b = pltpu.make_async_copy(b_hbm, b_ref, sems.at[0])
    copy_e = pltpu.make_async_copy(e_hbm, e_ref, sems.at[1])
    copy_o = pltpu.make_async_copy(o_hbm, o_ref, sems.at[2])
    others = (
        pltpu.make_async_copy(w_hbm.at[comp], w_ref, sems.at[3]),
        pltpu.make_async_copy(speed_hbm, speed_ref, sems.at[4]),
        pltpu.make_async_copy(couple_hbm, couple_ref, sems.at[5]),
    )
    copy_b.start()
    pl.when(member == 0)(copy_e.start)
    pl.when(member != 0)(copy_o.start)
    for copy in others:
        copy.start()
    lane = lax.broadcasted_iota(jnp.int32, (ROWS, LANES), 1)
    row = lax.broadcasted_iota(jnp.int32, (ROWS, LANES), 0)
    group = ROWS // share

    def raw(ref, first):
        for level in range(levels):
            for f in range(FIELDS):
                for c in range(full + 1):
                    half, tile = c // TILES, c % TILES
                    width = LANES if c < full else rest
                    value = ref[f, level, :, pl.ds(c * LANES, width)].astype(jnp.float32)
                    start = (half * levels + level) * share * ROWS_IN + first + f * TILES + tile
                    out_ref[pl.ds(start, share, stride=ROWS_IN), pl.ds(0, width)] = value

    def place(half, g, k):
        return pl.ds((half * levels + g * group) * share * ROWS_IN + k, ROWS, stride=ROWS_IN), slice(None)

    def windows(first, third, last):
        before = pltpu.roll(last, LANES - rest, 1)
        after = jnp.where(lane < rest, last, pltpu.roll(first, rest, 1))
        ends = ((third, before), (after, third))
        merged = [jnp.where(lane < m, x, y) for m, (x, y) in zip(merges, ends)]
        extra = [jnp.where(lane < m, y, x) for m, (x, y) in zip(merges, ends)]
        return merged, extra

    def merge(g, k):
        merged, extra = windows(
            out_ref[place(0, g, k)], out_ref[place(0, g, k + TILES - 1)], out_ref[place(1, g, k + TILES - 1)]
        )
        for half in range(2):
            out_ref[place(half, g, k + TILES - 1)] = merged[half]
        return extra

    def by_level(ref, g):
        value = jnp.full((ROWS, LANES), ref[g * group], jnp.float32)
        for i in range(1, group):
            value = jnp.where(row < i * share, value, ref[g * group + i])
        return value

    copy_b.wait()
    raw(b_ref, 0)
    for copy in others:
        copy.wait()
    for level in range(levels):
        for c in range(full + 1):
            width = LANES if c < full else rest
            stage_ref[c, pl.ds(level * share, share), pl.ds(0, width)] = w_ref[level, :, pl.ds(c * LANES, width)]
    for g in range(levels // group):
        mixed = [None, None]
        for f in range(FIELDS):
            extra = merge(g, f * TILES)
            for half, m in enumerate(merges):
                at = WINDS + f * SLOT
                moved = pltpu.roll(extra[half], (at - (m - REACH)) % LANES, 1)
                mixed[half] = moved if f == 0 else jnp.where(lane < at, mixed[half], moved)
        tiles = [stage_ref[c, pl.ds(g * ROWS, ROWS), :] for c in range(full + 1)]
        merged, extra = windows(tiles[0], tiles[2], tiles[5])
        speed, couple = by_level(speed_ref, g), by_level(couple_ref, g)
        for half, m in enumerate(merges):
            parts = tiles[TILES * half : TILES * half + 2] + [merged[half]]
            wind, left = parts[TILES - 1], pltpu.roll(parts[TILES - 1], LANES - SLOT * FIELDS, 1)
            for c in reversed(range(TILES - 1)):
                wind = jnp.where(jnp.logical_or(turn == c, turn == TILES + c), parts[c], wind)
                by = (c + 1) * SLOT * FIELDS
                left = jnp.where(lane < by, pltpu.roll(parts[c], by, 1), left)
            wind = jnp.where(turn < 2 * TILES, wind, left)
            value = jnp.where(lane < WINDS, wind, mixed[half])
            value = jnp.where(lane == WINDS + SLOT, speed, value)
            value = jnp.where(lane == WINDS + 2 * SLOT - 1, couple, value)
            ends = pltpu.roll(extra[half], LANES - 1 - m, 1)
            value = jnp.where(lane >= LANES - 2, ends, value)
            out_ref[place(half, g, MIXED)] = value

    def share_of(copy, ref):
        copy.wait()
        raw(ref, FIELDS * TILES)

    pl.when(member == 0)(lambda: share_of(copy_e, e_ref))
    pl.when(member != 0)(lambda: share_of(copy_o, o_ref))
    for g in range(levels // group):
        for f in range(FIELDS):
            merge(g, (FIELDS + f) * TILES)


def layer_kernel(lon, merges, subwins, in_ref, out_ref):
    half = lax.axis_index("ens")
    lane = lax.broadcasted_iota(jnp.int32, (ROWS, LANES), 1)
    row = lax.broadcasted_iota(jnp.int32, (ROWS, LANES), 0)
    below = lane < jnp.where(half == 0, merges[0], merges[1])
    free_lo = jnp.where(half == 0, merges[0] - 3 * REACH, merges[1] - 3 * REACH)
    free = jnp.logical_and(lane >= free_lo, lane < free_lo + FREE)

    def load(member, t, k):
        return in_ref[pl.ds((member * subwins + t) * ROWS * ROWS_IN + k, ROWS, stride=ROWS_IN), :]

    def of_half(values):
        return jnp.where(half == 0, values[0] % LANES, values[1] % LANES)

    mixed = [[load(member, t, MIXED) for t in range(subwins)] for member in range(2)]
    speed_at, couple_at = WINDS + SLOT, WINDS + 2 * SLOT - 1
    speed = 0.5 * jnp.broadcast_to(mixed[0][0][:, speed_at : speed_at + 1], (ROWS, LANES))
    couple = jnp.broadcast_to(mixed[0][0][:, couple_at : couple_at + 1], (ROWS, LANES))

    def back(x, by):
        moved = [pltpu.roll(v, by, 1) for v in x]
        return [jnp.where(lane < by, moved[i - 1], v) for i, v in enumerate(moved)]

    def ahead(x, by):
        moved = [pltpu.roll(v, LANES - by, 1) for v in x]
        return [jnp.where(lane >= LANES - by, moved[(i + 1) % len(x)], v) for i, v in enumerate(moved)]

    def up(x, by):
        return [pltpu.roll(v, ROWS - by, 0) for v in x]

    def down(x, by):
        return [pltpu.roll(v, by, 0) for v in x]

    def staggered(f, x):
        if f == 1:
            return ahead(x, 1)
        if f == 2:
            return up(x, 1)
        return x

    def aligned(f, x):
        if f == 1:
            return back(x, 1)
        if f == 2:
            return down(x, 1)
        return x

    def widened(x, extra):
        return x[:2] + [jnp.where(below, x[2], extra), jnp.where(below, extra, x[2])]

    def narrowed(x):
        return x[:2] + [jnp.where(below, x[2], x[3])]

    def fields_of(member, t, at):
        return [[load(member, t, (at + f) * TILES + c) for c in range(TILES)] for f in range(FIELDS)]

    def extras_of(member, t):
        shifts = [of_half([m - REACH - WINDS - f * SLOT for m in merges]) for f in range(FIELDS)]
        return [pltpu.roll(mixed[member][t], by, 1) for by in shifts]

    def stag(state):
        return [staggered(f, x) for f, x in enumerate(state)]

    def wind(comp):
        sent = [mixed[turn % 2][turn // 2] for turn in range(2 * subwins)]
        left = sent[2 * TILES + comp]
        tiles = []
        for c in range(TILES):
            by = WINDS - c * SLOT * FIELDS
            tiles.append(jnp.where(lane < WINDS, sent[comp * TILES + c], pltpu.roll(left, by, 1)))
        return tiles, pltpu.roll(sent[comp * TILES], of_half([m + 1 - LANES for m in merges]), 1)

    stay = 1.0 - 4.0 * diffusion
    grad_p = jnp.where(row == ROWS - 2, 0.0, speed)
    grad_m = jnp.where(row == ROWS - 1, 0.0, speed)
    div_p = jnp.where(row == ROWS - 1, 0.0, speed)
    div_m = jnp.where(row == 0, 0.0, speed)

    def coefficients(east, north):
        return (
            [diffusion - 0.5 * v for v in east],
            [diffusion + 0.5 * v for v in east],
            [jnp.where(row == ROWS - 1, 0.0, diffusion - 0.5 * v) for v in north],
            [jnp.where(row == 0, 0.0, diffusion + 0.5 * v) for v in north],
        )

    (east, east_extra), (north, north_extra) = wind(0), wind(1)
    narrow = coefficients(east, north)
    wide = coefficients(widened(east, east_extra), widened(north, north_extra))

    def tangent(state, coefs):
        h, u, v, q = state
        u = [a - speed * (n - m) for a, n, m in zip(u, ahead(h, 2), h)]
        v = [a - (grad_p * n - grad_m * m) for a, n, m in zip(v, up(h, 2), h)]
        h = [
            a - (speed * (p - m) + (div_p * n - div_m * s))
            for a, p, m, n, s in zip(h, u, back(u, 2), v, down(v, 2))
        ]
        q = [
            stay * a + (em * e + ep * w) + (nm * n + np * s) + couple * p
            for a, em, e, ep, w, nm, n, np, s, p in zip(
                q, coefs[0], ahead(q, 1), coefs[1], back(q, 1), coefs[2], up(q, 1), coefs[3], down(q, 1), h
            )
        ]
        return [h, u, v, q]

    def adjoint(state, coefs):
        h, u, v, q = state
        h = [a + couple * b for a, b in zip(h, q)]
        u = [a + speed * (n - m) for a, n, m in zip(u, ahead(h, 2), h)]
        v = [a + (grad_p * n - grad_m * m) for a, n, m in zip(v, up(h, 2), h)]
        h = [
            a + (speed * (p - m) + (div_p * n - div_m * s))
            for a, p, m, n, s in zip(h, u, back(u, 2), v, down(v, 2))
        ]
        e = ahead([a * b for a, b in zip(coefs[1], q)], 1)
        w = back([a * b for a, b in zip(coefs[0], q)], 1)
        n = up([a * b for a, b in zip(coefs[3], q)], 1)
        s = down([a * b for a, b in zip(coefs[2], q)], 1)
        q = [stay * a + (b + c) + (d + f) for a, b, c, d, f in zip(q, e, w, n, s)]
        return [h, u, v, q]

    def each(fn, *states):
        return [[fn(*vals) for vals in zip(*xs)] for xs in zip(*states)]

    def operate(p, p_wide, precision, observed):
        weighted = []
        for t in range(subwins):
            change = p[t]
            if t > 0:
                moved, coefs = (p[t - 1], narrow) if p_wide is None else (p_wide[t - 1], wide)
                for _ in range(STEPS):
                    moved = tangent(moved, coefs)
                if p_wide is not None:
                    moved = [narrowed(x) for x in moved]
                change = each(lambda a, b: a - b, change, moved)
            weighted.append(each(lambda a, b: a * b, precision[t], change))
        image = []
        for t in range(subwins):
            out = each(lambda w, o, d: w + o * d, weighted[t], observed[t], p[t])
            if t + 1 < subwins:
                moved = weighted[t + 1]
                for _ in range(STEPS):
                    moved = adjoint(moved, narrow)
                out = each(lambda a, b: a - b, out, moved)
            image.append(out)
        return image

    def flat(x):
        return [(c, v) for state in x for field in state for c, v in enumerate(field)]

    def total(terms):
        inner, edge = None, None
        for c, v in terms:
            if c < TILES - 1:
                inner = v if inner is None else inner + v
            else:
                edge = v if edge is None else edge + v
        both = inner + jnp.where(free, 0.0, edge)
        return jnp.sum(both, axis=(0, 1), keepdims=True)

    def dot(x, y):
        return total([(c, v * w) for (c, v), (_, w) in zip(x, y)])

    precision = [stag(fields_of(0, t, FIELDS)) for t in range(subwins)]
    observed = [stag(fields_of(1, t, FIELDS)) for t in range(subwins)]
    for member in range(2):
        plain = [fields_of(member, t, 0) for t in range(subwins)]
        b = [stag(x) for x in plain]
        b_wide = [
            stag([widened(x, e) for x, e in zip(plain[t], extras_of(member, t))]) for t in range(subwins - 1)
        ]
        one = operate(b, b_wide, precision, observed)
        two = operate(one, None, precision, observed)
        one, two = [[[aligned(f, x) for f, x in enumerate(state)] for state in y] for y in (one, two)]
        f0, f1, f2 = flat(plain), flat(one), flat(two)
        s00, s01, s11, s02, s12 = dot(f0, f0), dot(f0, f1), dot(f1, f1), dot(f0, f2), dot(f1, f2)
        step = jnp.where(s01 > 0.0, s00 / jnp.where(s01 > 0.0, s01, 1.0), 0.0)
        more = jnp.where(s00 > 0.0, step * step * s11 / jnp.where(s00 > 0.0, s00, 1.0), 1.0)
        step_t = jnp.broadcast_to(step, (ROWS, LANES))
        more_t = jnp.broadcast_to(more, (ROWS, LANES))
        res = [(c, v - step_t * w) for (c, v), (_, w) in zip(f0, f1)]
        mov = [(c, more_t * v - step_t * w) for (c, v), (_, w) in zip(f0, f1)]
        img = [(c, more_t * v - step_t * w) for (c, v), (_, w) in zip(f1, f2)]
        sums = [step, more, s00, s01, s11, s02, s12, dot(res, res), dot(mov, img)]
        sums += [sums[-1]] * (-len(sums) % 6)
        for t in range(subwins):

            def put(k, value):
                start = (member * subwins + t) * ROWS * ROWS_OUT + k
                out_ref[pl.ds(start, ROWS, stride=ROWS_OUT), :] = value

            images = one[t] + two[t]
            last = images[-1][TILES - 1]
            for k, x in enumerate(images):
                put(2 * k, x[0])
                put(2 * k + 1, x[1])
                if k < 5:
                    put(THIRDS + k, jnp.where(free, pltpu.roll(last, (-(k + 1) * FREE) % LANES, 1), x[2]))
                elif k < 2 * FIELDS - 1:
                    rows = []
                    for i in (k - 5, k - 3):
                        value = sums[3 * i + 2]
                        for j in (1, 0):
                            value = jnp.where(lane < free_lo + (j + 1) * SLOT, sums[3 * i + j], value)
                        rows.append(value)
                    put(THIRDS + k, jnp.where(free, jnp.where(row % 2 == 0, rows[0], rows[1]), x[2]))


def finish_kernel(lon, merges, b_ref, in_ref, x_hbm, r_hbm, x_ref, r_ref, last_ref, sems):
    _, levels, share, _ = b_ref.shape
    full = lon // LANES
    rest = lon - full * LANES
    size = share * ROWS_OUT
    apart = merges[0] - merges[1]
    at_lane = merges[0] - 3 * REACH

    group = ROWS // share

    slots = []
    for i in range(3):
        at = THIRDS + 5 + i % 2 + (i // 2) * ROWS_OUT
        halves = [in_ref[pl.ds(half * levels * size + at, levels, stride=size), :] for half in range(2)]
        slots.append(jnp.concatenate([halves[0], pltpu.roll(halves[1], apart, 1)], axis=0))

    def sums(i):
        value = slots[i // 3]
        return pltpu.roll(value, LANES - (i % 3) * SLOT, 1) if i % 3 else value

    step, more, s00, s01, s11, s02, s12, rr, mi = [sums(i) for i in range(9)]

    def total(x):
        return jnp.sum(x, axis=0, keepdims=True)

    norm_0 = total(s00)
    alpha_0 = norm_0 / total(s01)
    d = step - alpha_0
    norm_1 = total(rr + d * (2.0 * (s01 - step * s11) + d * s11))
    beta = norm_1 / norm_0
    g = (1.0 + beta) - more
    cross_d = more * (s02 + s11) - 2.0 * step * s12
    cross_g = 2.0 * more * s01 - step * (s11 + s02)
    curve = total(mi + d * (cross_d + d * s12 + g * (s11 + s02)) + g * (cross_g + g * s01))
    alpha_1 = norm_1 / curve
    first = alpha_0 + alpha_1 * (1.0 + beta)
    second = alpha_0 * alpha_1
    first = jnp.broadcast_to(first[:, at_lane : at_lane + 1], (share, LANES))
    second = jnp.broadcast_to(second[:, at_lane : at_lane + 1], (share, LANES))
    lane = lax.broadcasted_iota(jnp.int32, (share, LANES), 1)

    lane_8 = lax.broadcasted_iota(jnp.int32, (ROWS, LANES), 1)
    for half in range(2):
        for g in range(levels // group):
            value = None
            for k in range(5):
                start = (half * levels + g * group) * size + THIRDS + k
                part = pltpu.roll(in_ref[pl.ds(start, ROWS, stride=ROWS_OUT), :], (k + 1) * FREE % LANES, 1)
                begin = (merges[half] - 3 * REACH + (k + 1) * FREE) % LANES
                here = jnp.logical_and(lane_8 >= begin, lane_8 < begin + FREE)
                value = part if value is None else jnp.where(here, part, value)
            last_ref[half, pl.ds(g * ROWS, ROWS), :] = value

    def image(level, k):
        got = []
        for half in range(2):
            start = (half * levels + level) * size
            tiles = [in_ref[pl.ds(start + 2 * k + c, share, stride=ROWS_OUT), :] for c in range(2)]
            if k < 2 * FIELDS - 1:
                tiles.append(in_ref[pl.ds(start + THIRDS + k, share, stride=ROWS_OUT), :])
            else:
                tiles.append(last_ref[half, pl.ds(level * share, share), :])
            got.append(tiles)
        middle = jnp.where(lane < at_lane, got[0][2], got[1][2])
        return got[0][:2] + [middle] + got[1]

    copies = []
    for f in range(FIELDS):
        for level in range(levels):
            b = b_ref[f, level]
            ones, twos = image(level, f), image(level, FIELDS + f)
            for c, (one, two) in enumerate(zip(ones, twos)):
                width = LANES if c < full else rest
                cols = pl.ds(c * LANES, width)
                one, two = one[:, :width], two[:, :width]
                part = b[:, c * LANES : c * LANES + width]
                x_ref[f, level, :, cols] = first[:, :width] * part - second[:, :width] * one
                r_ref[f, level, :, cols] = (part - first[:, :width] * one) + second[:, :width] * two
        for i, (src, dst) in enumerate(((x_ref, x_hbm), (r_ref, r_hbm))):
            copies.append(pltpu.make_async_copy(src.at[f], dst.at[f], sems.at[i, f]))
            copies[-1].start()
    for copy in copies:
        copy.wait()


def by_layer(right_side, error_precision, obs_count, background_wind, wave_speed, tracer_coupling):
    _, fields, levels, share, lon = right_side.shape
    subwins = lax.axis_size("tm")
    merges = merge_lanes(lon)
    vmem = pl.BlockSpec(memory_space=pltpu.VMEM)
    hbm = pl.BlockSpec(memory_space=pltpu.HBM)
    params = pltpu.CompilerParams(vmem_limit_bytes=48 * 1024 * 1024)
    state = (fields, levels, share, lon)

    def exchange(x):
        x = x.reshape(2 * levels, -1, 1, LANES)
        return lax.all_to_all(x, ("ens", "tm", "space"), 0, 0, tiled=True).reshape(-1, LANES)

    b = right_side.reshape(state)
    given = (b, error_precision.reshape(state), obs_count.reshape(state), background_wind, wave_speed, tracer_coupling)
    with jax.named_scope("pack"):
        packed = pl.pallas_call(
            lambda *refs: pack_kernel(lon, merges, *refs),
            out_shape=jax.ShapeDtypeStruct((2 * levels * share * ROWS_IN, LANES), jnp.float32),
            in_specs=[hbm] * len(given),
            out_specs=vmem,
            scratch_shapes=[
                pltpu.VMEM(state, jnp.float32),
                pltpu.VMEM(state, jnp.float32),
                pltpu.VMEM(state, jnp.int32),
                pltpu.VMEM(background_wind.shape[1:], jnp.float32),
                pltpu.SMEM(wave_speed.shape, jnp.float32),
                pltpu.SMEM(tracer_coupling.shape, jnp.float32),
                pltpu.VMEM((lon // LANES + 1, levels * share, LANES), jnp.float32),
                pltpu.SemaphoreType.DMA((len(given),)),
            ],
            compiler_params=params,
        )(*[pltpu.with_memory_space_constraint(x, pltpu.HBM) for x in given])
    packed = exchange(packed)
    with jax.named_scope("layer"):
        images = pl.pallas_call(
            lambda *refs: layer_kernel(lon, merges, subwins, *refs),
            out_shape=jax.ShapeDtypeStruct((2 * levels * share * ROWS_OUT, LANES), jnp.float32),
            in_specs=[vmem],
            out_specs=vmem,
            compiler_params=params,
        )(packed)
    images = exchange(images)
    with jax.named_scope("finish"):
        x, r = pl.pallas_call(
            lambda *refs: finish_kernel(lon, merges, *refs),
            out_shape=[jax.ShapeDtypeStruct(state, jnp.float32)] * 2,
            in_specs=[vmem] * 2,
            out_specs=[hbm] * 2,
            scratch_shapes=[
                pltpu.VMEM(state, jnp.float32),
                pltpu.VMEM(state, jnp.float32),
                pltpu.VMEM((2, levels * share, LANES), jnp.float32),
                pltpu.SemaphoreType.DMA((2, FIELDS)),
            ],
            compiler_params=params,
        )(b, images)
    return x.reshape(right_side.shape), r.reshape(right_side.shape)


def fits_by_layer(mesh, shape):
    space, tm, ens = mesh.shape["space"], mesh.shape["tm"], mesh.shape["ens"]
    subwins, fields, levels, lats, lon = shape
    return (
        (ens, tm, space, fields, lats) == (2, 4, 4, FIELDS, ROWS)
        and subwins == ens * tm
        and levels == space * tm
        and lon == 720
    )


def extended_2(cells, sides, width):
    for axis, dim in sides:
        count = lax.axis_size(axis)
        ends = count - 1
        head = lax.slice_in_dim(cells, 0, width, axis=dim)
        tail = lax.slice_in_dim(cells, cells.shape[dim] - width, cells.shape[dim], axis=dim)
        cells = jnp.concatenate(
            [
                lax.ppermute(tail, axis, [(i, (i + 1) % count) for i in range(ends)]),
                cells,
                lax.ppermute(head, axis, [((i + 1) % count, i) for i in range(ends)]),
            ],
            axis=dim,
        )
    return cells


def shifted(value, axis, by):
    peers = lax.axis_size(axis)
    pairs = [(i, i + by) for i in range(peers) if 0 <= i + by < peers]
    return lax.ppermute(value, axis, pairs)


def along_x(field):
    return 0.5 * (jnp.roll(field, -1, axis=-1) - jnp.roll(field, 1, axis=-1))


def second_x(field):
    return jnp.roll(field, -1, axis=-1) + jnp.roll(field, 1, axis=-1) - 2.0 * field


def along_y(extended):
    return 0.5 * (extended[..., 2:, :] - extended[..., :-2, :])


def trimmed(field, count):
    if count == 0:
        return field
    return field[..., count : field.shape[-2] - count, :]


def row_valid(lat_rows):
    first_row = lax.axis_index("space") * lat_rows - 4
    row_total = lat_rows * lax.axis_size("space")
    global_rows = first_row + jnp.arange(lat_rows + 8, dtype=jnp.int32)
    inside = jnp.logical_and(global_rows >= 0, global_rows < row_total)
    return inside.astype(jnp.float32)[:, None]


def tangent_core(state, margin, coefs):
    speed_col, couple_col, winds, have, valid = coefs
    height, east, north, tracer = (state[:, 0], state[:, 1], state[:, 2], state[:, 3])
    east_mid = east - speed_col * along_x(height)
    north_mid = (trimmed(north, 1) - speed_col * along_y(height)) * trimmed(valid, 5 - margin)
    height_new = trimmed(height, 2) - speed_col * (
        along_x(trimmed(east_mid, 2)) + along_y(north_mid)
    )
    tracer_one = trimmed(tracer, 1)
    inner = trimmed(tracer, 2)
    tracer_lap = second_x(inner) + tracer_one[..., 2:, :] + tracer_one[..., :-2, :] - 2.0 * inner
    wind_east = trimmed(winds[0], have - margin + 2)
    wind_north = trimmed(winds[1], have - margin + 2)
    tracer_new = (
        inner
        - wind_east * along_x(inner)
        - wind_north * along_y(tracer_one)
        + diffusion * tracer_lap
        + couple_col * height_new
    )
    result = jnp.stack(
        [height_new, trimmed(east_mid, 2), trimmed(north_mid, 1), tracer_new], axis=1
    )
    return result * trimmed(valid, 6 - margin)


def adjoint_core(state, margin, coefs):
    speed_col, couple_col, winds, have, valid = coefs
    height, east, north, tracer = (state[:, 0], state[:, 1], state[:, 2], state[:, 3])
    height_mix = height + couple_col * tracer
    east_mid = east + speed_col * along_x(height_mix)
    north_mid = (trimmed(north, 1) + speed_col * along_y(height_mix)) * trimmed(valid, 5 - margin)
    height_new = trimmed(height_mix, 2) + speed_col * (
        along_x(trimmed(east_mid, 2)) + along_y(north_mid)
    )
    tracer_one = trimmed(tracer, 1)
    inner = trimmed(tracer, 2)
    tracer_lap = second_x(inner) + tracer_one[..., 2:, :] + tracer_one[..., :-2, :] - 2.0 * inner
    wind_east = trimmed(winds[0], have - margin + 2)
    wind_north = trimmed(winds[1], have - margin + 1)
    tracer_new = (
        inner
        + along_x(wind_east * inner)
        + along_y(wind_north * tracer_one)
        + diffusion * tracer_lap
    )
    result = jnp.stack(
        [height_new, trimmed(east_mid, 2), trimmed(north_mid, 1), tracer_new], axis=1
    )
    return result * trimmed(valid, 6 - margin)


def rebuild(state, sent):
    widths = [(0, 0)] * (state.ndim - 3) + [(2, 2), (0, 0)]
    east_wide = jnp.pad(state[:, 1], widths)
    return jnp.stack([sent[:, 0], east_wide, sent[:, 1], sent[:, 2]], axis=1)


def tangent_near(state):
    picked = jnp.stack([state[:, 0], state[:, 2], state[:, 3]], axis=1)
    sent = extended_2(picked, (("space", 3),), 2)
    return rebuild(state, sent)


def adjoint_near(state):
    picked = jnp.stack([state[:, 0], state[:, 2], state[:, 3]], axis=1)
    sent = extended_2(picked, (("space", 3),), 2)
    return rebuild(state, sent)


def propagate(fields, step_core, near_fn, coefs):
    current = fields
    for step in range(STEPS):
        current = step_core(near_fn(current), 2, coefs)
    return current


def operate(direction, error_precision, observed, coefs):
    moved = propagate(direction, tangent_core, tangent_near, coefs)
    incoming = shifted(moved, "tm", 1)
    previous = jnp.concatenate([incoming, moved[:-1]], axis=0)
    weighted = error_precision * (direction - previous)
    back = propagate(weighted, adjoint_core, adjoint_near, coefs)
    arriving = shifted(back, "tm", -1)
    following = jnp.concatenate([back[1:], arriving], axis=0)
    return weighted - following + observed * direction


def squares(residual):
    return lax.psum(jnp.sum(residual * residual), ("space", "tm"))


def on_device(right_side, error_precision, obs_count, background_wind, wave_speed, tracer_coupling):
    lat_rows = right_side.shape[3]
    valid = row_valid(lat_rows)
    winds = extended_2(background_wind, (("space", 2),), 1)
    have = 1
    coefs = (wave_speed[:, None, None], tracer_coupling[:, None, None], winds, have, valid)
    observed = obs_count.astype(jnp.float32)
    solution_field = jnp.zeros_like(right_side)
    residual = right_side
    direction = right_side
    norm_now = squares(residual)
    for step in range(ITERS):
        image = operate(direction, error_precision, observed, coefs)
        alpha = norm_now / lax.psum(jnp.sum(direction * image), ("space", "tm"))
        solution_field = solution_field + alpha * direction
        residual = residual - alpha * image
        norm_next = squares(residual)
        direction = residual + norm_next / norm_now * direction
        norm_now = norm_next
    return (solution_field, residual)


def solution(mesh):
    def run(right_side, *others):
        body = by_layer if fits_by_layer(mesh, right_side.shape) else on_device
        return jax.shard_map(
            body,
            mesh=mesh,
            in_specs=(
                P(("ens", "tm"), None, None, "space", None),
                P("tm", None, None, "space", None),
                P("tm", None, None, "space", None),
                P(None, None, "space", None),
                P(),
                P(),
            ),
            out_specs=(
                P(("ens", "tm"), None, None, "space", None),
                P(("ens", "tm"), None, None, "space", None),
            ),
            check_vma=False,
        )(right_side, *others)

    return run
```

```python
import jax
import jax.numpy as jnp
from jax import lax
from jax.experimental import pallas as pl
from jax.experimental.pallas import tpu as pltpu
from jax.sharding import PartitionSpec as P

STEPS = 2
ITERS = 2


diffusion = 0.1


LANES = 128
ROWS = 8
TILES = 3
REACH = 4
FIELDS = 4
SLOT = 2 * REACH
WINDS = LANES - FIELDS * SLOT
FREE = 6 * REACH
MIXED = 2 * FIELDS * TILES
ROWS_IN = MIXED + 1
THIRDS = 4 * FIELDS
ROWS_OUT = THIRDS + 2 * FIELDS - 1


def merge_lanes(lon):
    core = lon // 2
    return (core + 3 * REACH) % LANES, (core - 3 * REACH) % LANES


def pack_kernel(
    lon, merges, b_hbm, e_hbm, o_hbm, w_hbm, speed_hbm, couple_hbm, out_ref,
    b_ref, e_ref, o_ref, w_ref, speed_ref, couple_ref, stage_ref, sems,
):
    _, levels, share, _ = b_ref.shape
    full = lon // LANES
    rest = lon - full * LANES
    member = lax.axis_index("ens")
    turn = lax.axis_index("tm") * 2 + member
    comp = jnp.where(turn < 2 * TILES, turn // TILES, turn - 2 * TILES)

    def by_field(hbm, ref, first):
        return [pltpu.make_async_copy(hbm, ref, sems.at[first])]

    def start(copies):
        for copy in copies:
            copy.start()

    copies_b, copies_e, copies_o = by_field(b_hbm, b_ref, 0), by_field(e_hbm, e_ref, FIELDS), by_field(o_hbm, o_ref, FIELDS)
    others = (
        pltpu.make_async_copy(w_hbm.at[comp], w_ref, sems.at[2 * FIELDS]),
        pltpu.make_async_copy(speed_hbm, speed_ref, sems.at[2 * FIELDS + 1]),
        pltpu.make_async_copy(couple_hbm, couple_ref, sems.at[2 * FIELDS + 2]),
    )
    start(copies_b)
    pl.when(member == 0)(lambda: start(copies_e))
    pl.when(member != 0)(lambda: start(copies_o))
    start(others)
    lane = lax.broadcasted_iota(jnp.int32, (ROWS, LANES), 1)
    row = lax.broadcasted_iota(jnp.int32, (ROWS, LANES), 0)
    group = ROWS // share

    def raw(copies, ref, first):
        copies[0].wait()
        for f in range(FIELDS):
            for level in range(levels):
                for c in range(full + 1):
                    half, tile = c // TILES, c % TILES
                    width = LANES if c < full else rest
                    value = ref[f, level, :, pl.ds(c * LANES, width)].astype(jnp.float32)
                    start = (half * levels + level) * share * ROWS_IN + first + f * TILES + tile
                    out_ref[pl.ds(start, share, stride=ROWS_IN), pl.ds(0, width)] = value

    def place(half, g, k):
        return pl.ds((half * levels + g * group) * share * ROWS_IN + k, ROWS, stride=ROWS_IN), slice(None)

    def windows(first, third, last):
        before = pltpu.roll(last, LANES - rest, 1)
        after = jnp.where(lane < rest, last, pltpu.roll(first, rest, 1))
        ends = ((third, before), (after, third))
        merged = [jnp.where(lane < m, x, y) for m, (x, y) in zip(merges, ends)]
        extra = [jnp.where(lane < m, y, x) for m, (x, y) in zip(merges, ends)]
        return merged, extra

    def merge(g, k):
        merged, extra = windows(
            out_ref[place(0, g, k)], out_ref[place(0, g, k + TILES - 1)], out_ref[place(1, g, k + TILES - 1)]
        )
        for half in range(2):
            out_ref[place(half, g, k + TILES - 1)] = merged[half]
        return extra

    def by_level(ref, g):
        value = jnp.full((ROWS, LANES), ref[g * group], jnp.float32)
        for i in range(1, group):
            value = jnp.where(row < i * share, value, ref[g * group + i])
        return value

    raw(copies_b, b_ref, 0)
    pl.when(member == 0)(lambda: raw(copies_e, e_ref, FIELDS * TILES))
    pl.when(member != 0)(lambda: raw(copies_o, o_ref, FIELDS * TILES))
    for copy in others:
        copy.wait()
    for level in range(levels):
        for c in range(full + 1):
            width = LANES if c < full else rest
            stage_ref[c, pl.ds(level * share, share), pl.ds(0, width)] = w_ref[level, :, pl.ds(c * LANES, width)]
    for g in range(levels // group):
        mixed = [None, None]
        for f in range(FIELDS):
            extra = merge(g, f * TILES)
            for half, m in enumerate(merges):
                at = WINDS + f * SLOT
                moved = pltpu.roll(extra[half], (at - (m - REACH)) % LANES, 1)
                mixed[half] = moved if f == 0 else jnp.where(lane < at, mixed[half], moved)
        tiles = [stage_ref[c, pl.ds(g * ROWS, ROWS), :] for c in range(full + 1)]
        merged, extra = windows(tiles[0], tiles[2], tiles[5])
        speed, couple = by_level(speed_ref, g), by_level(couple_ref, g)
        for half, m in enumerate(merges):
            parts = tiles[TILES * half : TILES * half + 2] + [merged[half]]
            wind, left = parts[TILES - 1], pltpu.roll(parts[TILES - 1], LANES - SLOT * FIELDS, 1)
            for c in reversed(range(TILES - 1)):
                wind = jnp.where(jnp.logical_or(turn == c, turn == TILES + c), parts[c], wind)
                by = (c + 1) * SLOT * FIELDS
                left = jnp.where(lane < by, pltpu.roll(parts[c], by, 1), left)
            wind = jnp.where(turn < 2 * TILES, wind, left)
            value = jnp.where(lane < WINDS, wind, mixed[half])
            value = jnp.where(lane == WINDS + SLOT, speed, value)
            value = jnp.where(lane == WINDS + 2 * SLOT - 1, couple, value)
            ends = pltpu.roll(extra[half], LANES - 1 - m, 1)
            value = jnp.where(lane >= LANES - 2, ends, value)
            out_ref[place(half, g, MIXED)] = value

    for g in range(levels // group):
        for f in range(FIELDS):
            merge(g, (FIELDS + f) * TILES)


def layer_kernel(lon, merges, subwins, in_ref, out_ref):
    half = lax.axis_index("ens")
    lane = lax.broadcasted_iota(jnp.int32, (ROWS, LANES), 1)
    row = lax.broadcasted_iota(jnp.int32, (ROWS, LANES), 0)
    below = lane < jnp.where(half == 0, merges[0], merges[1])
    free_lo = jnp.where(half == 0, merges[0] - 3 * REACH, merges[1] - 3 * REACH)
    free = jnp.logical_and(lane >= free_lo, lane < free_lo + FREE)

    def load(member, t, k):
        return in_ref[pl.ds((member * subwins + t) * ROWS * ROWS_IN + k, ROWS, stride=ROWS_IN), :]

    def of_half(values):
        return jnp.where(half == 0, values[0] % LANES, values[1] % LANES)

    mixed = [[load(member, t, MIXED) for t in range(subwins)] for member in range(2)]
    speed_at, couple_at = WINDS + SLOT, WINDS + 2 * SLOT - 1
    speed = 0.5 * jnp.broadcast_to(mixed[0][0][:, speed_at : speed_at + 1], (ROWS, LANES))
    couple = jnp.broadcast_to(mixed[0][0][:, couple_at : couple_at + 1], (ROWS, LANES))

    def back(x, by):
        moved = [pltpu.roll(v, by, 1) for v in x]
        return [jnp.where(lane < by, moved[i - 1], v) for i, v in enumerate(moved)]

    def ahead(x, by):
        moved = [pltpu.roll(v, LANES - by, 1) for v in x]
        return [jnp.where(lane >= LANES - by, moved[(i + 1) % len(x)], v) for i, v in enumerate(moved)]

    def up(x, by):
        return [pltpu.roll(v, ROWS - by, 0) for v in x]

    def down(x, by):
        return [pltpu.roll(v, by, 0) for v in x]

    def staggered(f, x):
        if f == 1:
            return ahead(x, 1)
        if f == 2:
            return up(x, 1)
        return x

    def aligned(f, x):
        if f == 1:
            return back(x, 1)
        if f == 2:
            return down(x, 1)
        return x

    def widened(x, extra):
        return x[:2] + [jnp.where(below, x[2], extra), jnp.where(below, extra, x[2])]

    def narrowed(x):
        return x[:2] + [jnp.where(below, x[2], x[3])]

    def fields_of(member, t, at):
        return [[load(member, t, (at + f) * TILES + c) for c in range(TILES)] for f in range(FIELDS)]

    def extras_of(member, t):
        shifts = [of_half([m - REACH - WINDS - f * SLOT for m in merges]) for f in range(FIELDS)]
        return [pltpu.roll(mixed[member][t], by, 1) for by in shifts]

    def stag(state):
        return [staggered(f, x) for f, x in enumerate(state)]

    def wind(comp):
        sent = [mixed[turn % 2][turn // 2] for turn in range(2 * subwins)]
        left = sent[2 * TILES + comp]
        tiles = []
        for c in range(TILES):
            by = WINDS - c * SLOT * FIELDS
            tiles.append(jnp.where(lane < WINDS, sent[comp * TILES + c], pltpu.roll(left, by, 1)))
        return tiles, pltpu.roll(sent[comp * TILES], of_half([m + 1 - LANES for m in merges]), 1)

    stay = 1.0 - 4.0 * diffusion
    grad_p = jnp.where(row == ROWS - 2, 0.0, speed)
    grad_m = jnp.where(row == ROWS - 1, 0.0, speed)
    div_p = jnp.where(row == ROWS - 1, 0.0, speed)
    div_m = jnp.where(row == 0, 0.0, speed)

    def coefficients(east, north):
        return (
            [diffusion - 0.5 * v for v in east],
            [diffusion + 0.5 * v for v in east],
            [jnp.where(row == ROWS - 1, 0.0, diffusion - 0.5 * v) for v in north],
            [jnp.where(row == 0, 0.0, diffusion + 0.5 * v) for v in north],
        )

    (east, east_extra), (north, north_extra) = wind(0), wind(1)
    narrow = coefficients(east, north)
    wide = coefficients(widened(east, east_extra), widened(north, north_extra))

    def tangent(state, coefs):
        h, u, v, q = state
        u = [a - speed * (n - m) for a, n, m in zip(u, ahead(h, 2), h)]
        v = [a - (grad_p * n - grad_m * m) for a, n, m in zip(v, up(h, 2), h)]
        h = [
            a - (speed * (p - m) + (div_p * n - div_m * s))
            for a, p, m, n, s in zip(h, u, back(u, 2), v, down(v, 2))
        ]
        q = [
            stay * a + (em * e + ep * w) + (nm * n + np * s) + couple * p
            for a, em, e, ep, w, nm, n, np, s, p in zip(
                q, coefs[0], ahead(q, 1), coefs[1], back(q, 1), coefs[2], up(q, 1), coefs[3], down(q, 1), h
            )
        ]
        return [h, u, v, q]

    def adjoint(state, coefs):
        h, u, v, q = state
        h = [a + couple * b for a, b in zip(h, q)]
        u = [a + speed * (n - m) for a, n, m in zip(u, ahead(h, 2), h)]
        v = [a + (grad_p * n - grad_m * m) for a, n, m in zip(v, up(h, 2), h)]
        h = [
            a + (speed * (p - m) + (div_p * n - div_m * s))
            for a, p, m, n, s in zip(h, u, back(u, 2), v, down(v, 2))
        ]
        e = ahead([a * b for a, b in zip(coefs[1], q)], 1)
        w = back([a * b for a, b in zip(coefs[0], q)], 1)
        n = up([a * b for a, b in zip(coefs[3], q)], 1)
        s = down([a * b for a, b in zip(coefs[2], q)], 1)
        q = [stay * a + (b + c) + (d + f) for a, b, c, d, f in zip(q, e, w, n, s)]
        return [h, u, v, q]

    def each(fn, *states):
        return [[fn(*vals) for vals in zip(*xs)] for xs in zip(*states)]

    def operate(p, p_wide, precision, observed):
        weighted = []
        for t in range(subwins):
            change = p[t]
            if t > 0:
                moved, coefs = (p[t - 1], narrow) if p_wide is None else (p_wide[t - 1], wide)
                for _ in range(STEPS):
                    moved = tangent(moved, coefs)
                if p_wide is not None:
                    moved = [narrowed(x) for x in moved]
                change = each(lambda a, b: a - b, change, moved)
            weighted.append(each(lambda a, b: a * b, precision[t], change))
        image = []
        for t in range(subwins):
            out = each(lambda w, o, d: w + o * d, weighted[t], observed[t], p[t])
            if t + 1 < subwins:
                moved = weighted[t + 1]
                for _ in range(STEPS):
                    moved = adjoint(moved, narrow)
                out = each(lambda a, b: a - b, out, moved)
            image.append(out)
        return image

    def flat(x):
        return [(c, v) for state in x for field in state for c, v in enumerate(field)]

    def total(terms):
        inner, edge = None, None
        for c, v in terms:
            if c < TILES - 1:
                inner = v if inner is None else inner + v
            else:
                edge = v if edge is None else edge + v
        both = inner + jnp.where(free, 0.0, edge)
        return jnp.sum(both, axis=(0, 1), keepdims=True)

    def dot(x, y):
        return total([(c, v * w) for (c, v), (_, w) in zip(x, y)])

    precision = [stag(fields_of(0, t, FIELDS)) for t in range(subwins)]
    observed = [stag(fields_of(1, t, FIELDS)) for t in range(subwins)]
    for member in range(2):
        plain = [fields_of(member, t, 0) for t in range(subwins)]
        b_wide = [
            stag([widened(x, e) for x, e in zip(plain[t], extras_of(member, t))]) for t in range(subwins - 1)
        ]
        b = [[narrowed(x) for x in state] for state in b_wide] + [stag(plain[-1])]
        one = operate(b, b_wide, precision, observed)
        two = operate(one, None, precision, observed)
        one, two = [[[aligned(f, x) for f, x in enumerate(state)] for state in y] for y in (one, two)]
        f0, f1, f2 = flat(plain), flat(one), flat(two)
        s00, s01, s11, s02, s12 = dot(f0, f0), dot(f0, f1), dot(f1, f1), dot(f0, f2), dot(f1, f2)
        step = jnp.where(s11 > 0.0, s01 / jnp.where(s11 > 0.0, s11, 1.0), 0.0)
        more = 2.0 - jnp.where(s00 > 0.0, step * s01 / jnp.where(s00 > 0.0, s00, 1.0), 0.0)
        step_t = jnp.broadcast_to(step, (ROWS, LANES))
        more_t = jnp.broadcast_to(more, (ROWS, LANES))
        res = [(c, v - step_t * w) for (c, v), (_, w) in zip(f0, f1)]
        mov = [(c, more_t * v - step_t * w) for (c, v), (_, w) in zip(f0, f1)]
        img = [(c, more_t * v - step_t * w) for (c, v), (_, w) in zip(f1, f2)]
        sums = [step, more, s00, s01, s11, s02, s12, dot(res, res), dot(mov, img)]
        sums += [sums[-1]] * (-len(sums) % 6)
        for t in range(subwins):

            def put(k, value):
                start = (member * subwins + t) * ROWS * ROWS_OUT + k
                out_ref[pl.ds(start, ROWS, stride=ROWS_OUT), :] = value

            images = one[t] + two[t]
            last = images[-1][TILES - 1]
            for k, x in enumerate(images):
                put(2 * k, x[0])
                put(2 * k + 1, x[1])
                if k < 5:
                    put(THIRDS + k, jnp.where(free, pltpu.roll(last, (-(k + 1) * FREE) % LANES, 1), x[2]))
                elif k < 2 * FIELDS - 1:
                    rows = []
                    for i in (k - 5, k - 3):
                        value = sums[3 * i + 2]
                        for j in (1, 0):
                            value = jnp.where(lane < free_lo + (j + 1) * SLOT, sums[3 * i + j], value)
                        rows.append(value)
                    put(THIRDS + k, jnp.where(free, jnp.where(row % 2 == 0, rows[0], rows[1]), x[2]))


def finish_kernel(lon, merges, b_ref, in_ref, x_hbm, r_hbm, x_ref, r_ref, last_ref, sems):
    _, levels, share, _ = b_ref.shape
    full = lon // LANES
    rest = lon - full * LANES
    size = share * ROWS_OUT
    apart = merges[0] - merges[1]
    at_lane = merges[0] - 3 * REACH

    group = ROWS // share

    slots = []
    for i in range(3):
        at = THIRDS + 5 + i % 2 + (i // 2) * ROWS_OUT
        halves = [in_ref[pl.ds(half * levels * size + at, levels, stride=size), :] for half in range(2)]
        slots.append(jnp.concatenate([halves[0], pltpu.roll(halves[1], apart, 1)], axis=0))

    def sums(i):
        value = slots[i // 3]
        return pltpu.roll(value, LANES - (i % 3) * SLOT, 1) if i % 3 else value

    step, more, s00, s01, s11, s02, s12, rr, mi = [sums(i) for i in range(9)]

    def total(x):
        return jnp.sum(x, axis=0, keepdims=True)

    norm_0 = total(s00)
    alpha_0 = norm_0 / total(s01)
    d = step - alpha_0
    norm_1 = total(rr + d * (2.0 * (s01 - step * s11) + d * s11))
    beta = norm_1 / norm_0
    g = (1.0 + beta) - more
    cross_d = more * (s02 + s11) - 2.0 * step * s12
    cross_g = 2.0 * more * s01 - step * (s11 + s02)
    curve = total(mi + d * (cross_d + d * s12 + g * (s11 + s02)) + g * (cross_g + g * s01))
    alpha_1 = norm_1 / curve
    first = alpha_0 + alpha_1 * (1.0 + beta)
    second = alpha_0 * alpha_1
    first = jnp.broadcast_to(first[:, at_lane : at_lane + 1], (share, LANES))
    second = jnp.broadcast_to(second[:, at_lane : at_lane + 1], (share, LANES))
    lane = lax.broadcasted_iota(jnp.int32, (share, LANES), 1)

    def gather_last():
        lane_8 = lax.broadcasted_iota(jnp.int32, (ROWS, LANES), 1)
        for half in range(2):
            for g in range(levels // group):
                value = None
                for k in range(5):
                    start = (half * levels + g * group) * size + THIRDS + k
                    part = pltpu.roll(in_ref[pl.ds(start, ROWS, stride=ROWS_OUT), :], (k + 1) * FREE % LANES, 1)
                    begin = (merges[half] - 3 * REACH + (k + 1) * FREE) % LANES
                    here = jnp.logical_and(lane_8 >= begin, lane_8 < begin + FREE)
                    value = part if value is None else jnp.where(here, part, value)
                last_ref[half, pl.ds(g * ROWS, ROWS), :] = value

    def image(level, k):
        got = []
        for half in range(2):
            start = (half * levels + level) * size
            tiles = [in_ref[pl.ds(start + 2 * k + c, share, stride=ROWS_OUT), :] for c in range(2)]
            if k < 2 * FIELDS - 1:
                tiles.append(in_ref[pl.ds(start + THIRDS + k, share, stride=ROWS_OUT), :])
            else:
                tiles.append(last_ref[half, pl.ds(level * share, share), :])
            got.append(tiles)
        middle = jnp.where(lane < at_lane, got[0][2], got[1][2])
        return got[0][:2] + [middle] + got[1]

    copies = []
    for f in range(FIELDS):
        if f == FIELDS - 1:
            gather_last()
        for level in range(levels):
            b = b_ref[f, level]
            ones, twos = image(level, f), image(level, FIELDS + f)
            for c, (one, two) in enumerate(zip(ones, twos)):
                width = LANES if c < full else rest
                cols = pl.ds(c * LANES, width)
                one, two = one[:, :width], two[:, :width]
                part = b[:, c * LANES : c * LANES + width]
                x_ref[f, level, :, cols] = first[:, :width] * part - second[:, :width] * one
                r_ref[f, level, :, cols] = (part - first[:, :width] * one) + second[:, :width] * two
        for i, (src, dst) in enumerate(((x_ref, x_hbm), (r_ref, r_hbm))):
            copies.append(pltpu.make_async_copy(src.at[f], dst.at[f], sems.at[i, f]))
            copies[-1].start()
    for copy in copies:
        copy.wait()


def by_layer(right_side, error_precision, obs_count, background_wind, wave_speed, tracer_coupling):
    _, fields, levels, share, lon = right_side.shape
    subwins = lax.axis_size("tm")
    merges = merge_lanes(lon)
    vmem = pl.BlockSpec(memory_space=pltpu.VMEM)
    hbm = pl.BlockSpec(memory_space=pltpu.HBM)
    params = pltpu.CompilerParams(vmem_limit_bytes=48 * 1024 * 1024)
    state = (fields, levels, share, lon)

    def exchange(x):
        x = x.reshape(2 * levels, -1, 1, LANES)
        return lax.all_to_all(x, ("ens", "tm", "space"), 0, 0, tiled=True).reshape(-1, LANES)

    b = right_side.reshape(state)
    given = (b, error_precision.reshape(state), obs_count.reshape(state), background_wind, wave_speed, tracer_coupling)
    with jax.named_scope("pack"):
        packed = pl.pallas_call(
            lambda *refs: pack_kernel(lon, merges, *refs),
            out_shape=jax.ShapeDtypeStruct((2 * levels * share * ROWS_IN, LANES), jnp.float32),
            in_specs=[hbm] * len(given),
            out_specs=vmem,
            scratch_shapes=[
                pltpu.VMEM(state, jnp.float32),
                pltpu.VMEM(state, jnp.float32),
                pltpu.VMEM(state, jnp.int32),
                pltpu.VMEM(background_wind.shape[1:], jnp.float32),
                pltpu.SMEM(wave_speed.shape, jnp.float32),
                pltpu.SMEM(tracer_coupling.shape, jnp.float32),
                pltpu.VMEM((lon // LANES + 1, levels * share, LANES), jnp.float32),
                pltpu.SemaphoreType.DMA((2 * FIELDS + 3,)),
            ],
            compiler_params=params,
        )(*[pltpu.with_memory_space_constraint(x, pltpu.HBM) for x in given])
    packed = exchange(packed)
    with jax.named_scope("layer"):
        images = pl.pallas_call(
            lambda *refs: layer_kernel(lon, merges, subwins, *refs),
            out_shape=jax.ShapeDtypeStruct((2 * levels * share * ROWS_OUT, LANES), jnp.float32),
            in_specs=[vmem],
            out_specs=vmem,
            compiler_params=params,
        )(packed)
    images = exchange(images)
    with jax.named_scope("finish"):
        x, r = pl.pallas_call(
            lambda *refs: finish_kernel(lon, merges, *refs),
            out_shape=[jax.ShapeDtypeStruct(state, jnp.float32)] * 2,
            in_specs=[vmem] * 2,
            out_specs=[hbm] * 2,
            scratch_shapes=[
                pltpu.VMEM(state, jnp.float32),
                pltpu.VMEM(state, jnp.float32),
                pltpu.VMEM((2, levels * share, LANES), jnp.float32),
                pltpu.SemaphoreType.DMA((2, FIELDS)),
            ],
            compiler_params=params,
        )(b, images)
    return x.reshape(right_side.shape), r.reshape(right_side.shape)


def fits_by_layer(mesh, shape):
    space, tm, ens = mesh.shape["space"], mesh.shape["tm"], mesh.shape["ens"]
    subwins, fields, levels, lats, lon = shape
    return (
        (ens, tm, space, fields, lats) == (2, 4, 4, FIELDS, ROWS)
        and subwins == ens * tm
        and levels == space * tm
        and lon == 720
    )


def extended_2(cells, sides, width):
    for axis, dim in sides:
        count = lax.axis_size(axis)
        ends = count - 1
        head = lax.slice_in_dim(cells, 0, width, axis=dim)
        tail = lax.slice_in_dim(cells, cells.shape[dim] - width, cells.shape[dim], axis=dim)
        cells = jnp.concatenate(
            [
                lax.ppermute(tail, axis, [(i, (i + 1) % count) for i in range(ends)]),
                cells,
                lax.ppermute(head, axis, [((i + 1) % count, i) for i in range(ends)]),
            ],
            axis=dim,
        )
    return cells


def shifted(value, axis, by):
    peers = lax.axis_size(axis)
    pairs = [(i, i + by) for i in range(peers) if 0 <= i + by < peers]
    return lax.ppermute(value, axis, pairs)


def along_x(field):
    return 0.5 * (jnp.roll(field, -1, axis=-1) - jnp.roll(field, 1, axis=-1))


def second_x(field):
    return jnp.roll(field, -1, axis=-1) + jnp.roll(field, 1, axis=-1) - 2.0 * field


def along_y(extended):
    return 0.5 * (extended[..., 2:, :] - extended[..., :-2, :])


def trimmed(field, count):
    if count == 0:
        return field
    return field[..., count : field.shape[-2] - count, :]


def row_valid(lat_rows):
    first_row = lax.axis_index("space") * lat_rows - 4
    row_total = lat_rows * lax.axis_size("space")
    global_rows = first_row + jnp.arange(lat_rows + 8, dtype=jnp.int32)
    inside = jnp.logical_and(global_rows >= 0, global_rows < row_total)
    return inside.astype(jnp.float32)[:, None]


def tangent_core(state, margin, coefs):
    speed_col, couple_col, winds, have, valid = coefs
    height, east, north, tracer = (state[:, 0], state[:, 1], state[:, 2], state[:, 3])
    east_mid = east - speed_col * along_x(height)
    north_mid = (trimmed(north, 1) - speed_col * along_y(height)) * trimmed(valid, 5 - margin)
    height_new = trimmed(height, 2) - speed_col * (
        along_x(trimmed(east_mid, 2)) + along_y(north_mid)
    )
    tracer_one = trimmed(tracer, 1)
    inner = trimmed(tracer, 2)
    tracer_lap = second_x(inner) + tracer_one[..., 2:, :] + tracer_one[..., :-2, :] - 2.0 * inner
    wind_east = trimmed(winds[0], have - margin + 2)
    wind_north = trimmed(winds[1], have - margin + 2)
    tracer_new = (
        inner
        - wind_east * along_x(inner)
        - wind_north * along_y(tracer_one)
        + diffusion * tracer_lap
        + couple_col * height_new
    )
    result = jnp.stack(
        [height_new, trimmed(east_mid, 2), trimmed(north_mid, 1), tracer_new], axis=1
    )
    return result * trimmed(valid, 6 - margin)


def adjoint_core(state, margin, coefs):
    speed_col, couple_col, winds, have, valid = coefs
    height, east, north, tracer = (state[:, 0], state[:, 1], state[:, 2], state[:, 3])
    height_mix = height + couple_col * tracer
    east_mid = east + speed_col * along_x(height_mix)
    north_mid = (trimmed(north, 1) + speed_col * along_y(height_mix)) * trimmed(valid, 5 - margin)
    height_new = trimmed(height_mix, 2) + speed_col * (
        along_x(trimmed(east_mid, 2)) + along_y(north_mid)
    )
    tracer_one = trimmed(tracer, 1)
    inner = trimmed(tracer, 2)
    tracer_lap = second_x(inner) + tracer_one[..., 2:, :] + tracer_one[..., :-2, :] - 2.0 * inner
    wind_east = trimmed(winds[0], have - margin + 2)
    wind_north = trimmed(winds[1], have - margin + 1)
    tracer_new = (
        inner
        + along_x(wind_east * inner)
        + along_y(wind_north * tracer_one)
        + diffusion * tracer_lap
    )
    result = jnp.stack(
        [height_new, trimmed(east_mid, 2), trimmed(north_mid, 1), tracer_new], axis=1
    )
    return result * trimmed(valid, 6 - margin)


def rebuild(state, sent):
    widths = [(0, 0)] * (state.ndim - 3) + [(2, 2), (0, 0)]
    east_wide = jnp.pad(state[:, 1], widths)
    return jnp.stack([sent[:, 0], east_wide, sent[:, 1], sent[:, 2]], axis=1)


def tangent_near(state):
    picked = jnp.stack([state[:, 0], state[:, 2], state[:, 3]], axis=1)
    sent = extended_2(picked, (("space", 3),), 2)
    return rebuild(state, sent)


def adjoint_near(state):
    picked = jnp.stack([state[:, 0], state[:, 2], state[:, 3]], axis=1)
    sent = extended_2(picked, (("space", 3),), 2)
    return rebuild(state, sent)


def propagate(fields, step_core, near_fn, coefs):
    current = fields
    for step in range(STEPS):
        current = step_core(near_fn(current), 2, coefs)
    return current


def operate(direction, error_precision, observed, coefs):
    moved = propagate(direction, tangent_core, tangent_near, coefs)
    incoming = shifted(moved, "tm", 1)
    previous = jnp.concatenate([incoming, moved[:-1]], axis=0)
    weighted = error_precision * (direction - previous)
    back = propagate(weighted, adjoint_core, adjoint_near, coefs)
    arriving = shifted(back, "tm", -1)
    following = jnp.concatenate([back[1:], arriving], axis=0)
    return weighted - following + observed * direction


def squares(residual):
    return lax.psum(jnp.sum(residual * residual), ("space", "tm"))


def on_device(right_side, error_precision, obs_count, background_wind, wave_speed, tracer_coupling):
    lat_rows = right_side.shape[3]
    valid = row_valid(lat_rows)
    winds = extended_2(background_wind, (("space", 2),), 1)
    have = 1
    coefs = (wave_speed[:, None, None], tracer_coupling[:, None, None], winds, have, valid)
    observed = obs_count.astype(jnp.float32)
    solution_field = jnp.zeros_like(right_side)
    residual = right_side
    direction = right_side
    norm_now = squares(residual)
    for step in range(ITERS):
        image = operate(direction, error_precision, observed, coefs)
        alpha = norm_now / lax.psum(jnp.sum(direction * image), ("space", "tm"))
        solution_field = solution_field + alpha * direction
        residual = residual - alpha * image
        norm_next = squares(residual)
        direction = residual + norm_next / norm_now * direction
        norm_now = norm_next
    return (solution_field, residual)


def solution(mesh):
    def run(right_side, *others):
        body = by_layer if fits_by_layer(mesh, right_side.shape) else on_device
        return jax.shard_map(
            body,
            mesh=mesh,
            in_specs=(
                P(("ens", "tm"), None, None, "space", None),
                P("tm", None, None, "space", None),
                P("tm", None, None, "space", None),
                P(None, None, "space", None),
                P(),
                P(),
            ),
            out_specs=(
                P(("ens", "tm"), None, None, "space", None),
                P(("ens", "tm"), None, None, "space", None),
            ),
            check_vma=False,
        )(right_side, *others)

    return run
```

```python
import jax
import jax.numpy as jnp
from jax import lax
from jax.experimental import pallas as pl
from jax.experimental.pallas import tpu as pltpu
from jax.sharding import PartitionSpec as P

STEPS = 2
ITERS = 2


diffusion = 0.1


LANES = 128
ROWS = 8
TILES = 3
REACH = 4
FIELDS = 4
SLOT = 2 * REACH
WINDS = LANES - FIELDS * SLOT
FREE = 6 * REACH
MIXED = 2 * FIELDS * TILES
ROWS_IN = MIXED + 1
THIRDS = 4 * FIELDS
ROWS_OUT = THIRDS + 2 * FIELDS - 1


def merge_lanes(lon):
    core = lon // 2
    return (core + 3 * REACH) % LANES, (core - 3 * REACH) % LANES


def pack_kernel(
    lon, merges, b_hbm, e_hbm, o_hbm, w_hbm, speed_hbm, couple_hbm, out_ref,
    b_ref, e_ref, o_ref, w_ref, speed_ref, couple_ref, stage_ref, sems,
):
    _, levels, share, _ = b_ref.shape
    full = lon // LANES
    rest = lon - full * LANES
    member = lax.axis_index("ens")
    turn = lax.axis_index("tm") * 2 + member
    comp = jnp.where(turn < 2 * TILES, turn // TILES, turn - 2 * TILES)

    def in_halves(hbm, ref, first):
        n = FIELDS // 2
        return [
            pltpu.make_async_copy(hbm.at[pl.ds(i * n, n)], ref.at[pl.ds(i * n, n)], sems.at[first + i]) for i in range(2)
        ]

    def start(copies):
        for copy in copies:
            copy.start()

    copies_b, copies_e, copies_o = in_halves(b_hbm, b_ref, 0), in_halves(e_hbm, e_ref, 2), in_halves(o_hbm, o_ref, 7)
    others = (
        pltpu.make_async_copy(w_hbm.at[comp], w_ref, sems.at[4]),
        pltpu.make_async_copy(speed_hbm, speed_ref, sems.at[5]),
        pltpu.make_async_copy(couple_hbm, couple_ref, sems.at[6]),
    )
    start(copies_b)
    pl.when(member == 0)(lambda: start(copies_e))
    pl.when(member != 0)(lambda: start(copies_o))
    start(others)
    lane = lax.broadcasted_iota(jnp.int32, (ROWS, LANES), 1)
    row = lax.broadcasted_iota(jnp.int32, (ROWS, LANES), 0)
    group = ROWS // share

    def raw(copies, ref, first):
        for f in range(FIELDS):
            if f % 2 == 0:
                copies[f // 2].wait()
            for level in range(levels):
                for c in range(full + 1):
                    half, tile = c // TILES, c % TILES
                    width = LANES if c < full else rest
                    value = ref[f, level, :, pl.ds(c * LANES, width)].astype(jnp.float32)
                    start = (half * levels + level) * share * ROWS_IN + first + f * TILES + tile
                    out_ref[pl.ds(start, share, stride=ROWS_IN), pl.ds(0, width)] = value

    def place(half, g, k):
        return pl.ds((half * levels + g * group) * share * ROWS_IN + k, ROWS, stride=ROWS_IN), slice(None)

    def windows(first, third, last):
        before = pltpu.roll(last, LANES - rest, 1)
        after = jnp.where(lane < rest, last, pltpu.roll(first, rest, 1))
        ends = ((third, before), (after, third))
        merged = [jnp.where(lane < m, x, y) for m, (x, y) in zip(merges, ends)]
        extra = [jnp.where(lane < m, y, x) for m, (x, y) in zip(merges, ends)]
        return merged, extra

    def merge(g, k):
        merged, extra = windows(
            out_ref[place(0, g, k)], out_ref[place(0, g, k + TILES - 1)], out_ref[place(1, g, k + TILES - 1)]
        )
        for half in range(2):
            out_ref[place(half, g, k + TILES - 1)] = merged[half]
        return extra

    def by_level(ref, g):
        value = jnp.full((ROWS, LANES), ref[g * group], jnp.float32)
        for i in range(1, group):
            value = jnp.where(row < i * share, value, ref[g * group + i])
        return value

    raw(copies_b, b_ref, 0)
    pl.when(member == 0)(lambda: raw(copies_e, e_ref, FIELDS * TILES))
    pl.when(member != 0)(lambda: raw(copies_o, o_ref, FIELDS * TILES))
    for copy in others:
        copy.wait()
    for level in range(levels):
        for c in range(full + 1):
            width = LANES if c < full else rest
            stage_ref[c, pl.ds(level * share, share), pl.ds(0, width)] = w_ref[level, :, pl.ds(c * LANES, width)]
    for g in range(levels // group):
        mixed = [None, None]
        for f in range(FIELDS):
            extra = merge(g, f * TILES)
            for half, m in enumerate(merges):
                at = WINDS + f * SLOT
                moved = pltpu.roll(extra[half], (at - (m - REACH)) % LANES, 1)
                mixed[half] = moved if f == 0 else jnp.where(lane < at, mixed[half], moved)
        tiles = [stage_ref[c, pl.ds(g * ROWS, ROWS), :] for c in range(full + 1)]
        merged, extra = windows(tiles[0], tiles[2], tiles[5])
        speed, couple = by_level(speed_ref, g), by_level(couple_ref, g)
        for half, m in enumerate(merges):
            parts = tiles[TILES * half : TILES * half + 2] + [merged[half]]
            wind, left = parts[TILES - 1], pltpu.roll(parts[TILES - 1], LANES - SLOT * FIELDS, 1)
            for c in reversed(range(TILES - 1)):
                wind = jnp.where(jnp.logical_or(turn == c, turn == TILES + c), parts[c], wind)
                by = (c + 1) * SLOT * FIELDS
                left = jnp.where(lane < by, pltpu.roll(parts[c], by, 1), left)
            wind = jnp.where(turn < 2 * TILES, wind, left)
            value = jnp.where(lane < WINDS, wind, mixed[half])
            value = jnp.where(lane == WINDS + SLOT, speed, value)
            value = jnp.where(lane == WINDS + 2 * SLOT - 1, couple, value)
            ends = pltpu.roll(extra[half], LANES - 1 - m, 1)
            value = jnp.where(lane >= LANES - 2, ends, value)
            out_ref[place(half, g, MIXED)] = value

    for g in range(levels // group):
        for f in range(FIELDS):
            merge(g, (FIELDS + f) * TILES)


def layer_kernel(lon, merges, subwins, in_ref, out_ref):
    half = lax.axis_index("ens")
    lane = lax.broadcasted_iota(jnp.int32, (ROWS, LANES), 1)
    row = lax.broadcasted_iota(jnp.int32, (ROWS, LANES), 0)
    below = lane < jnp.where(half == 0, merges[0], merges[1])
    free_lo = jnp.where(half == 0, merges[0] - 3 * REACH, merges[1] - 3 * REACH)
    free = jnp.logical_and(lane >= free_lo, lane < free_lo + FREE)

    def load(member, t, k):
        return in_ref[pl.ds((member * subwins + t) * ROWS * ROWS_IN + k, ROWS, stride=ROWS_IN), :]

    def of_half(values):
        return jnp.where(half == 0, values[0] % LANES, values[1] % LANES)

    mixed = [[load(member, t, MIXED) for t in range(subwins)] for member in range(2)]
    speed_at, couple_at = WINDS + SLOT, WINDS + 2 * SLOT - 1
    speed = 0.5 * jnp.broadcast_to(mixed[0][0][:, speed_at : speed_at + 1], (ROWS, LANES))
    couple = jnp.broadcast_to(mixed[0][0][:, couple_at : couple_at + 1], (ROWS, LANES))

    def back(x, by):
        moved = [pltpu.roll(v, by, 1) for v in x]
        return [jnp.where(lane < by, moved[i - 1], v) for i, v in enumerate(moved)]

    def ahead(x, by):
        moved = [pltpu.roll(v, LANES - by, 1) for v in x]
        return [jnp.where(lane >= LANES - by, moved[(i + 1) % len(x)], v) for i, v in enumerate(moved)]

    def up(x, by):
        return [pltpu.roll(v, ROWS - by, 0) for v in x]

    def down(x, by):
        return [pltpu.roll(v, by, 0) for v in x]

    def staggered(f, x):
        if f == 1:
            return ahead(x, 1)
        if f == 2:
            return up(x, 1)
        return x

    def aligned(f, x):
        if f == 1:
            return back(x, 1)
        if f == 2:
            return down(x, 1)
        return x

    def widened(x, extra):
        return x[:2] + [jnp.where(below, x[2], extra), jnp.where(below, extra, x[2])]

    def narrowed(x):
        return x[:2] + [jnp.where(below, x[2], x[3])]

    def fields_of(member, t, at):
        return [[load(member, t, (at + f) * TILES + c) for c in range(TILES)] for f in range(FIELDS)]

    def extras_of(member, t):
        shifts = [of_half([m - REACH - WINDS - f * SLOT for m in merges]) for f in range(FIELDS)]
        return [pltpu.roll(mixed[member][t], by, 1) for by in shifts]

    def stag(state):
        return [staggered(f, x) for f, x in enumerate(state)]

    def wind(comp):
        sent = [mixed[turn % 2][turn // 2] for turn in range(2 * subwins)]
        left = sent[2 * TILES + comp]
        tiles = []
        for c in range(TILES):
            by = WINDS - c * SLOT * FIELDS
            tiles.append(jnp.where(lane < WINDS, sent[comp * TILES + c], pltpu.roll(left, by, 1)))
        return tiles, pltpu.roll(sent[comp * TILES], of_half([m + 1 - LANES for m in merges]), 1)

    stay = 1.0 - 4.0 * diffusion
    grad_p = jnp.where(row == ROWS - 2, 0.0, speed)
    grad_m = jnp.where(row == ROWS - 1, 0.0, speed)
    div_p = jnp.where(row == ROWS - 1, 0.0, speed)
    div_m = jnp.where(row == 0, 0.0, speed)

    def coefficients(east, north):
        return (
            [diffusion - 0.5 * v for v in east],
            [diffusion + 0.5 * v for v in east],
            [jnp.where(row == ROWS - 1, 0.0, diffusion - 0.5 * v) for v in north],
            [jnp.where(row == 0, 0.0, diffusion + 0.5 * v) for v in north],
        )

    (east, east_extra), (north, north_extra) = wind(0), wind(1)
    narrow = coefficients(east, north)
    wide = coefficients(widened(east, east_extra), widened(north, north_extra))

    def tangent(state, coefs):
        h, u, v, q = state
        u_back = [a - speed * (n - m) for a, n, m in zip(back(u, 2), h, back(h, 2))]
        u = [a - speed * (n - m) for a, n, m in zip(u, ahead(h, 2), h)]
        v = [a - (grad_p * n - grad_m * m) for a, n, m in zip(v, up(h, 2), h)]
        h = [
            a - (speed * (p - m) + (div_p * n - div_m * s))
            for a, p, m, n, s in zip(h, u, u_back, v, down(v, 2))
        ]
        q = [
            stay * a + (em * e + ep * w) + (nm * n + np * s) + couple * p
            for a, em, e, ep, w, nm, n, np, s, p in zip(
                q, coefs[0], ahead(q, 1), coefs[1], back(q, 1), coefs[2], up(q, 1), coefs[3], down(q, 1), h
            )
        ]
        return [h, u, v, q]

    def adjoint(state, coefs):
        h, u, v, q = state
        h = [a + couple * b for a, b in zip(h, q)]
        u_back = [a + speed * (n - m) for a, n, m in zip(back(u, 2), h, back(h, 2))]
        u = [a + speed * (n - m) for a, n, m in zip(u, ahead(h, 2), h)]
        v = [a + (grad_p * n - grad_m * m) for a, n, m in zip(v, up(h, 2), h)]
        h = [
            a + (speed * (p - m) + (div_p * n - div_m * s))
            for a, p, m, n, s in zip(h, u, u_back, v, down(v, 2))
        ]
        e = ahead([a * b for a, b in zip(coefs[1], q)], 1)
        w = back([a * b for a, b in zip(coefs[0], q)], 1)
        n = up([a * b for a, b in zip(coefs[3], q)], 1)
        s = down([a * b for a, b in zip(coefs[2], q)], 1)
        q = [stay * a + (b + c) + (d + f) for a, b, c, d, f in zip(q, e, w, n, s)]
        return [h, u, v, q]

    def each(fn, *states):
        return [[fn(*vals) for vals in zip(*xs)] for xs in zip(*states)]

    def operate(p, p_wide, precision, observed):
        weighted = []
        for t in range(subwins):
            change = p[t]
            if t > 0:
                moved, coefs = (p[t - 1], narrow) if p_wide is None else (p_wide[t - 1], wide)
                for _ in range(STEPS):
                    moved = tangent(moved, coefs)
                if p_wide is not None:
                    moved = [narrowed(x) for x in moved]
                change = each(lambda a, b: a - b, change, moved)
            weighted.append(each(lambda a, b: a * b, precision[t], change))
        image = []
        for t in range(subwins):
            out = each(lambda w, o, d: w + o * d, weighted[t], observed[t], p[t])
            if t + 1 < subwins:
                moved = weighted[t + 1]
                for _ in range(STEPS):
                    moved = adjoint(moved, narrow)
                out = each(lambda a, b: a - b, out, moved)
            image.append(out)
        return image

    def flat(x):
        return [(c, v) for state in x for field in state for c, v in enumerate(field)]

    def total(terms):
        inner, edge = None, None
        for c, v in terms:
            if c < TILES - 1:
                inner = v if inner is None else inner + v
            else:
                edge = v if edge is None else edge + v
        both = inner + jnp.where(free, 0.0, edge)
        return jnp.sum(both, axis=(0, 1), keepdims=True)

    def dot(x, y):
        return total([(c, v * w) for (c, v), (_, w) in zip(x, y)])

    precision = [stag(fields_of(0, t, FIELDS)) for t in range(subwins)]
    observed = [stag(fields_of(1, t, FIELDS)) for t in range(subwins)]
    for member in range(2):
        plain = [fields_of(member, t, 0) for t in range(subwins)]
        b_wide = [
            stag([widened(x, e) for x, e in zip(plain[t], extras_of(member, t))]) for t in range(subwins - 1)
        ]
        b = [[narrowed(x) for x in state] for state in b_wide] + [stag(plain[-1])]
        one = operate(b, b_wide, precision, observed)
        two = operate(one, None, precision, observed)
        one, two = [[[aligned(f, x) for f, x in enumerate(state)] for state in y] for y in (one, two)]
        f0, f1, f2 = flat(plain), flat(one), flat(two)
        s00, s01, s11, s02, s12 = dot(f0, f0), dot(f0, f1), dot(f1, f1), dot(f0, f2), dot(f1, f2)
        step = jnp.where(s11 > 0.0, s01 / jnp.where(s11 > 0.0, s11, 1.0), 0.0)
        more = 2.0 - jnp.where(s00 > 0.0, step * s01 / jnp.where(s00 > 0.0, s00, 1.0), 0.0)
        step_t = jnp.broadcast_to(step, (ROWS, LANES))
        more_t = jnp.broadcast_to(more, (ROWS, LANES))
        res = [(c, v - step_t * w) for (c, v), (_, w) in zip(f0, f1)]
        mov = [(c, more_t * v - step_t * w) for (c, v), (_, w) in zip(f0, f1)]
        img = [(c, more_t * v - step_t * w) for (c, v), (_, w) in zip(f1, f2)]
        sums = [step, more, s00, s01, s11, s02, s12, dot(res, res), dot(mov, img)]
        sums += [sums[-1]] * (-len(sums) % 6)
        for t in range(subwins):

            def put(k, value):
                start = (member * subwins + t) * ROWS * ROWS_OUT + k
                out_ref[pl.ds(start, ROWS, stride=ROWS_OUT), :] = value

            images = one[t] + two[t]
            last = images[-1][TILES - 1]
            for k, x in enumerate(images):
                put(2 * k, x[0])
                put(2 * k + 1, x[1])
                if k < 5:
                    put(THIRDS + k, jnp.where(free, pltpu.roll(last, (-(k + 1) * FREE) % LANES, 1), x[2]))
                elif k < 2 * FIELDS - 1:
                    rows = []
                    for i in (k - 5, k - 3):
                        value = sums[3 * i + 2]
                        for j in (1, 0):
                            value = jnp.where(lane < free_lo + (j + 1) * SLOT, sums[3 * i + j], value)
                        rows.append(value)
                    put(THIRDS + k, jnp.where(free, jnp.where(row % 2 == 0, rows[0], rows[1]), x[2]))


def finish_kernel(lon, merges, b_ref, in_ref, x_hbm, r_hbm, x_ref, r_ref, last_ref, sems):
    _, levels, share, _ = b_ref.shape
    full = lon // LANES
    rest = lon - full * LANES
    size = share * ROWS_OUT
    apart = merges[0] - merges[1]
    at_lane = merges[0] - 3 * REACH

    group = ROWS // share

    slots = []
    for i in range(3):
        at = THIRDS + 5 + i % 2 + (i // 2) * ROWS_OUT
        halves = [in_ref[pl.ds(half * levels * size + at, levels, stride=size), :] for half in range(2)]
        slots.append(jnp.concatenate([halves[0], pltpu.roll(halves[1], apart, 1)], axis=0))

    def sums(i):
        value = slots[i // 3]
        return pltpu.roll(value, LANES - (i % 3) * SLOT, 1) if i % 3 else value

    step, more, s00, s01, s11, s02, s12, rr, mi = [sums(i) for i in range(9)]

    def total(x):
        return jnp.sum(x, axis=0, keepdims=True)

    norm_0 = total(s00)
    alpha_0 = norm_0 / total(s01)
    d = step - alpha_0
    norm_1 = total(rr + d * (2.0 * (s01 - step * s11) + d * s11))
    beta = norm_1 / norm_0
    g = (1.0 + beta) - more
    cross_d = more * (s02 + s11) - 2.0 * step * s12
    cross_g = 2.0 * more * s01 - step * (s11 + s02)
    curve = total(mi + d * (cross_d + d * s12 + g * (s11 + s02)) + g * (cross_g + g * s01))
    alpha_1 = norm_1 / curve
    first = alpha_0 + alpha_1 * (1.0 + beta)
    second = alpha_0 * alpha_1
    first = jnp.broadcast_to(first[:, at_lane : at_lane + 1], (share, LANES))
    second = jnp.broadcast_to(second[:, at_lane : at_lane + 1], (share, LANES))
    lane = lax.broadcasted_iota(jnp.int32, (share, LANES), 1)

    def gather_last():
        lane_8 = lax.broadcasted_iota(jnp.int32, (ROWS, LANES), 1)
        for half in range(2):
            for g in range(levels // group):
                value = None
                for k in range(5):
                    start = (half * levels + g * group) * size + THIRDS + k
                    part = pltpu.roll(in_ref[pl.ds(start, ROWS, stride=ROWS_OUT), :], (k + 1) * FREE % LANES, 1)
                    begin = (merges[half] - 3 * REACH + (k + 1) * FREE) % LANES
                    here = jnp.logical_and(lane_8 >= begin, lane_8 < begin + FREE)
                    value = part if value is None else jnp.where(here, part, value)
                last_ref[half, pl.ds(g * ROWS, ROWS), :] = value

    def image(level, k):
        got = []
        for half in range(2):
            start = (half * levels + level) * size
            tiles = [in_ref[pl.ds(start + 2 * k + c, share, stride=ROWS_OUT), :] for c in range(2)]
            if k < 2 * FIELDS - 1:
                tiles.append(in_ref[pl.ds(start + THIRDS + k, share, stride=ROWS_OUT), :])
            else:
                tiles.append(last_ref[half, pl.ds(level * share, share), :])
            got.append(tiles)
        middle = jnp.where(lane < at_lane, got[0][2], got[1][2])
        return got[0][:2] + [middle] + got[1]

    copies = []
    for f in range(FIELDS):
        if f == FIELDS - 1:
            gather_last()
        for level in range(levels):
            b = b_ref[f, level]
            ones, twos = image(level, f), image(level, FIELDS + f)
            for c, (one, two) in enumerate(zip(ones, twos)):
                width = LANES if c < full else rest
                cols = pl.ds(c * LANES, width)
                one, two = one[:, :width], two[:, :width]
                part = b[:, c * LANES : c * LANES + width]
                x_ref[f, level, :, cols] = first[:, :width] * part - second[:, :width] * one
                r_ref[f, level, :, cols] = (part - first[:, :width] * one) + second[:, :width] * two
        for i, (src, dst) in enumerate(((x_ref, x_hbm), (r_ref, r_hbm))):
            copies.append(pltpu.make_async_copy(src.at[f], dst.at[f], sems.at[i, f]))
            copies[-1].start()
    for copy in copies:
        copy.wait()


def by_layer(right_side, error_precision, obs_count, background_wind, wave_speed, tracer_coupling):
    _, fields, levels, share, lon = right_side.shape
    subwins = lax.axis_size("tm")
    merges = merge_lanes(lon)
    vmem = pl.BlockSpec(memory_space=pltpu.VMEM)
    hbm = pl.BlockSpec(memory_space=pltpu.HBM)
    params = pltpu.CompilerParams(vmem_limit_bytes=48 * 1024 * 1024)
    state = (fields, levels, share, lon)

    def exchange(x):
        x = x.reshape(2 * levels, -1, 1, LANES)
        return lax.all_to_all(x, ("ens", "tm", "space"), 0, 0, tiled=True).reshape(-1, LANES)

    b = right_side.reshape(state)
    given = (b, error_precision.reshape(state), obs_count.reshape(state), background_wind, wave_speed, tracer_coupling)
    with jax.named_scope("pack"):
        packed = pl.pallas_call(
            lambda *refs: pack_kernel(lon, merges, *refs),
            out_shape=jax.ShapeDtypeStruct((2 * levels * share * ROWS_IN, LANES), jnp.float32),
            in_specs=[hbm] * len(given),
            out_specs=vmem,
            scratch_shapes=[
                pltpu.VMEM(state, jnp.float32),
                pltpu.VMEM(state, jnp.float32),
                pltpu.VMEM(state, jnp.int32),
                pltpu.VMEM(background_wind.shape[1:], jnp.float32),
                pltpu.SMEM(wave_speed.shape, jnp.float32),
                pltpu.SMEM(tracer_coupling.shape, jnp.float32),
                pltpu.VMEM((lon // LANES + 1, levels * share, LANES), jnp.float32),
                pltpu.SemaphoreType.DMA((9,)),
            ],
            compiler_params=params,
        )(*[pltpu.with_memory_space_constraint(x, pltpu.HBM) for x in given])
    packed = exchange(packed)
    with jax.named_scope("layer"):
        images = pl.pallas_call(
            lambda *refs: layer_kernel(lon, merges, subwins, *refs),
            out_shape=jax.ShapeDtypeStruct((2 * levels * share * ROWS_OUT, LANES), jnp.float32),
            in_specs=[vmem],
            out_specs=vmem,
            compiler_params=params,
        )(packed)
    images = exchange(images)
    with jax.named_scope("finish"):
        x, r = pl.pallas_call(
            lambda *refs: finish_kernel(lon, merges, *refs),
            out_shape=[jax.ShapeDtypeStruct(state, jnp.float32)] * 2,
            in_specs=[vmem] * 2,
            out_specs=[hbm] * 2,
            scratch_shapes=[
                pltpu.VMEM(state, jnp.float32),
                pltpu.VMEM(state, jnp.float32),
                pltpu.VMEM((2, levels * share, LANES), jnp.float32),
                pltpu.SemaphoreType.DMA((2, FIELDS)),
            ],
            compiler_params=params,
        )(b, images)
    return x.reshape(right_side.shape), r.reshape(right_side.shape)


def fits_by_layer(mesh, shape):
    space, tm, ens = mesh.shape["space"], mesh.shape["tm"], mesh.shape["ens"]
    subwins, fields, levels, lats, lon = shape
    return (
        (ens, tm, space, fields, lats) == (2, 4, 4, FIELDS, ROWS)
        and subwins == ens * tm
        and levels == space * tm
        and lon == 720
    )


def extended_2(cells, sides, width):
    for axis, dim in sides:
        count = lax.axis_size(axis)
        ends = count - 1
        head = lax.slice_in_dim(cells, 0, width, axis=dim)
        tail = lax.slice_in_dim(cells, cells.shape[dim] - width, cells.shape[dim], axis=dim)
        cells = jnp.concatenate(
            [
                lax.ppermute(tail, axis, [(i, (i + 1) % count) for i in range(ends)]),
                cells,
                lax.ppermute(head, axis, [((i + 1) % count, i) for i in range(ends)]),
            ],
            axis=dim,
        )
    return cells


def shifted(value, axis, by):
    peers = lax.axis_size(axis)
    pairs = [(i, i + by) for i in range(peers) if 0 <= i + by < peers]
    return lax.ppermute(value, axis, pairs)


def along_x(field):
    return 0.5 * (jnp.roll(field, -1, axis=-1) - jnp.roll(field, 1, axis=-1))


def second_x(field):
    return jnp.roll(field, -1, axis=-1) + jnp.roll(field, 1, axis=-1) - 2.0 * field


def along_y(extended):
    return 0.5 * (extended[..., 2:, :] - extended[..., :-2, :])


def trimmed(field, count):
    if count == 0:
        return field
    return field[..., count : field.shape[-2] - count, :]


def row_valid(lat_rows):
    first_row = lax.axis_index("space") * lat_rows - 4
    row_total = lat_rows * lax.axis_size("space")
    global_rows = first_row + jnp.arange(lat_rows + 8, dtype=jnp.int32)
    inside = jnp.logical_and(global_rows >= 0, global_rows < row_total)
    return inside.astype(jnp.float32)[:, None]


def tangent_core(state, margin, coefs):
    speed_col, couple_col, winds, have, valid = coefs
    height, east, north, tracer = (state[:, 0], state[:, 1], state[:, 2], state[:, 3])
    east_mid = east - speed_col * along_x(height)
    north_mid = (trimmed(north, 1) - speed_col * along_y(height)) * trimmed(valid, 5 - margin)
    height_new = trimmed(height, 2) - speed_col * (
        along_x(trimmed(east_mid, 2)) + along_y(north_mid)
    )
    tracer_one = trimmed(tracer, 1)
    inner = trimmed(tracer, 2)
    tracer_lap = second_x(inner) + tracer_one[..., 2:, :] + tracer_one[..., :-2, :] - 2.0 * inner
    wind_east = trimmed(winds[0], have - margin + 2)
    wind_north = trimmed(winds[1], have - margin + 2)
    tracer_new = (
        inner
        - wind_east * along_x(inner)
        - wind_north * along_y(tracer_one)
        + diffusion * tracer_lap
        + couple_col * height_new
    )
    result = jnp.stack(
        [height_new, trimmed(east_mid, 2), trimmed(north_mid, 1), tracer_new], axis=1
    )
    return result * trimmed(valid, 6 - margin)


def adjoint_core(state, margin, coefs):
    speed_col, couple_col, winds, have, valid = coefs
    height, east, north, tracer = (state[:, 0], state[:, 1], state[:, 2], state[:, 3])
    height_mix = height + couple_col * tracer
    east_mid = east + speed_col * along_x(height_mix)
    north_mid = (trimmed(north, 1) + speed_col * along_y(height_mix)) * trimmed(valid, 5 - margin)
    height_new = trimmed(height_mix, 2) + speed_col * (
        along_x(trimmed(east_mid, 2)) + along_y(north_mid)
    )
    tracer_one = trimmed(tracer, 1)
    inner = trimmed(tracer, 2)
    tracer_lap = second_x(inner) + tracer_one[..., 2:, :] + tracer_one[..., :-2, :] - 2.0 * inner
    wind_east = trimmed(winds[0], have - margin + 2)
    wind_north = trimmed(winds[1], have - margin + 1)
    tracer_new = (
        inner
        + along_x(wind_east * inner)
        + along_y(wind_north * tracer_one)
        + diffusion * tracer_lap
    )
    result = jnp.stack(
        [height_new, trimmed(east_mid, 2), trimmed(north_mid, 1), tracer_new], axis=1
    )
    return result * trimmed(valid, 6 - margin)


def rebuild(state, sent):
    widths = [(0, 0)] * (state.ndim - 3) + [(2, 2), (0, 0)]
    east_wide = jnp.pad(state[:, 1], widths)
    return jnp.stack([sent[:, 0], east_wide, sent[:, 1], sent[:, 2]], axis=1)


def tangent_near(state):
    picked = jnp.stack([state[:, 0], state[:, 2], state[:, 3]], axis=1)
    sent = extended_2(picked, (("space", 3),), 2)
    return rebuild(state, sent)


def adjoint_near(state):
    picked = jnp.stack([state[:, 0], state[:, 2], state[:, 3]], axis=1)
    sent = extended_2(picked, (("space", 3),), 2)
    return rebuild(state, sent)


def propagate(fields, step_core, near_fn, coefs):
    current = fields
    for step in range(STEPS):
        current = step_core(near_fn(current), 2, coefs)
    return current


def operate(direction, error_precision, observed, coefs):
    moved = propagate(direction, tangent_core, tangent_near, coefs)
    incoming = shifted(moved, "tm", 1)
    previous = jnp.concatenate([incoming, moved[:-1]], axis=0)
    weighted = error_precision * (direction - previous)
    back = propagate(weighted, adjoint_core, adjoint_near, coefs)
    arriving = shifted(back, "tm", -1)
    following = jnp.concatenate([back[1:], arriving], axis=0)
    return weighted - following + observed * direction


def squares(residual):
    return lax.psum(jnp.sum(residual * residual), ("space", "tm"))


def on_device(right_side, error_precision, obs_count, background_wind, wave_speed, tracer_coupling):
    lat_rows = right_side.shape[3]
    valid = row_valid(lat_rows)
    winds = extended_2(background_wind, (("space", 2),), 1)
    have = 1
    coefs = (wave_speed[:, None, None], tracer_coupling[:, None, None], winds, have, valid)
    observed = obs_count.astype(jnp.float32)
    solution_field = jnp.zeros_like(right_side)
    residual = right_side
    direction = right_side
    norm_now = squares(residual)
    for step in range(ITERS):
        image = operate(direction, error_precision, observed, coefs)
        alpha = norm_now / lax.psum(jnp.sum(direction * image), ("space", "tm"))
        solution_field = solution_field + alpha * direction
        residual = residual - alpha * image
        norm_next = squares(residual)
        direction = residual + norm_next / norm_now * direction
        norm_now = norm_next
    return (solution_field, residual)


def solution(mesh):
    def run(right_side, *others):
        body = by_layer if fits_by_layer(mesh, right_side.shape) else on_device
        return jax.shard_map(
            body,
            mesh=mesh,
            in_specs=(
                P(("ens", "tm"), None, None, "space", None),
                P("tm", None, None, "space", None),
                P("tm", None, None, "space", None),
                P(None, None, "space", None),
                P(),
                P(),
            ),
            out_specs=(
                P(("ens", "tm"), None, None, "space", None),
                P(("ens", "tm"), None, None, "space", None),
            ),
            check_vma=False,
        )(right_side, *others)

    return run
```

```python
import jax
import jax.numpy as jnp
from jax import lax
from jax.experimental import pallas as pl
from jax.experimental.pallas import tpu as pltpu
from jax.sharding import PartitionSpec as P

STEPS = 2
ITERS = 2


diffusion = 0.1


LANES = 128
ROWS = 8
TILES = 3
REACH = 4
FIELDS = 4
SLOT = 2 * REACH
WINDS = LANES - FIELDS * SLOT
FREE = 6 * REACH
MIXED = 2 * FIELDS * TILES
ROWS_IN = MIXED + 1
THIRDS = 4 * FIELDS
ROWS_OUT = THIRDS + 2 * FIELDS - 1


def merge_lanes(lon):
    core = lon // 2
    return (core + 3 * REACH) % LANES, (core - 3 * REACH) % LANES


def pack_kernel(
    lon, merges, b_hbm, e_hbm, o_hbm, w_hbm, speed_hbm, couple_hbm, out_ref,
    b_ref, e_ref, o_ref, w_ref, speed_ref, couple_ref, stage_ref, sems,
):
    _, levels, share, _ = b_ref.shape
    full = lon // LANES
    rest = lon - full * LANES
    member = lax.axis_index("ens")
    turn = lax.axis_index("tm") * 2 + member
    comp = jnp.where(turn < 2 * TILES, turn // TILES, turn - 2 * TILES)

    def in_halves(hbm, ref, first):
        n = FIELDS // 2
        return [
            pltpu.make_async_copy(hbm.at[pl.ds(i * n, n)], ref.at[pl.ds(i * n, n)], sems.at[first + i]) for i in range(2)
        ]

    def start(copies):
        for copy in copies:
            copy.start()

    copies_b, copies_e, copies_o = in_halves(b_hbm, b_ref, 0), in_halves(e_hbm, e_ref, 2), in_halves(o_hbm, o_ref, 7)
    others = (
        pltpu.make_async_copy(w_hbm.at[comp], w_ref, sems.at[4]),
        pltpu.make_async_copy(speed_hbm, speed_ref, sems.at[5]),
        pltpu.make_async_copy(couple_hbm, couple_ref, sems.at[6]),
    )
    start(copies_b)
    pl.when(member == 0)(lambda: start(copies_e))
    pl.when(member != 0)(lambda: start(copies_o))
    start(others)
    lane = lax.broadcasted_iota(jnp.int32, (ROWS, LANES), 1)
    row = lax.broadcasted_iota(jnp.int32, (ROWS, LANES), 0)
    group = ROWS // share

    def raw(copies, ref, first):
        for f in range(FIELDS):
            if f % 2 == 0:
                copies[f // 2].wait()
            for level in range(levels):
                for c in range(full + 1):
                    half, tile = c // TILES, c % TILES
                    width = LANES if c < full else rest
                    value = ref[f, level, :, pl.ds(c * LANES, width)].astype(jnp.float32)
                    start = (half * levels + level) * share * ROWS_IN + first + f * TILES + tile
                    out_ref[pl.ds(start, share, stride=ROWS_IN), pl.ds(0, width)] = value

    def place(half, g, k):
        return pl.ds((half * levels + g * group) * share * ROWS_IN + k, ROWS, stride=ROWS_IN), slice(None)

    def windows(first, third, last):
        before = pltpu.roll(last, LANES - rest, 1)
        after = jnp.where(lane < rest, last, pltpu.roll(first, rest, 1))
        ends = ((third, before), (after, third))
        merged = [jnp.where(lane < m, x, y) for m, (x, y) in zip(merges, ends)]
        extra = [jnp.where(lane < m, y, x) for m, (x, y) in zip(merges, ends)]
        return merged, extra

    def merge(g, k):
        merged, extra = windows(
            out_ref[place(0, g, k)], out_ref[place(0, g, k + TILES - 1)], out_ref[place(1, g, k + TILES - 1)]
        )
        for half in range(2):
            out_ref[place(half, g, k + TILES - 1)] = merged[half]
        return extra

    def by_level(ref, g):
        value = jnp.full((ROWS, LANES), ref[g * group], jnp.float32)
        for i in range(1, group):
            value = jnp.where(row < i * share, value, ref[g * group + i])
        return value

    raw(copies_b, b_ref, 0)
    pl.when(member == 0)(lambda: raw(copies_e, e_ref, FIELDS * TILES))
    pl.when(member != 0)(lambda: raw(copies_o, o_ref, FIELDS * TILES))
    for copy in others:
        copy.wait()
    for level in range(levels):
        for c in range(full + 1):
            width = LANES if c < full else rest
            stage_ref[c, pl.ds(level * share, share), pl.ds(0, width)] = w_ref[level, :, pl.ds(c * LANES, width)]
    for g in range(levels // group):
        mixed = [None, None]
        for f in range(FIELDS):
            extra = merge(g, f * TILES)
            for half, m in enumerate(merges):
                at = WINDS + f * SLOT
                moved = pltpu.roll(extra[half], (at - (m - REACH)) % LANES, 1)
                mixed[half] = moved if f == 0 else jnp.where(lane < at, mixed[half], moved)
        tiles = [stage_ref[c, pl.ds(g * ROWS, ROWS), :] for c in range(full + 1)]
        merged, extra = windows(tiles[0], tiles[2], tiles[5])
        speed, couple = by_level(speed_ref, g), by_level(couple_ref, g)
        for half, m in enumerate(merges):
            parts = tiles[TILES * half : TILES * half + 2] + [merged[half]]
            wind, left = parts[TILES - 1], pltpu.roll(parts[TILES - 1], LANES - SLOT * FIELDS, 1)
            for c in reversed(range(TILES - 1)):
                wind = jnp.where(jnp.logical_or(turn == c, turn == TILES + c), parts[c], wind)
                by = (c + 1) * SLOT * FIELDS
                left = jnp.where(lane < by, pltpu.roll(parts[c], by, 1), left)
            wind = jnp.where(turn < 2 * TILES, wind, left)
            value = jnp.where(lane < WINDS, wind, mixed[half])
            value = jnp.where(lane == WINDS + SLOT, speed, value)
            value = jnp.where(lane == WINDS + 2 * SLOT - 1, couple, value)
            ends = pltpu.roll(extra[half], LANES - 1 - m, 1)
            value = jnp.where(lane >= LANES - 2, ends, value)
            out_ref[place(half, g, MIXED)] = value

    for g in range(levels // group):
        for f in range(FIELDS):
            merge(g, (FIELDS + f) * TILES)


def layer_kernel(lon, merges, subwins, in_ref, out_ref):
    half = lax.axis_index("ens")
    lane = lax.broadcasted_iota(jnp.int32, (ROWS, LANES), 1)
    row = lax.broadcasted_iota(jnp.int32, (ROWS, LANES), 0)
    below = lane < jnp.where(half == 0, merges[0], merges[1])
    free_lo = jnp.where(half == 0, merges[0] - 3 * REACH, merges[1] - 3 * REACH)
    free = jnp.logical_and(lane >= free_lo, lane < free_lo + FREE)

    def load(member, t, k):
        return in_ref[pl.ds((member * subwins + t) * ROWS * ROWS_IN + k, ROWS, stride=ROWS_IN), :]

    def of_half(values):
        return jnp.where(half == 0, values[0] % LANES, values[1] % LANES)

    mixed = [[load(member, t, MIXED) for t in range(subwins)] for member in range(2)]
    speed_at, couple_at = WINDS + SLOT, WINDS + 2 * SLOT - 1
    speed = 0.5 * jnp.broadcast_to(mixed[0][0][:, speed_at : speed_at + 1], (ROWS, LANES))
    couple = jnp.broadcast_to(mixed[0][0][:, couple_at : couple_at + 1], (ROWS, LANES))

    def back(x, by):
        moved = [pltpu.roll(v, by, 1) for v in x]
        return [jnp.where(lane < by, moved[i - 1], v) for i, v in enumerate(moved)]

    def ahead(x, by):
        moved = [pltpu.roll(v, LANES - by, 1) for v in x]
        return [jnp.where(lane >= LANES - by, moved[(i + 1) % len(x)], v) for i, v in enumerate(moved)]

    def up(x, by):
        return [pltpu.roll(v, ROWS - by, 0) for v in x]

    def down(x, by):
        return [pltpu.roll(v, by, 0) for v in x]

    def staggered(f, x):
        if f == 1:
            return ahead(x, 1)
        if f == 2:
            return up(x, 1)
        return x

    def aligned(f, x):
        if f == 1:
            return back(x, 1)
        if f == 2:
            return down(x, 1)
        return x

    def widened(x, extra):
        return x[:2] + [jnp.where(below, x[2], extra), jnp.where(below, extra, x[2])]

    def narrowed(x):
        return x[:2] + [jnp.where(below, x[2], x[3])]

    def fields_of(member, t, at):
        return [[load(member, t, (at + f) * TILES + c) for c in range(TILES)] for f in range(FIELDS)]

    def extras_of(member, t):
        shifts = [of_half([m - REACH - WINDS - f * SLOT for m in merges]) for f in range(FIELDS)]
        return [pltpu.roll(mixed[member][t], by, 1) for by in shifts]

    def stag(state):
        return [staggered(f, x) for f, x in enumerate(state)]

    def wind(comp):
        sent = [mixed[turn % 2][turn // 2] for turn in range(2 * subwins)]
        left = sent[2 * TILES + comp]
        tiles = []
        for c in range(TILES):
            by = WINDS - c * SLOT * FIELDS
            tiles.append(jnp.where(lane < WINDS, sent[comp * TILES + c], pltpu.roll(left, by, 1)))
        return tiles, pltpu.roll(sent[comp * TILES], of_half([m + 1 - LANES for m in merges]), 1)

    stay = 1.0 - 4.0 * diffusion
    grad_p = jnp.where(row == ROWS - 2, 0.0, speed)
    grad_m = jnp.where(row == ROWS - 1, 0.0, speed)
    before_p = jnp.where(row == 0, 0.0, speed)
    before_m = jnp.where(row == 1, 0.0, speed)
    div_p = jnp.where(row == ROWS - 1, 0.0, speed)
    div_m = jnp.where(row == 0, 0.0, speed)

    def coefficients(east, north):
        return (
            [diffusion - 0.5 * v for v in east],
            [diffusion + 0.5 * v for v in east],
            [jnp.where(row == ROWS - 1, 0.0, diffusion - 0.5 * v) for v in north],
            [jnp.where(row == 0, 0.0, diffusion + 0.5 * v) for v in north],
        )

    (east, east_extra), (north, north_extra) = wind(0), wind(1)
    narrow = coefficients(east, north)
    wide = coefficients(widened(east, east_extra), widened(north, north_extra))

    here = 2.0 * speed * speed + (div_p * grad_m + div_m * before_p)
    along, north_of, south_of = speed * speed, div_p * grad_p, div_m * before_m

    def divergence(u, v):
        return [
            speed * (a - b) + (div_p * c - div_m * d) for a, b, c, d in zip(u, back(u, 2), v, down(v, 2))
        ]

    def spread(h):
        ahead_h, up_h = ahead(h, 2), up(h, 2)
        change = [
            (along * (n + m) + (north_of * p + south_of * q)) - here * a
            for a, n, m, p, q in zip(h, ahead_h, back(h, 2), up_h, down(h, 2))
        ]
        return change, ahead_h, up_h

    def gradients(hs, aheads, ups):
        here_h, ahead_h, up_h = ([sum(x[1:], x[0]) for x in zip(*y)] for y in (hs, aheads, ups))
        east = [speed * (n - m) for n, m in zip(ahead_h, here_h)]
        north = [grad_p * n - grad_m * m for n, m in zip(up_h, here_h)]
        return east, north

    def tangent(state, coefs):
        h, u, v, q = state
        flow = divergence(u, v)
        passed = []
        for _ in range(STEPS):
            change, ahead_h, up_h = spread(h)
            passed.append((h, ahead_h, up_h))
            flow = [a - b for a, b in zip(flow, change)]
            h = [a - b for a, b in zip(h, flow)]
            q = [
                stay * a + (em * e + ep * w) + (nm * n + np * s) + couple * p
                for a, em, e, ep, w, nm, n, np, s, p in zip(
                    q, coefs[0], ahead(q, 1), coefs[1], back(q, 1), coefs[2], up(q, 1), coefs[3], down(q, 1), h
                )
            ]
        east, north = gradients(*zip(*passed))
        return [h, [a - b for a, b in zip(u, east)], [a - b for a, b in zip(v, north)], q]

    def adjoint(state, coefs):
        h, u, v, q = state
        flow = divergence(u, v)
        passed = []
        for _ in range(STEPS):
            h = [a + couple * b for a, b in zip(h, q)]
            change, ahead_h, up_h = spread(h)
            passed.append((h, ahead_h, up_h))
            flow = [a + b for a, b in zip(flow, change)]
            h = [a + b for a, b in zip(h, flow)]
            e = ahead([a * b for a, b in zip(coefs[1], q)], 1)
            w = back([a * b for a, b in zip(coefs[0], q)], 1)
            n = up([a * b for a, b in zip(coefs[3], q)], 1)
            s = down([a * b for a, b in zip(coefs[2], q)], 1)
            q = [stay * a + (b + c) + (d + f) for a, b, c, d, f in zip(q, e, w, n, s)]
        east, north = gradients(*zip(*passed))
        return [h, [a + b for a, b in zip(u, east)], [a + b for a, b in zip(v, north)], q]

    def each(fn, *states):
        return [[fn(*vals) for vals in zip(*xs)] for xs in zip(*states)]

    def operate(p, p_wide, precision, observed):
        weighted = []
        for t in range(subwins):
            change = p[t]
            if t > 0:
                moved = tangent(p[t - 1], narrow) if p_wide is None else tangent(p_wide[t - 1], wide)
                if p_wide is not None:
                    moved = [narrowed(x) for x in moved]
                change = each(lambda a, b: a - b, change, moved)
            weighted.append(each(lambda a, b: a * b, precision[t], change))
        image = []
        for t in range(subwins):
            out = each(lambda w, o, d: w + o * d, weighted[t], observed[t], p[t])
            if t + 1 < subwins:
                moved = adjoint(weighted[t + 1], narrow)
                out = each(lambda a, b: a - b, out, moved)
            image.append(out)
        return image

    def flat(x):
        return [(c, v) for state in x for field in state for c, v in enumerate(field)]

    def total(terms):
        inner, edge = None, None
        for c, v in terms:
            if c < TILES - 1:
                inner = v if inner is None else inner + v
            else:
                edge = v if edge is None else edge + v
        both = inner + jnp.where(free, 0.0, edge)
        return jnp.sum(both, axis=(0, 1), keepdims=True)

    def dot(x, y):
        return total([(c, v * w) for (c, v), (_, w) in zip(x, y)])

    precision = [stag(fields_of(0, t, FIELDS)) for t in range(subwins)]
    observed = [stag(fields_of(1, t, FIELDS)) for t in range(subwins)]
    for member in range(2):
        plain = [fields_of(member, t, 0) for t in range(subwins)]
        b_wide = [
            stag([widened(x, e) for x, e in zip(plain[t], extras_of(member, t))]) for t in range(subwins - 1)
        ]
        b = [[narrowed(x) for x in state] for state in b_wide] + [stag(plain[-1])]
        one = operate(b, b_wide, precision, observed)
        two = operate(one, None, precision, observed)
        one, two = [[[aligned(f, x) for f, x in enumerate(state)] for state in y] for y in (one, two)]
        f0, f1, f2 = flat(plain), flat(one), flat(two)
        s00, s01, s11, s02, s12 = dot(f0, f0), dot(f0, f1), dot(f1, f1), dot(f0, f2), dot(f1, f2)
        step = jnp.where(s11 > 0.0, s01 / jnp.where(s11 > 0.0, s11, 1.0), 0.0)
        more = 2.0 - jnp.where(s00 > 0.0, step * s01 / jnp.where(s00 > 0.0, s00, 1.0), 0.0)
        step_t = jnp.broadcast_to(step, (ROWS, LANES))
        more_t = jnp.broadcast_to(more, (ROWS, LANES))
        res = [(c, v - step_t * w) for (c, v), (_, w) in zip(f0, f1)]
        mov = [(c, more_t * v - step_t * w) for (c, v), (_, w) in zip(f0, f1)]
        img = [(c, more_t * v - step_t * w) for (c, v), (_, w) in zip(f1, f2)]
        sums = [step, more, s00, s01, s11, s02, s12, dot(res, res), dot(mov, img)]
        sums += [sums[-1]] * (-len(sums) % 6)
        for t in range(subwins):

            def put(k, value):
                start = (member * subwins + t) * ROWS * ROWS_OUT + k
                out_ref[pl.ds(start, ROWS, stride=ROWS_OUT), :] = value

            images = one[t] + two[t]
            last = images[-1][TILES - 1]
            for k, x in enumerate(images):
                put(2 * k, x[0])
                put(2 * k + 1, x[1])
                if k < 5:
                    put(THIRDS + k, jnp.where(free, pltpu.roll(last, (-(k + 1) * FREE) % LANES, 1), x[2]))
                elif k < 2 * FIELDS - 1:
                    rows = []
                    for i in (k - 5, k - 3):
                        value = sums[3 * i + 2]
                        for j in (1, 0):
                            value = jnp.where(lane < free_lo + (j + 1) * SLOT, sums[3 * i + j], value)
                        rows.append(value)
                    put(THIRDS + k, jnp.where(free, jnp.where(row % 2 == 0, rows[0], rows[1]), x[2]))


def finish_kernel(lon, merges, b_ref, in_ref, x_hbm, r_hbm, x_ref, r_ref, last_ref, sems):
    _, levels, share, _ = b_ref.shape
    full = lon // LANES
    rest = lon - full * LANES
    size = share * ROWS_OUT
    apart = merges[0] - merges[1]
    at_lane = merges[0] - 3 * REACH

    group = ROWS // share

    slots = []
    for i in range(3):
        at = THIRDS + 5 + i % 2 + (i // 2) * ROWS_OUT
        halves = [in_ref[pl.ds(half * levels * size + at, levels, stride=size), :] for half in range(2)]
        slots.append(jnp.concatenate([halves[0], pltpu.roll(halves[1], apart, 1)], axis=0))

    def sums(i):
        value = slots[i // 3]
        return pltpu.roll(value, LANES - (i % 3) * SLOT, 1) if i % 3 else value

    step, more, s00, s01, s11, s02, s12, rr, mi = [sums(i) for i in range(9)]

    def total(x):
        return jnp.sum(x, axis=0, keepdims=True)

    norm_0 = total(s00)
    alpha_0 = norm_0 / total(s01)
    d = step - alpha_0
    norm_1 = total(rr + d * (2.0 * (s01 - step * s11) + d * s11))
    beta = norm_1 / norm_0
    g = (1.0 + beta) - more
    cross_d = more * (s02 + s11) - 2.0 * step * s12
    cross_g = 2.0 * more * s01 - step * (s11 + s02)
    curve = total(mi + d * (cross_d + d * s12 + g * (s11 + s02)) + g * (cross_g + g * s01))
    alpha_1 = norm_1 / curve
    first = alpha_0 + alpha_1 * (1.0 + beta)
    second = alpha_0 * alpha_1
    first = jnp.broadcast_to(first[:, at_lane : at_lane + 1], (share, LANES))
    second = jnp.broadcast_to(second[:, at_lane : at_lane + 1], (share, LANES))
    lane = lax.broadcasted_iota(jnp.int32, (share, LANES), 1)

    def gather_last():
        lane_8 = lax.broadcasted_iota(jnp.int32, (ROWS, LANES), 1)
        for half in range(2):
            for g in range(levels // group):
                value = None
                for k in range(5):
                    start = (half * levels + g * group) * size + THIRDS + k
                    part = pltpu.roll(in_ref[pl.ds(start, ROWS, stride=ROWS_OUT), :], (k + 1) * FREE % LANES, 1)
                    begin = (merges[half] - 3 * REACH + (k + 1) * FREE) % LANES
                    here = jnp.logical_and(lane_8 >= begin, lane_8 < begin + FREE)
                    value = part if value is None else jnp.where(here, part, value)
                last_ref[half, pl.ds(g * ROWS, ROWS), :] = value

    def image(level, k):
        got = []
        for half in range(2):
            start = (half * levels + level) * size
            tiles = [in_ref[pl.ds(start + 2 * k + c, share, stride=ROWS_OUT), :] for c in range(2)]
            if k < 2 * FIELDS - 1:
                tiles.append(in_ref[pl.ds(start + THIRDS + k, share, stride=ROWS_OUT), :])
            else:
                tiles.append(last_ref[half, pl.ds(level * share, share), :])
            got.append(tiles)
        middle = jnp.where(lane < at_lane, got[0][2], got[1][2])
        return got[0][:2] + [middle] + got[1]

    copies = []
    for f in range(FIELDS):
        if f == FIELDS - 1:
            gather_last()
        for level in range(levels):
            b = b_ref[f, level]
            ones, twos = image(level, f), image(level, FIELDS + f)
            for c, (one, two) in enumerate(zip(ones, twos)):
                width = LANES if c < full else rest
                cols = pl.ds(c * LANES, width)
                one, two = one[:, :width], two[:, :width]
                part = b[:, c * LANES : c * LANES + width]
                x_ref[f, level, :, cols] = first[:, :width] * part - second[:, :width] * one
                r_ref[f, level, :, cols] = (part - first[:, :width] * one) + second[:, :width] * two
        for i, (src, dst) in enumerate(((x_ref, x_hbm), (r_ref, r_hbm))):
            copies.append(pltpu.make_async_copy(src.at[f], dst.at[f], sems.at[i, f]))
            copies[-1].start()
    for copy in copies:
        copy.wait()


def by_layer(right_side, error_precision, obs_count, background_wind, wave_speed, tracer_coupling):
    _, fields, levels, share, lon = right_side.shape
    subwins = lax.axis_size("tm")
    merges = merge_lanes(lon)
    vmem = pl.BlockSpec(memory_space=pltpu.VMEM)
    hbm = pl.BlockSpec(memory_space=pltpu.HBM)
    params = pltpu.CompilerParams(vmem_limit_bytes=48 * 1024 * 1024)
    state = (fields, levels, share, lon)

    def exchange(x):
        x = x.reshape(2 * levels, -1, 1, LANES)
        return lax.all_to_all(x, ("ens", "tm", "space"), 0, 0, tiled=True).reshape(-1, LANES)

    b = right_side.reshape(state)
    given = (b, error_precision.reshape(state), obs_count.reshape(state), background_wind, wave_speed, tracer_coupling)
    with jax.named_scope("pack"):
        packed = pl.pallas_call(
            lambda *refs: pack_kernel(lon, merges, *refs),
            out_shape=jax.ShapeDtypeStruct((2 * levels * share * ROWS_IN, LANES), jnp.float32),
            in_specs=[hbm] * len(given),
            out_specs=vmem,
            scratch_shapes=[
                pltpu.VMEM(state, jnp.float32),
                pltpu.VMEM(state, jnp.float32),
                pltpu.VMEM(state, jnp.int32),
                pltpu.VMEM(background_wind.shape[1:], jnp.float32),
                pltpu.SMEM(wave_speed.shape, jnp.float32),
                pltpu.SMEM(tracer_coupling.shape, jnp.float32),
                pltpu.VMEM((lon // LANES + 1, levels * share, LANES), jnp.float32),
                pltpu.SemaphoreType.DMA((9,)),
            ],
            compiler_params=params,
        )(*[pltpu.with_memory_space_constraint(x, pltpu.HBM) for x in given])
    packed = exchange(packed)
    with jax.named_scope("layer"):
        images = pl.pallas_call(
            lambda *refs: layer_kernel(lon, merges, subwins, *refs),
            out_shape=jax.ShapeDtypeStruct((2 * levels * share * ROWS_OUT, LANES), jnp.float32),
            in_specs=[vmem],
            out_specs=vmem,
            compiler_params=params,
        )(packed)
    images = exchange(images)
    with jax.named_scope("finish"):
        x, r = pl.pallas_call(
            lambda *refs: finish_kernel(lon, merges, *refs),
            out_shape=[jax.ShapeDtypeStruct(state, jnp.float32)] * 2,
            in_specs=[vmem] * 2,
            out_specs=[hbm] * 2,
            scratch_shapes=[
                pltpu.VMEM(state, jnp.float32),
                pltpu.VMEM(state, jnp.float32),
                pltpu.VMEM((2, levels * share, LANES), jnp.float32),
                pltpu.SemaphoreType.DMA((2, FIELDS)),
            ],
            compiler_params=params,
        )(b, images)
    return x.reshape(right_side.shape), r.reshape(right_side.shape)


def fits_by_layer(mesh, shape):
    space, tm, ens = mesh.shape["space"], mesh.shape["tm"], mesh.shape["ens"]
    subwins, fields, levels, lats, lon = shape
    return (
        (ens, tm, space, fields, lats) == (2, 4, 4, FIELDS, ROWS)
        and subwins == ens * tm
        and levels == space * tm
        and lon == 720
    )


def extended_2(cells, sides, width):
    for axis, dim in sides:
        count = lax.axis_size(axis)
        ends = count - 1
        head = lax.slice_in_dim(cells, 0, width, axis=dim)
        tail = lax.slice_in_dim(cells, cells.shape[dim] - width, cells.shape[dim], axis=dim)
        cells = jnp.concatenate(
            [
                lax.ppermute(tail, axis, [(i, (i + 1) % count) for i in range(ends)]),
                cells,
                lax.ppermute(head, axis, [((i + 1) % count, i) for i in range(ends)]),
            ],
            axis=dim,
        )
    return cells


def shifted(value, axis, by):
    peers = lax.axis_size(axis)
    pairs = [(i, i + by) for i in range(peers) if 0 <= i + by < peers]
    return lax.ppermute(value, axis, pairs)


def along_x(field):
    return 0.5 * (jnp.roll(field, -1, axis=-1) - jnp.roll(field, 1, axis=-1))


def second_x(field):
    return jnp.roll(field, -1, axis=-1) + jnp.roll(field, 1, axis=-1) - 2.0 * field


def along_y(extended):
    return 0.5 * (extended[..., 2:, :] - extended[..., :-2, :])


def trimmed(field, count):
    if count == 0:
        return field
    return field[..., count : field.shape[-2] - count, :]


def row_valid(lat_rows):
    first_row = lax.axis_index("space") * lat_rows - 4
    row_total = lat_rows * lax.axis_size("space")
    global_rows = first_row + jnp.arange(lat_rows + 8, dtype=jnp.int32)
    inside = jnp.logical_and(global_rows >= 0, global_rows < row_total)
    return inside.astype(jnp.float32)[:, None]


def tangent_core(state, margin, coefs):
    speed_col, couple_col, winds, have, valid = coefs
    height, east, north, tracer = (state[:, 0], state[:, 1], state[:, 2], state[:, 3])
    east_mid = east - speed_col * along_x(height)
    north_mid = (trimmed(north, 1) - speed_col * along_y(height)) * trimmed(valid, 5 - margin)
    height_new = trimmed(height, 2) - speed_col * (
        along_x(trimmed(east_mid, 2)) + along_y(north_mid)
    )
    tracer_one = trimmed(tracer, 1)
    inner = trimmed(tracer, 2)
    tracer_lap = second_x(inner) + tracer_one[..., 2:, :] + tracer_one[..., :-2, :] - 2.0 * inner
    wind_east = trimmed(winds[0], have - margin + 2)
    wind_north = trimmed(winds[1], have - margin + 2)
    tracer_new = (
        inner
        - wind_east * along_x(inner)
        - wind_north * along_y(tracer_one)
        + diffusion * tracer_lap
        + couple_col * height_new
    )
    result = jnp.stack(
        [height_new, trimmed(east_mid, 2), trimmed(north_mid, 1), tracer_new], axis=1
    )
    return result * trimmed(valid, 6 - margin)


def adjoint_core(state, margin, coefs):
    speed_col, couple_col, winds, have, valid = coefs
    height, east, north, tracer = (state[:, 0], state[:, 1], state[:, 2], state[:, 3])
    height_mix = height + couple_col * tracer
    east_mid = east + speed_col * along_x(height_mix)
    north_mid = (trimmed(north, 1) + speed_col * along_y(height_mix)) * trimmed(valid, 5 - margin)
    height_new = trimmed(height_mix, 2) + speed_col * (
        along_x(trimmed(east_mid, 2)) + along_y(north_mid)
    )
    tracer_one = trimmed(tracer, 1)
    inner = trimmed(tracer, 2)
    tracer_lap = second_x(inner) + tracer_one[..., 2:, :] + tracer_one[..., :-2, :] - 2.0 * inner
    wind_east = trimmed(winds[0], have - margin + 2)
    wind_north = trimmed(winds[1], have - margin + 1)
    tracer_new = (
        inner
        + along_x(wind_east * inner)
        + along_y(wind_north * tracer_one)
        + diffusion * tracer_lap
    )
    result = jnp.stack(
        [height_new, trimmed(east_mid, 2), trimmed(north_mid, 1), tracer_new], axis=1
    )
    return result * trimmed(valid, 6 - margin)


def rebuild(state, sent):
    widths = [(0, 0)] * (state.ndim - 3) + [(2, 2), (0, 0)]
    east_wide = jnp.pad(state[:, 1], widths)
    return jnp.stack([sent[:, 0], east_wide, sent[:, 1], sent[:, 2]], axis=1)


def tangent_near(state):
    picked = jnp.stack([state[:, 0], state[:, 2], state[:, 3]], axis=1)
    sent = extended_2(picked, (("space", 3),), 2)
    return rebuild(state, sent)


def adjoint_near(state):
    picked = jnp.stack([state[:, 0], state[:, 2], state[:, 3]], axis=1)
    sent = extended_2(picked, (("space", 3),), 2)
    return rebuild(state, sent)


def propagate(fields, step_core, near_fn, coefs):
    current = fields
    for step in range(STEPS):
        current = step_core(near_fn(current), 2, coefs)
    return current


def operate(direction, error_precision, observed, coefs):
    moved = propagate(direction, tangent_core, tangent_near, coefs)
    incoming = shifted(moved, "tm", 1)
    previous = jnp.concatenate([incoming, moved[:-1]], axis=0)
    weighted = error_precision * (direction - previous)
    back = propagate(weighted, adjoint_core, adjoint_near, coefs)
    arriving = shifted(back, "tm", -1)
    following = jnp.concatenate([back[1:], arriving], axis=0)
    return weighted - following + observed * direction


def squares(residual):
    return lax.psum(jnp.sum(residual * residual), ("space", "tm"))


def on_device(right_side, error_precision, obs_count, background_wind, wave_speed, tracer_coupling):
    lat_rows = right_side.shape[3]
    valid = row_valid(lat_rows)
    winds = extended_2(background_wind, (("space", 2),), 1)
    have = 1
    coefs = (wave_speed[:, None, None], tracer_coupling[:, None, None], winds, have, valid)
    observed = obs_count.astype(jnp.float32)
    solution_field = jnp.zeros_like(right_side)
    residual = right_side
    direction = right_side
    norm_now = squares(residual)
    for step in range(ITERS):
        image = operate(direction, error_precision, observed, coefs)
        alpha = norm_now / lax.psum(jnp.sum(direction * image), ("space", "tm"))
        solution_field = solution_field + alpha * direction
        residual = residual - alpha * image
        norm_next = squares(residual)
        direction = residual + norm_next / norm_now * direction
        norm_now = norm_next
    return (solution_field, residual)


def solution(mesh):
    def run(right_side, *others):
        body = by_layer if fits_by_layer(mesh, right_side.shape) else on_device
        return jax.shard_map(
            body,
            mesh=mesh,
            in_specs=(
                P(("ens", "tm"), None, None, "space", None),
                P("tm", None, None, "space", None),
                P("tm", None, None, "space", None),
                P(None, None, "space", None),
                P(),
                P(),
            ),
            out_specs=(
                P(("ens", "tm"), None, None, "space", None),
                P(("ens", "tm"), None, None, "space", None),
            ),
            check_vma=False,
        )(right_side, *others)

    return run
```

```python
import jax
import jax.numpy as jnp
from jax import lax
from jax.experimental import pallas as pl
from jax.experimental.pallas import tpu as pltpu
from jax.sharding import PartitionSpec as P

STEPS = 2
ITERS = 2


diffusion = 0.1


LANES = 128
ROWS = 8
TILES = 3
REACH = 4
FIELDS = 4
SLOT = 2 * REACH
WINDS = LANES - FIELDS * SLOT
FREE = 6 * REACH
MIXED = 2 * FIELDS * TILES
ROWS_IN = MIXED + 1
THIRDS = 4 * FIELDS
ROWS_OUT = THIRDS + 2 * FIELDS - 1


def merge_lanes(lon):
    core = lon // 2
    return (core + 3 * REACH) % LANES, (core - 3 * REACH) % LANES


def pack_kernel(
    lon, merges, b_hbm, e_hbm, o_hbm, w_hbm, speed_hbm, couple_hbm, out_ref,
    b_ref, e_ref, o_ref, w_ref, speed_ref, couple_ref, b_row_ref, s_row_ref, w_row_ref, sems,
):
    _, levels, share, _ = b_ref.shape
    full = lon // LANES
    rest = lon - full * LANES
    member = lax.axis_index("ens")
    turn = lax.axis_index("tm") * 2 + member
    comp = jnp.where(turn < 2 * TILES, turn // TILES, turn - 2 * TILES)

    def in_halves(hbm, ref, first):
        n = FIELDS
        return [
            pltpu.make_async_copy(hbm.at[pl.ds(i * n, n)], ref.at[pl.ds(i * n, n)], sems.at[first + i]) for i in range(1)
        ]

    def start(copies):
        for copy in copies:
            copy.start()

    copies_b, copies_e, copies_o = in_halves(b_hbm, b_ref, 0), in_halves(e_hbm, e_ref, 2), in_halves(o_hbm, o_ref, 7)
    others = (
        pltpu.make_async_copy(w_hbm.at[comp], w_ref, sems.at[4]),
        pltpu.make_async_copy(speed_hbm, speed_ref, sems.at[5]),
        pltpu.make_async_copy(couple_hbm, couple_ref, sems.at[6]),
    )
    start(copies_b)
    pl.when(member == 0)(lambda: start(copies_e))
    pl.when(member != 0)(lambda: start(copies_o))
    start(others)
    lane = lax.broadcasted_iota(jnp.int32, (ROWS, LANES), 1)
    row = lax.broadcasted_iota(jnp.int32, (ROWS, LANES), 0)
    group = ROWS // share

    def stage(copies, ref, row_ref):
        n = FIELDS // len(copies)
        for i, copy in enumerate(copies):
            copy.wait()
            for f in range(i * n, (i + 1) * n):
                for level in range(levels):
                    at = f, pl.ds(level * share, share), pl.ds(0, lon)
                    row_ref[at] = ref[f, level].astype(jnp.float32)

    def place(half, g, k):
        return pl.ds((half * levels + g * group) * share * ROWS_IN + k, ROWS, stride=ROWS_IN), slice(None)

    def windows(first, third, last):
        before = pltpu.roll(last, LANES - rest, 1)
        after = jnp.where(lane < rest, last, pltpu.roll(first, rest, 1))
        ends = ((third, before), (after, third))
        merged = [jnp.where(lane < m, x, y) for m, (x, y) in zip(merges, ends)]
        extra = [jnp.where(lane < m, y, x) for m, (x, y) in zip(merges, ends)]
        return merged, extra

    def put(g, k, row_ref, f):
        tiles = [row_ref[f, pl.ds(g * ROWS, ROWS), pl.ds(c * LANES, LANES)] for c in range(full + 1)]
        merged, extra = windows(tiles[0], tiles[2], tiles[5])
        for half in range(2):
            for c, value in enumerate(tiles[TILES * half : TILES * half + 2] + [merged[half]]):
                out_ref[place(half, g, k + c)] = value
        return extra

    def by_level(ref, g):
        value = jnp.full((ROWS, LANES), ref[g * group], jnp.float32)
        for i in range(1, group):
            value = jnp.where(row < i * share, value, ref[g * group + i])
        return value

    stage(copies_b, b_ref, b_row_ref)
    pl.when(member == 0)(lambda: stage(copies_e, e_ref, s_row_ref))
    pl.when(member != 0)(lambda: stage(copies_o, o_ref, s_row_ref))
    for copy in others:
        copy.wait()
    for level in range(levels):
        w_row_ref[pl.ds(level * share, share), pl.ds(0, lon)] = w_ref[level]
    for g in range(levels // group):
        mixed = [None, None]
        for f in range(FIELDS):
            extra = put(g, f * TILES, b_row_ref, f)
            for half, m in enumerate(merges):
                at = WINDS + f * SLOT
                moved = pltpu.roll(extra[half], (at - (m - REACH)) % LANES, 1)
                mixed[half] = moved if f == 0 else jnp.where(lane < at, mixed[half], moved)
        tiles = [w_row_ref[pl.ds(g * ROWS, ROWS), pl.ds(c * LANES, LANES)] for c in range(full + 1)]
        merged, extra = windows(tiles[0], tiles[2], tiles[5])
        speed, couple = by_level(speed_ref, g), by_level(couple_ref, g)
        for half, m in enumerate(merges):
            parts = tiles[TILES * half : TILES * half + 2] + [merged[half]]
            wind, left = parts[TILES - 1], pltpu.roll(parts[TILES - 1], LANES - SLOT * FIELDS, 1)
            for c in reversed(range(TILES - 1)):
                wind = jnp.where(jnp.logical_or(turn == c, turn == TILES + c), parts[c], wind)
                by = (c + 1) * SLOT * FIELDS
                left = jnp.where(lane < by, pltpu.roll(parts[c], by, 1), left)
            wind = jnp.where(turn < 2 * TILES, wind, left)
            value = jnp.where(lane < WINDS, wind, mixed[half])
            value = jnp.where(lane == WINDS + SLOT, speed, value)
            value = jnp.where(lane == WINDS + 2 * SLOT - 1, couple, value)
            ends = pltpu.roll(extra[half], LANES - 1 - m, 1)
            value = jnp.where(lane >= LANES - 2, ends, value)
            out_ref[place(half, g, MIXED)] = value

    for g in range(levels // group):
        for f in range(FIELDS):
            put(g, (FIELDS + f) * TILES, s_row_ref, f)


def layer_kernel(lon, merges, subwins, in_ref, out_ref):
    half = lax.axis_index("ens")
    lane = lax.broadcasted_iota(jnp.int32, (ROWS, LANES), 1)
    row = lax.broadcasted_iota(jnp.int32, (ROWS, LANES), 0)
    below = lane < jnp.where(half == 0, merges[0], merges[1])
    free_lo = jnp.where(half == 0, merges[0] - 3 * REACH, merges[1] - 3 * REACH)
    free = jnp.logical_and(lane >= free_lo, lane < free_lo + FREE)

    def load(member, t, k):
        return in_ref[pl.ds((member * subwins + t) * ROWS * ROWS_IN + k, ROWS, stride=ROWS_IN), :]

    def of_half(values):
        return jnp.where(half == 0, values[0] % LANES, values[1] % LANES)

    mixed = [[load(member, t, MIXED) for t in range(subwins)] for member in range(2)]
    speed_at, couple_at = WINDS + SLOT, WINDS + 2 * SLOT - 1
    speed = 0.5 * jnp.broadcast_to(mixed[0][0][:, speed_at : speed_at + 1], (ROWS, LANES))
    couple = jnp.broadcast_to(mixed[0][0][:, couple_at : couple_at + 1], (ROWS, LANES))

    def back(x, by):
        moved = [pltpu.roll(v, by, 1) for v in x]
        return [jnp.where(lane < by, moved[i - 1], v) for i, v in enumerate(moved)]

    def ahead(x, by):
        moved = [pltpu.roll(v, LANES - by, 1) for v in x]
        return [jnp.where(lane >= LANES - by, moved[(i + 1) % len(x)], v) for i, v in enumerate(moved)]

    def up(x, by):
        return [pltpu.roll(v, ROWS - by, 0) for v in x]

    def down(x, by):
        return [pltpu.roll(v, by, 0) for v in x]

    def staggered(f, x):
        if f == 1:
            return ahead(x, 1)
        if f == 2:
            return up(x, 1)
        return x

    def aligned(f, x):
        if f == 1:
            return back(x, 1)
        if f == 2:
            return down(x, 1)
        return x

    def widened(x, extra):
        return x[:2] + [jnp.where(below, x[2], extra), jnp.where(below, extra, x[2])]

    def narrowed(x):
        return x[:2] + [jnp.where(below, x[2], x[3])]

    def fields_of(member, t, at):
        return [[load(member, t, (at + f) * TILES + c) for c in range(TILES)] for f in range(FIELDS)]

    def extras_of(member, t):
        shifts = [of_half([m - REACH - WINDS - f * SLOT for m in merges]) for f in range(FIELDS)]
        return [pltpu.roll(mixed[member][t], by, 1) for by in shifts]

    def stag(state):
        return [staggered(f, x) for f, x in enumerate(state)]

    def wind(comp):
        sent = [mixed[turn % 2][turn // 2] for turn in range(2 * subwins)]
        left = sent[2 * TILES + comp]
        tiles = []
        for c in range(TILES):
            by = WINDS - c * SLOT * FIELDS
            tiles.append(jnp.where(lane < WINDS, sent[comp * TILES + c], pltpu.roll(left, by, 1)))
        return tiles, pltpu.roll(sent[comp * TILES], of_half([m + 1 - LANES for m in merges]), 1)

    stay = 1.0 - 4.0 * diffusion
    grad_p = jnp.where(row == ROWS - 2, 0.0, speed)
    grad_m = jnp.where(row == ROWS - 1, 0.0, speed)
    before_p = jnp.where(row == 0, 0.0, speed)
    before_m = jnp.where(row == 1, 0.0, speed)
    div_p = jnp.where(row == ROWS - 1, 0.0, speed)
    div_m = jnp.where(row == 0, 0.0, speed)

    def coefficients(east, north):
        return (
            [diffusion - 0.5 * v for v in east],
            [diffusion + 0.5 * v for v in east],
            [jnp.where(row == ROWS - 1, 0.0, diffusion - 0.5 * v) for v in north],
            [jnp.where(row == 0, 0.0, diffusion + 0.5 * v) for v in north],
        )

    (east, east_extra), (north, north_extra) = wind(0), wind(1)
    narrow = coefficients(east, north)
    wide = coefficients(widened(east, east_extra), widened(north, north_extra))

    here = 2.0 * speed * speed + (div_p * grad_m + div_m * before_p)
    along, north_of, south_of = speed * speed, div_p * grad_p, div_m * before_m

    def divergence(u, v):
        return [
            speed * (a - b) + (div_p * c - div_m * d) for a, b, c, d in zip(u, back(u, 2), v, down(v, 2))
        ]

    def spread(h):
        ahead_h, up_h = ahead(h, 2), up(h, 2)
        change = [
            (along * (n + m) + (north_of * p + south_of * q)) - here * a
            for a, n, m, p, q in zip(h, ahead_h, back(h, 2), up_h, down(h, 2))
        ]
        return change, ahead_h, up_h

    def gradients(hs, aheads, ups):
        here_h, ahead_h, up_h = ([sum(x[1:], x[0]) for x in zip(*y)] for y in (hs, aheads, ups))
        east = [speed * (n - m) for n, m in zip(ahead_h, here_h)]
        north = [grad_p * n - grad_m * m for n, m in zip(up_h, here_h)]
        return east, north

    def tangent(state, coefs):
        h, u, v, q = state
        flow = divergence(u, v)
        passed = []
        for _ in range(STEPS):
            change, ahead_h, up_h = spread(h)
            passed.append((h, ahead_h, up_h))
            flow = [a - b for a, b in zip(flow, change)]
            h = [a - b for a, b in zip(h, flow)]
            q = [
                stay * a + (em * e + ep * w) + (nm * n + np * s) + couple * p
                for a, em, e, ep, w, nm, n, np, s, p in zip(
                    q, coefs[0], ahead(q, 1), coefs[1], back(q, 1), coefs[2], up(q, 1), coefs[3], down(q, 1), h
                )
            ]
        east, north = gradients(*zip(*passed))
        return [h, [a - b for a, b in zip(u, east)], [a - b for a, b in zip(v, north)], q]

    def adjoint(state, coefs):
        h, u, v, q = state
        flow = divergence(u, v)
        passed = []
        for _ in range(STEPS):
            h = [a + couple * b for a, b in zip(h, q)]
            change, ahead_h, up_h = spread(h)
            passed.append((h, ahead_h, up_h))
            flow = [a + b for a, b in zip(flow, change)]
            h = [a + b for a, b in zip(h, flow)]
            e = ahead([a * b for a, b in zip(coefs[1], q)], 1)
            w = back([a * b for a, b in zip(coefs[0], q)], 1)
            n = up([a * b for a, b in zip(coefs[3], q)], 1)
            s = down([a * b for a, b in zip(coefs[2], q)], 1)
            q = [stay * a + (b + c) + (d + f) for a, b, c, d, f in zip(q, e, w, n, s)]
        east, north = gradients(*zip(*passed))
        return [h, [a + b for a, b in zip(u, east)], [a + b for a, b in zip(v, north)], q]

    def each(fn, *states):
        return [[fn(*vals) for vals in zip(*xs)] for xs in zip(*states)]

    def operate(p, p_wide, precision, observed):
        weighted = []
        for t in range(subwins):
            change = p[t]
            if t > 0:
                moved = tangent(p[t - 1], narrow) if p_wide is None else tangent(p_wide[t - 1], wide)
                if p_wide is not None:
                    moved = [narrowed(x) for x in moved]
                change = each(lambda a, b: a - b, change, moved)
            weighted.append(each(lambda a, b: a * b, precision[t], change))
        image = []
        for t in range(subwins):
            out = each(lambda w, o, d: w + o * d, weighted[t], observed[t], p[t])
            if t + 1 < subwins:
                moved = adjoint(weighted[t + 1], narrow)
                out = each(lambda a, b: a - b, out, moved)
            image.append(out)
        return image

    def flat(x):
        return [(c, v) for state in x for field in state for c, v in enumerate(field)]

    def total(terms):
        inner, edge = None, None
        for c, v in terms:
            if c < TILES - 1:
                inner = v if inner is None else inner + v
            else:
                edge = v if edge is None else edge + v
        both = inner + jnp.where(free, 0.0, edge)
        return jnp.sum(both, axis=(0, 1), keepdims=True)

    def dot(x, y):
        return total([(c, v * w) for (c, v), (_, w) in zip(x, y)])

    precision = [stag(fields_of(0, t, FIELDS)) for t in range(subwins)]
    observed = [stag(fields_of(1, t, FIELDS)) for t in range(subwins)]
    for member in range(2):
        plain = [fields_of(member, t, 0) for t in range(subwins)]
        b_wide = [
            stag([widened(x, e) for x, e in zip(plain[t], extras_of(member, t))]) for t in range(subwins - 1)
        ]
        b = [[narrowed(x) for x in state] for state in b_wide] + [stag(plain[-1])]
        one = operate(b, b_wide, precision, observed)
        two = operate(one, None, precision, observed)
        one, two = [[[aligned(f, x) for f, x in enumerate(state)] for state in y] for y in (one, two)]
        f0, f1, f2 = flat(plain), flat(one), flat(two)
        s00, s01, s11, s02, s12 = dot(f0, f0), dot(f0, f1), dot(f1, f1), dot(f0, f2), dot(f1, f2)
        step = jnp.where(s11 > 0.0, s01 / jnp.where(s11 > 0.0, s11, 1.0), 0.0)
        more = 2.0 - jnp.where(s00 > 0.0, step * s01 / jnp.where(s00 > 0.0, s00, 1.0), 0.0)
        step_t = jnp.broadcast_to(step, (ROWS, LANES))
        more_t = jnp.broadcast_to(more, (ROWS, LANES))
        res = [(c, v - step_t * w) for (c, v), (_, w) in zip(f0, f1)]
        mov = [(c, more_t * v - step_t * w) for (c, v), (_, w) in zip(f0, f1)]
        img = [(c, more_t * v - step_t * w) for (c, v), (_, w) in zip(f1, f2)]
        sums = [step, more, s00, s01, s11, s02, s12, dot(res, res), dot(mov, img)]
        sums += [sums[-1]] * (-len(sums) % 6)
        for t in range(subwins):

            def put(k, value):
                start = (member * subwins + t) * ROWS * ROWS_OUT + k
                out_ref[pl.ds(start, ROWS, stride=ROWS_OUT), :] = value

            images = one[t] + two[t]
            last = images[-1][TILES - 1]
            for k, x in enumerate(images):
                put(2 * k, x[0])
                put(2 * k + 1, x[1])
                if k < 5:
                    put(THIRDS + k, jnp.where(free, pltpu.roll(last, (-(k + 1) * FREE) % LANES, 1), x[2]))
                elif k < 2 * FIELDS - 1:
                    rows = []
                    for i in (k - 5, k - 3):
                        value = sums[3 * i + 2]
                        for j in (1, 0):
                            value = jnp.where(lane < free_lo + (j + 1) * SLOT, sums[3 * i + j], value)
                        rows.append(value)
                    put(THIRDS + k, jnp.where(free, jnp.where(row % 2 == 0, rows[0], rows[1]), x[2]))


def finish_kernel(lon, merges, b_ref, in_ref, x_hbm, r_hbm, x_ref, r_ref, from_x_ref, from_r_ref, sems):
    _, levels, share, _ = b_ref.shape
    full = lon // LANES
    rest = lon - full * LANES
    size = share * ROWS_OUT
    apart = merges[0] - merges[1]
    at_lane = merges[0] - 3 * REACH

    group = ROWS // share

    slots = []
    for i in range(3):
        at = THIRDS + 5 + i % 2 + (i // 2) * ROWS_OUT
        halves = [in_ref[pl.ds(half * levels * size + at, levels, stride=size), :] for half in range(2)]
        slots.append(jnp.concatenate([halves[0], pltpu.roll(halves[1], apart, 1)], axis=0))

    def sums(i):
        value = slots[i // 3]
        return pltpu.roll(value, LANES - (i % 3) * SLOT, 1) if i % 3 else value

    step, more, s00, s01, s11, s02, s12, rr, mi = [sums(i) for i in range(9)]

    def total(x):
        return jnp.sum(x, axis=0, keepdims=True)

    norm_0 = total(s00)
    alpha_0 = norm_0 / total(s01)
    d = step - alpha_0
    norm_1 = total(rr + d * (2.0 * (s01 - step * s11) + d * s11))
    beta = norm_1 / norm_0
    g = (1.0 + beta) - more
    cross_d = more * (s02 + s11) - 2.0 * step * s12
    cross_g = 2.0 * more * s01 - step * (s11 + s02)
    curve = total(mi + d * (cross_d + d * s12 + g * (s11 + s02)) + g * (cross_g + g * s01))
    alpha_1 = norm_1 / curve
    first = alpha_0 + alpha_1 * (1.0 + beta)
    second = alpha_0 * alpha_1
    first = jnp.broadcast_to(first[:, at_lane : at_lane + 1], (ROWS, LANES))
    second = jnp.broadcast_to(second[:, at_lane : at_lane + 1], (ROWS, LANES))
    lane = lax.broadcasted_iota(jnp.int32, (ROWS, LANES), 1)

    def tiles_of(g, k):
        halves = []
        for half in range(2):
            start = (half * levels + g * group) * size

            def rows(j):
                return in_ref[pl.ds(start + j, ROWS, stride=ROWS_OUT), :]

            if k < 2 * FIELDS - 1:
                third = rows(THIRDS + k)
            else:
                third = None
                for i in range(5):
                    part = pltpu.roll(rows(THIRDS + i), (i + 1) * FREE % LANES, 1)
                    begin = (merges[half] - 3 * REACH + (i + 1) * FREE) % LANES
                    here = jnp.logical_and(lane >= begin, lane < begin + FREE)
                    third = part if third is None else jnp.where(here, part, third)
            halves.append([rows(2 * k), rows(2 * k + 1), third])
        middle = jnp.where(lane < at_lane, halves[0][2], halves[1][2])
        return halves[0][:2] + [middle] + halves[1]

    copies = []
    for f in range(FIELDS):
        for g in range(levels // group):
            for c, (one, two) in enumerate(zip(tiles_of(g, f), tiles_of(g, FIELDS + f))):
                at = pl.ds(g * ROWS, ROWS), pl.ds(c * LANES, LANES)
                from_x_ref[(f, *at)] = second * one
                from_r_ref[(f, *at)] = second * two - first * one
            for level in range(g * group, (g + 1) * group):
                at = pl.ds(level * share, share), pl.ds(0, lon)
                b = b_ref[f, level]
                x_ref[f, level] = first[:share, :1] * b - from_x_ref[(f, *at)]
                r_ref[f, level] = b + from_r_ref[(f, *at)]
        for i, (src, dst) in enumerate(((x_ref, x_hbm), (r_ref, r_hbm))):
            copies.append(pltpu.make_async_copy(src.at[f], dst.at[f], sems.at[i, f]))
            copies[-1].start()
    for copy in copies:
        copy.wait()


def by_layer(right_side, error_precision, obs_count, background_wind, wave_speed, tracer_coupling):
    _, fields, levels, share, lon = right_side.shape
    subwins = lax.axis_size("tm")
    merges = merge_lanes(lon)
    vmem = pl.BlockSpec(memory_space=pltpu.VMEM)
    hbm = pl.BlockSpec(memory_space=pltpu.HBM)
    params = pltpu.CompilerParams(vmem_limit_bytes=48 * 1024 * 1024)
    state = (fields, levels, share, lon)
    wide = (lon // LANES + 1) * LANES

    def exchange(x):
        x = x.reshape(2 * levels, -1, 1, LANES)
        return lax.all_to_all(x, ("ens", "tm", "space"), 0, 0, tiled=True).reshape(-1, LANES)

    b = right_side.reshape(state)
    given = (b, error_precision.reshape(state), obs_count.reshape(state), background_wind, wave_speed, tracer_coupling)
    with jax.named_scope("pack"):
        packed = pl.pallas_call(
            lambda *refs: pack_kernel(lon, merges, *refs),
            out_shape=jax.ShapeDtypeStruct((2 * levels * share * ROWS_IN, LANES), jnp.float32),
            in_specs=[hbm] * len(given),
            out_specs=vmem,
            scratch_shapes=[
                pltpu.VMEM(state, jnp.float32),
                pltpu.VMEM(state, jnp.float32),
                pltpu.VMEM(state, jnp.int32),
                pltpu.VMEM(background_wind.shape[1:], jnp.float32),
                pltpu.SMEM(wave_speed.shape, jnp.float32),
                pltpu.SMEM(tracer_coupling.shape, jnp.float32),
                pltpu.VMEM((fields, levels * share, wide), jnp.float32),
                pltpu.VMEM((fields, levels * share, wide), jnp.float32),
                pltpu.VMEM((levels * share, wide), jnp.float32),
                pltpu.SemaphoreType.DMA((9,)),
            ],
            compiler_params=params,
        )(*[pltpu.with_memory_space_constraint(x, pltpu.HBM) for x in given])
    packed = exchange(packed)
    with jax.named_scope("layer"):
        images = pl.pallas_call(
            lambda *refs: layer_kernel(lon, merges, subwins, *refs),
            out_shape=jax.ShapeDtypeStruct((2 * levels * share * ROWS_OUT, LANES), jnp.float32),
            in_specs=[vmem],
            out_specs=vmem,
            compiler_params=params,
        )(packed)
    images = exchange(images)
    with jax.named_scope("finish"):
        x, r = pl.pallas_call(
            lambda *refs: finish_kernel(lon, merges, *refs),
            out_shape=[jax.ShapeDtypeStruct(state, jnp.float32)] * 2,
            in_specs=[vmem] * 2,
            out_specs=[hbm] * 2,
            scratch_shapes=[
                pltpu.VMEM(state, jnp.float32),
                pltpu.VMEM(state, jnp.float32),
                pltpu.VMEM((fields, levels * share, wide), jnp.float32),
                pltpu.VMEM((fields, levels * share, wide), jnp.float32),
                pltpu.SemaphoreType.DMA((2, FIELDS)),
            ],
            compiler_params=params,
        )(b, images)
    return x.reshape(right_side.shape), r.reshape(right_side.shape)


def fits_by_layer(mesh, shape):
    space, tm, ens = mesh.shape["space"], mesh.shape["tm"], mesh.shape["ens"]
    subwins, fields, levels, lats, lon = shape
    return (
        (ens, tm, space, fields, lats) == (2, 4, 4, FIELDS, ROWS)
        and subwins == ens * tm
        and levels == space * tm
        and lon == 720
    )


def extended_2(cells, sides, width):
    for axis, dim in sides:
        count = lax.axis_size(axis)
        ends = count - 1
        head = lax.slice_in_dim(cells, 0, width, axis=dim)
        tail = lax.slice_in_dim(cells, cells.shape[dim] - width, cells.shape[dim], axis=dim)
        cells = jnp.concatenate(
            [
                lax.ppermute(tail, axis, [(i, (i + 1) % count) for i in range(ends)]),
                cells,
                lax.ppermute(head, axis, [((i + 1) % count, i) for i in range(ends)]),
            ],
            axis=dim,
        )
    return cells


def shifted(value, axis, by):
    peers = lax.axis_size(axis)
    pairs = [(i, i + by) for i in range(peers) if 0 <= i + by < peers]
    return lax.ppermute(value, axis, pairs)


def along_x(field):
    return 0.5 * (jnp.roll(field, -1, axis=-1) - jnp.roll(field, 1, axis=-1))


def second_x(field):
    return jnp.roll(field, -1, axis=-1) + jnp.roll(field, 1, axis=-1) - 2.0 * field


def along_y(extended):
    return 0.5 * (extended[..., 2:, :] - extended[..., :-2, :])


def trimmed(field, count):
    if count == 0:
        return field
    return field[..., count : field.shape[-2] - count, :]


def row_valid(lat_rows):
    first_row = lax.axis_index("space") * lat_rows - 4
    row_total = lat_rows * lax.axis_size("space")
    global_rows = first_row + jnp.arange(lat_rows + 8, dtype=jnp.int32)
    inside = jnp.logical_and(global_rows >= 0, global_rows < row_total)
    return inside.astype(jnp.float32)[:, None]


def tangent_core(state, margin, coefs):
    speed_col, couple_col, winds, have, valid = coefs
    height, east, north, tracer = (state[:, 0], state[:, 1], state[:, 2], state[:, 3])
    east_mid = east - speed_col * along_x(height)
    north_mid = (trimmed(north, 1) - speed_col * along_y(height)) * trimmed(valid, 5 - margin)
    height_new = trimmed(height, 2) - speed_col * (
        along_x(trimmed(east_mid, 2)) + along_y(north_mid)
    )
    tracer_one = trimmed(tracer, 1)
    inner = trimmed(tracer, 2)
    tracer_lap = second_x(inner) + tracer_one[..., 2:, :] + tracer_one[..., :-2, :] - 2.0 * inner
    wind_east = trimmed(winds[0], have - margin + 2)
    wind_north = trimmed(winds[1], have - margin + 2)
    tracer_new = (
        inner
        - wind_east * along_x(inner)
        - wind_north * along_y(tracer_one)
        + diffusion * tracer_lap
        + couple_col * height_new
    )
    result = jnp.stack(
        [height_new, trimmed(east_mid, 2), trimmed(north_mid, 1), tracer_new], axis=1
    )
    return result * trimmed(valid, 6 - margin)


def adjoint_core(state, margin, coefs):
    speed_col, couple_col, winds, have, valid = coefs
    height, east, north, tracer = (state[:, 0], state[:, 1], state[:, 2], state[:, 3])
    height_mix = height + couple_col * tracer
    east_mid = east + speed_col * along_x(height_mix)
    north_mid = (trimmed(north, 1) + speed_col * along_y(height_mix)) * trimmed(valid, 5 - margin)
    height_new = trimmed(height_mix, 2) + speed_col * (
        along_x(trimmed(east_mid, 2)) + along_y(north_mid)
    )
    tracer_one = trimmed(tracer, 1)
    inner = trimmed(tracer, 2)
    tracer_lap = second_x(inner) + tracer_one[..., 2:, :] + tracer_one[..., :-2, :] - 2.0 * inner
    wind_east = trimmed(winds[0], have - margin + 2)
    wind_north = trimmed(winds[1], have - margin + 1)
    tracer_new = (
        inner
        + along_x(wind_east * inner)
        + along_y(wind_north * tracer_one)
        + diffusion * tracer_lap
    )
    result = jnp.stack(
        [height_new, trimmed(east_mid, 2), trimmed(north_mid, 1), tracer_new], axis=1
    )
    return result * trimmed(valid, 6 - margin)


def rebuild(state, sent):
    widths = [(0, 0)] * (state.ndim - 3) + [(2, 2), (0, 0)]
    east_wide = jnp.pad(state[:, 1], widths)
    return jnp.stack([sent[:, 0], east_wide, sent[:, 1], sent[:, 2]], axis=1)


def tangent_near(state):
    picked = jnp.stack([state[:, 0], state[:, 2], state[:, 3]], axis=1)
    sent = extended_2(picked, (("space", 3),), 2)
    return rebuild(state, sent)


def adjoint_near(state):
    picked = jnp.stack([state[:, 0], state[:, 2], state[:, 3]], axis=1)
    sent = extended_2(picked, (("space", 3),), 2)
    return rebuild(state, sent)


def propagate(fields, step_core, near_fn, coefs):
    current = fields
    for step in range(STEPS):
        current = step_core(near_fn(current), 2, coefs)
    return current


def operate(direction, error_precision, observed, coefs):
    moved = propagate(direction, tangent_core, tangent_near, coefs)
    incoming = shifted(moved, "tm", 1)
    previous = jnp.concatenate([incoming, moved[:-1]], axis=0)
    weighted = error_precision * (direction - previous)
    back = propagate(weighted, adjoint_core, adjoint_near, coefs)
    arriving = shifted(back, "tm", -1)
    following = jnp.concatenate([back[1:], arriving], axis=0)
    return weighted - following + observed * direction


def squares(residual):
    return lax.psum(jnp.sum(residual * residual), ("space", "tm"))


def on_device(right_side, error_precision, obs_count, background_wind, wave_speed, tracer_coupling):
    lat_rows = right_side.shape[3]
    valid = row_valid(lat_rows)
    winds = extended_2(background_wind, (("space", 2),), 1)
    have = 1
    coefs = (wave_speed[:, None, None], tracer_coupling[:, None, None], winds, have, valid)
    observed = obs_count.astype(jnp.float32)
    solution_field = jnp.zeros_like(right_side)
    residual = right_side
    direction = right_side
    norm_now = squares(residual)
    for step in range(ITERS):
        image = operate(direction, error_precision, observed, coefs)
        alpha = norm_now / lax.psum(jnp.sum(direction * image), ("space", "tm"))
        solution_field = solution_field + alpha * direction
        residual = residual - alpha * image
        norm_next = squares(residual)
        direction = residual + norm_next / norm_now * direction
        norm_now = norm_next
    return (solution_field, residual)


def solution(mesh):
    def run(right_side, *others):
        body = by_layer if fits_by_layer(mesh, right_side.shape) else on_device
        return jax.shard_map(
            body,
            mesh=mesh,
            in_specs=(
                P(("ens", "tm"), None, None, "space", None),
                P("tm", None, None, "space", None),
                P("tm", None, None, "space", None),
                P(None, None, "space", None),
                P(),
                P(),
            ),
            out_specs=(
                P(("ens", "tm"), None, None, "space", None),
                P(("ens", "tm"), None, None, "space", None),
            ),
            check_vma=False,
        )(right_side, *others)

    return run
```

```python
import jax
import jax.numpy as jnp
from jax import lax
from jax.experimental import pallas as pl
from jax.experimental.pallas import tpu as pltpu
from jax.sharding import PartitionSpec as P

STEPS = 2
ITERS = 2


diffusion = 0.1


LANES = 128
ROWS = 8
TILES = 3
REACH = 4
FIELDS = 4
SLOT = 2 * REACH
WINDS = LANES - FIELDS * SLOT
FREE = 6 * REACH
MIXED = 2 * FIELDS * TILES
ROWS_IN = MIXED + 1
THIRDS = 4 * FIELDS
ROWS_OUT = THIRDS + 2 * FIELDS - 1


def merge_lanes(lon):
    core = lon // 2
    return (core + 3 * REACH) % LANES, (core - 3 * REACH) % LANES


def pack_kernel(
    lon, merges, b_hbm, e_hbm, o_hbm, w_hbm, speed_hbm, couple_hbm, out_ref,
    b_ref, e_ref, o_ref, w_ref, speed_ref, couple_ref, b_row_ref, s_row_ref, w_row_ref, sems,
):
    _, levels, share, _ = b_ref.shape
    full = lon // LANES
    rest = lon - full * LANES
    member = lax.axis_index("ens")
    turn = lax.axis_index("tm") * 2 + member
    comp = jnp.where(turn < 2 * TILES, turn // TILES, turn - 2 * TILES)

    copy_b = pltpu.make_async_copy(b_hbm, b_ref, sems.at[0])
    copy_e = pltpu.make_async_copy(e_hbm, e_ref, sems.at[1])
    copy_o = pltpu.make_async_copy(o_hbm, o_ref, sems.at[2])
    others = (
        pltpu.make_async_copy(w_hbm.at[comp], w_ref, sems.at[3]),
        pltpu.make_async_copy(speed_hbm, speed_ref, sems.at[4]),
        pltpu.make_async_copy(couple_hbm, couple_ref, sems.at[5]),
    )
    copy_b.start()
    pl.when(member == 0)(copy_e.start)
    pl.when(member != 0)(copy_o.start)
    for copy in others:
        copy.start()
    lane = lax.broadcasted_iota(jnp.int32, (ROWS, LANES), 1)
    row = lax.broadcasted_iota(jnp.int32, (ROWS, LANES), 0)
    group = ROWS // share

    def stage(copy, ref, row_ref):
        copy.wait()
        for f in range(FIELDS):
            for level in range(levels):
                row_ref[f, pl.ds(level * share, share), pl.ds(0, lon)] = ref[f, level].astype(jnp.float32)

    def place(half, g, k):
        return pl.ds((half * levels + g * group) * share * ROWS_IN + k, ROWS, stride=ROWS_IN), slice(None)

    def windows(first, third, last):
        before = pltpu.roll(last, LANES - rest, 1)
        after = jnp.where(lane < rest, last, pltpu.roll(first, rest, 1))
        ends = ((third, before), (after, third))
        merged = [jnp.where(lane < m, x, y) for m, (x, y) in zip(merges, ends)]
        extra = [jnp.where(lane < m, y, x) for m, (x, y) in zip(merges, ends)]
        return merged, extra

    def put(g, k, row_ref, f):
        tiles = [row_ref[f, pl.ds(g * ROWS, ROWS), pl.ds(c * LANES, LANES)] for c in range(full + 1)]
        merged, extra = windows(tiles[0], tiles[2], tiles[5])
        for half in range(2):
            for c, value in enumerate(tiles[TILES * half : TILES * half + 2] + [merged[half]]):
                out_ref[place(half, g, k + c)] = value
        return extra

    def by_level(ref, g):
        value = jnp.full((ROWS, LANES), ref[g * group], jnp.float32)
        for i in range(1, group):
            value = jnp.where(row < i * share, value, ref[g * group + i])
        return value

    stage(copy_b, b_ref, b_row_ref)
    pl.when(member == 0)(lambda: stage(copy_e, e_ref, s_row_ref))
    pl.when(member != 0)(lambda: stage(copy_o, o_ref, s_row_ref))
    for copy in others:
        copy.wait()
    for level in range(levels):
        w_row_ref[pl.ds(level * share, share), pl.ds(0, lon)] = w_ref[level]
    for g in range(levels // group):
        mixed = [None, None]
        for f in range(FIELDS):
            extra = put(g, f * TILES, b_row_ref, f)
            for half, m in enumerate(merges):
                at = WINDS + f * SLOT
                moved = pltpu.roll(extra[half], (at - (m - REACH)) % LANES, 1)
                mixed[half] = moved if f == 0 else jnp.where(lane < at, mixed[half], moved)
        tiles = [w_row_ref[pl.ds(g * ROWS, ROWS), pl.ds(c * LANES, LANES)] for c in range(full + 1)]
        merged, extra = windows(tiles[0], tiles[2], tiles[5])
        speed, couple = by_level(speed_ref, g), by_level(couple_ref, g)
        for half, m in enumerate(merges):
            parts = tiles[TILES * half : TILES * half + 2] + [merged[half]]
            wind, left = parts[TILES - 1], pltpu.roll(parts[TILES - 1], LANES - SLOT * FIELDS, 1)
            for c in reversed(range(TILES - 1)):
                wind = jnp.where(jnp.logical_or(turn == c, turn == TILES + c), parts[c], wind)
                by = (c + 1) * SLOT * FIELDS
                left = jnp.where(lane < by, pltpu.roll(parts[c], by, 1), left)
            wind = jnp.where(turn < 2 * TILES, wind, left)
            value = jnp.where(lane < WINDS, wind, mixed[half])
            value = jnp.where(lane == WINDS + SLOT, speed, value)
            value = jnp.where(lane == WINDS + 2 * SLOT - 1, couple, value)
            ends = pltpu.roll(extra[half], LANES - 1 - m, 1)
            value = jnp.where(lane >= LANES - 2, ends, value)
            out_ref[place(half, g, MIXED)] = value

    for g in range(levels // group):
        for f in range(FIELDS):
            put(g, (FIELDS + f) * TILES, s_row_ref, f)


def layer_kernel(lon, merges, subwins, in_ref, out_ref):
    half = lax.axis_index("ens")
    lane = lax.broadcasted_iota(jnp.int32, (ROWS, LANES), 1)
    row = lax.broadcasted_iota(jnp.int32, (ROWS, LANES), 0)
    below = lane < jnp.where(half == 0, merges[0], merges[1])
    free_lo = jnp.where(half == 0, merges[0] - 3 * REACH, merges[1] - 3 * REACH)
    free = jnp.logical_and(lane >= free_lo, lane < free_lo + FREE)

    def load(member, t, k):
        return in_ref[pl.ds((member * subwins + t) * ROWS * ROWS_IN + k, ROWS, stride=ROWS_IN), :]

    def of_half(values):
        return jnp.where(half == 0, values[0] % LANES, values[1] % LANES)

    mixed = [[load(member, t, MIXED) for t in range(subwins)] for member in range(2)]
    speed_at, couple_at = WINDS + SLOT, WINDS + 2 * SLOT - 1
    speed = 0.5 * jnp.broadcast_to(mixed[0][0][:, speed_at : speed_at + 1], (ROWS, LANES))
    couple = jnp.broadcast_to(mixed[0][0][:, couple_at : couple_at + 1], (ROWS, LANES))

    def back(x, by):
        moved = [pltpu.roll(v, by, 1) for v in x]
        return [jnp.where(lane < by, moved[i - 1], v) for i, v in enumerate(moved)]

    def ahead(x, by):
        moved = [pltpu.roll(v, LANES - by, 1) for v in x]
        return [jnp.where(lane >= LANES - by, moved[(i + 1) % len(x)], v) for i, v in enumerate(moved)]

    def up(x, by):
        return [pltpu.roll(v, ROWS - by, 0) for v in x]

    def down(x, by):
        return [pltpu.roll(v, by, 0) for v in x]

    def staggered(f, x):
        if f == 1:
            return ahead(x, 1)
        if f == 2:
            return up(x, 1)
        return x

    def aligned(f, x):
        if f == 1:
            return back(x, 1)
        if f == 2:
            return down(x, 1)
        return x

    def widened(x, extra):
        return x[:2] + [jnp.where(below, x[2], extra), jnp.where(below, extra, x[2])]

    def narrowed(x):
        return x[:2] + [jnp.where(below, x[2], x[3])]

    def fields_of(member, t, at):
        return [[load(member, t, (at + f) * TILES + c) for c in range(TILES)] for f in range(FIELDS)]

    def extras_of(member, t):
        shifts = [of_half([m - REACH - WINDS - f * SLOT for m in merges]) for f in range(FIELDS)]
        return [pltpu.roll(mixed[member][t], by, 1) for by in shifts]

    def stag(state):
        return [staggered(f, x) for f, x in enumerate(state)]

    def wind(comp):
        sent = [mixed[turn % 2][turn // 2] for turn in range(2 * subwins)]
        left = sent[2 * TILES + comp]
        tiles = []
        for c in range(TILES):
            by = WINDS - c * SLOT * FIELDS
            tiles.append(jnp.where(lane < WINDS, sent[comp * TILES + c], pltpu.roll(left, by, 1)))
        return tiles, pltpu.roll(sent[comp * TILES], of_half([m + 1 - LANES for m in merges]), 1)

    stay = 1.0 - 4.0 * diffusion
    grad_p = jnp.where(row == ROWS - 2, 0.0, speed)
    grad_m = jnp.where(row == ROWS - 1, 0.0, speed)
    before_p = jnp.where(row == 0, 0.0, speed)
    before_m = jnp.where(row == 1, 0.0, speed)
    div_p = jnp.where(row == ROWS - 1, 0.0, speed)
    div_m = jnp.where(row == 0, 0.0, speed)

    def coefficients(east, north):
        return (
            [diffusion - 0.5 * v for v in east],
            [diffusion + 0.5 * v for v in east],
            [jnp.where(row == ROWS - 1, 0.0, diffusion - 0.5 * v) for v in north],
            [jnp.where(row == 0, 0.0, diffusion + 0.5 * v) for v in north],
        )

    (east, east_extra), (north, north_extra) = wind(0), wind(1)
    narrow = coefficients(east, north)
    wide = coefficients(widened(east, east_extra), widened(north, north_extra))

    here = 2.0 * speed * speed + (div_p * grad_m + div_m * before_p)
    along, north_of, south_of = speed * speed, div_p * grad_p, div_m * before_m

    def divergence(u, v):
        return [
            speed * (a - b) + (div_p * c - div_m * d) for a, b, c, d in zip(u, back(u, 2), v, down(v, 2))
        ]

    def spread(h):
        ahead_h, up_h = ahead(h, 2), up(h, 2)
        change = [
            (along * (n + m) + (north_of * p + south_of * q)) - here * a
            for a, n, m, p, q in zip(h, ahead_h, back(h, 2), up_h, down(h, 2))
        ]
        return change, ahead_h, up_h

    def gradients(hs, aheads, ups):
        here_h, ahead_h, up_h = ([sum(x[1:], x[0]) for x in zip(*y)] for y in (hs, aheads, ups))
        east = [speed * (n - m) for n, m in zip(ahead_h, here_h)]
        north = [grad_p * n - grad_m * m for n, m in zip(up_h, here_h)]
        return east, north

    def tangent(state, coefs):
        h, u, v, q = state
        flow = divergence(u, v)
        passed = []
        for _ in range(STEPS):
            change, ahead_h, up_h = spread(h)
            passed.append((h, ahead_h, up_h))
            flow = [a - b for a, b in zip(flow, change)]
            h = [a - b for a, b in zip(h, flow)]
            q = [
                stay * a + (em * e + ep * w) + (nm * n + np * s) + couple * p
                for a, em, e, ep, w, nm, n, np, s, p in zip(
                    q, coefs[0], ahead(q, 1), coefs[1], back(q, 1), coefs[2], up(q, 1), coefs[3], down(q, 1), h
                )
            ]
        east, north = gradients(*zip(*passed))
        return [h, [a - b for a, b in zip(u, east)], [a - b for a, b in zip(v, north)], q]

    def adjoint(state, coefs):
        h, u, v, q = state
        flow = divergence(u, v)
        passed = []
        for _ in range(STEPS):
            h = [a + couple * b for a, b in zip(h, q)]
            change, ahead_h, up_h = spread(h)
            passed.append((h, ahead_h, up_h))
            flow = [a + b for a, b in zip(flow, change)]
            h = [a + b for a, b in zip(h, flow)]
            e = ahead([a * b for a, b in zip(coefs[1], q)], 1)
            w = back([a * b for a, b in zip(coefs[0], q)], 1)
            n = up([a * b for a, b in zip(coefs[3], q)], 1)
            s = down([a * b for a, b in zip(coefs[2], q)], 1)
            q = [stay * a + (b + c) + (d + f) for a, b, c, d, f in zip(q, e, w, n, s)]
        east, north = gradients(*zip(*passed))
        return [h, [a + b for a, b in zip(u, east)], [a + b for a, b in zip(v, north)], q]

    def each(fn, *states):
        return [[fn(*vals) for vals in zip(*xs)] for xs in zip(*states)]

    def operate(p, p_wide, precision, observed):
        weighted = []
        for t in range(subwins):
            change = p[t]
            if t > 0:
                moved = tangent(p[t - 1], narrow) if p_wide is None else tangent(p_wide[t - 1], wide)
                if p_wide is not None:
                    moved = [narrowed(x) for x in moved]
                change = each(lambda a, b: a - b, change, moved)
            weighted.append(each(lambda a, b: a * b, precision[t], change))
        image = []
        for t in range(subwins):
            out = each(lambda w, o, d: w + o * d, weighted[t], observed[t], p[t])
            if t + 1 < subwins:
                moved = adjoint(weighted[t + 1], narrow)
                out = each(lambda a, b: a - b, out, moved)
            image.append(out)
        return image

    def flat(x):
        return [(c, v) for state in x for field in state for c, v in enumerate(field)]

    def total(terms):
        inner, edge = None, None
        for c, v in terms:
            if c < TILES - 1:
                inner = v if inner is None else inner + v
            else:
                edge = v if edge is None else edge + v
        both = inner + jnp.where(free, 0.0, edge)
        return jnp.sum(both, axis=(0, 1), keepdims=True)

    def dot(x, y):
        return total([(c, v * w) for (c, v), (_, w) in zip(x, y)])

    precision = [stag(fields_of(0, t, FIELDS)) for t in range(subwins)]
    observed = [stag(fields_of(1, t, FIELDS)) for t in range(subwins)]
    for member in range(2):
        plain = [fields_of(member, t, 0) for t in range(subwins)]
        b_wide = [
            stag([widened(x, e) for x, e in zip(plain[t], extras_of(member, t))]) for t in range(subwins - 1)
        ]
        b = [[narrowed(x) for x in state] for state in b_wide] + [stag(plain[-1])]
        one = operate(b, b_wide, precision, observed)
        two = operate(one, None, precision, observed)
        one, two = [[[aligned(f, x) for f, x in enumerate(state)] for state in y] for y in (one, two)]
        f0, f1, f2 = flat(plain), flat(one), flat(two)
        s00, s01, s11, s02, s12 = dot(f0, f0), dot(f0, f1), dot(f1, f1), dot(f0, f2), dot(f1, f2)
        step = jnp.where(s11 > 0.0, s01 / jnp.where(s11 > 0.0, s11, 1.0), 0.0)
        more = 2.0 - jnp.where(s00 > 0.0, step * s01 / jnp.where(s00 > 0.0, s00, 1.0), 0.0)
        step_t = jnp.broadcast_to(step, (ROWS, LANES))
        more_t = jnp.broadcast_to(more, (ROWS, LANES))
        res = [(c, v - step_t * w) for (c, v), (_, w) in zip(f0, f1)]
        mov = [(c, more_t * v - step_t * w) for (c, v), (_, w) in zip(f0, f1)]
        img = [(c, more_t * v - step_t * w) for (c, v), (_, w) in zip(f1, f2)]
        sums = [step, more, s00, s01, s11, s02, s12, dot(res, res), dot(mov, img)]
        sums += [sums[-1]] * (-len(sums) % 6)
        for t in range(subwins):

            def put(k, value):
                start = (member * subwins + t) * ROWS * ROWS_OUT + k
                out_ref[pl.ds(start, ROWS, stride=ROWS_OUT), :] = value

            images = one[t] + two[t]
            last = images[-1][TILES - 1]
            for k, x in enumerate(images):
                put(2 * k, x[0])
                put(2 * k + 1, x[1])
                if k < 5:
                    put(THIRDS + k, jnp.where(free, pltpu.roll(last, (-(k + 1) * FREE) % LANES, 1), x[2]))
                elif k < 2 * FIELDS - 1:
                    rows = []
                    for i in (k - 5, k - 3):
                        value = sums[3 * i + 2]
                        for j in (1, 0):
                            value = jnp.where(lane < free_lo + (j + 1) * SLOT, sums[3 * i + j], value)
                        rows.append(value)
                    put(THIRDS + k, jnp.where(free, jnp.where(row % 2 == 0, rows[0], rows[1]), x[2]))


def finish_kernel(lon, merges, b_ref, in_ref, x_hbm, r_hbm, x_ref, r_ref, from_x_ref, from_r_ref, sems):
    _, levels, share, _ = b_ref.shape
    full = lon // LANES
    rest = lon - full * LANES
    size = share * ROWS_OUT
    apart = merges[0] - merges[1]
    at_lane = merges[0] - 3 * REACH
    group = ROWS // share

    slots = []
    for i in range(3):
        at = THIRDS + 5 + i % 2 + (i // 2) * ROWS_OUT
        halves = [in_ref[pl.ds(half * levels * size + at, levels, stride=size), :] for half in range(2)]
        slots.append(jnp.concatenate([halves[0], pltpu.roll(halves[1], apart, 1)], axis=0))

    def sums(i):
        value = slots[i // 3]
        return pltpu.roll(value, LANES - (i % 3) * SLOT, 1) if i % 3 else value

    step, more, s00, s01, s11, s02, s12, rr, mi = [sums(i) for i in range(9)]

    def total(x):
        return jnp.sum(x, axis=0, keepdims=True)

    norm_0 = total(s00)
    alpha_0 = norm_0 / total(s01)
    d = step - alpha_0
    norm_1 = total(rr + d * (2.0 * (s01 - step * s11) + d * s11))
    beta = norm_1 / norm_0
    g = (1.0 + beta) - more
    cross_d = more * (s02 + s11) - 2.0 * step * s12
    cross_g = 2.0 * more * s01 - step * (s11 + s02)
    curve = total(mi + d * (cross_d + d * s12 + g * (s11 + s02)) + g * (cross_g + g * s01))
    alpha_1 = norm_1 / curve
    first = alpha_0 + alpha_1 * (1.0 + beta)
    second = alpha_0 * alpha_1
    first = jnp.broadcast_to(first[:, at_lane : at_lane + 1], (ROWS, LANES))
    second = jnp.broadcast_to(second[:, at_lane : at_lane + 1], (ROWS, LANES))
    lane = lax.broadcasted_iota(jnp.int32, (ROWS, LANES), 1)

    def tiles_of(g, k):
        halves = []
        for half in range(2):
            start = (half * levels + g * group) * size

            def rows(j):
                return in_ref[pl.ds(start + j, ROWS, stride=ROWS_OUT), :]

            if k < 2 * FIELDS - 1:
                third = rows(THIRDS + k)
            else:
                third = None
                for i in range(5):
                    part = pltpu.roll(rows(THIRDS + i), (i + 1) * FREE % LANES, 1)
                    begin = (merges[half] - 3 * REACH + (i + 1) * FREE) % LANES
                    here = jnp.logical_and(lane >= begin, lane < begin + FREE)
                    third = part if third is None else jnp.where(here, part, third)
            halves.append([rows(2 * k), rows(2 * k + 1), third])
        middle = jnp.where(lane < at_lane, halves[0][2], halves[1][2])
        return halves[0][:2] + [middle] + halves[1]

    copies = []
    for f in range(FIELDS):
        for g in range(levels // group):
            for c, (one, two) in enumerate(zip(tiles_of(g, f), tiles_of(g, FIELDS + f))):
                at = pl.ds(g * ROWS, ROWS), pl.ds(c * LANES, LANES)
                from_x_ref[(f, *at)] = second * one
                from_r_ref[(f, *at)] = second * two - first * one
            for level in range(g * group, (g + 1) * group):
                at = pl.ds(level * share, share), pl.ds(0, lon)
                b = b_ref[f, level]
                x_ref[f, level] = first[:share, :1] * b - from_x_ref[(f, *at)]
                r_ref[f, level] = b + from_r_ref[(f, *at)]
        for i, (src, dst) in enumerate(((x_ref, x_hbm), (r_ref, r_hbm))):
            copies.append(pltpu.make_async_copy(src.at[f], dst.at[f], sems.at[i, f]))
            copies[-1].start()
    for copy in copies:
        copy.wait()


def by_layer(right_side, error_precision, obs_count, background_wind, wave_speed, tracer_coupling):
    _, fields, levels, share, lon = right_side.shape
    subwins = lax.axis_size("tm")
    merges = merge_lanes(lon)
    vmem = pl.BlockSpec(memory_space=pltpu.VMEM)
    hbm = pl.BlockSpec(memory_space=pltpu.HBM)
    params = pltpu.CompilerParams(vmem_limit_bytes=48 * 1024 * 1024)
    state = (fields, levels, share, lon)
    wide = (lon // LANES + 1) * LANES

    def exchange(x):
        x = x.reshape(2 * levels, -1, 1, LANES)
        return lax.all_to_all(x, ("ens", "tm", "space"), 0, 0, tiled=True).reshape(-1, LANES)

    b = right_side.reshape(state)
    given = (b, error_precision.reshape(state), obs_count.reshape(state), background_wind, wave_speed, tracer_coupling)
    with jax.named_scope("pack"):
        packed = pl.pallas_call(
            lambda *refs: pack_kernel(lon, merges, *refs),
            out_shape=jax.ShapeDtypeStruct((2 * levels * share * ROWS_IN, LANES), jnp.float32),
            in_specs=[hbm] * len(given),
            out_specs=vmem,
            scratch_shapes=[
                pltpu.VMEM(state, jnp.float32),
                pltpu.VMEM(state, jnp.float32),
                pltpu.VMEM(state, jnp.int32),
                pltpu.VMEM(background_wind.shape[1:], jnp.float32),
                pltpu.SMEM(wave_speed.shape, jnp.float32),
                pltpu.SMEM(tracer_coupling.shape, jnp.float32),
                pltpu.VMEM((fields, levels * share, wide), jnp.float32),
                pltpu.VMEM((fields, levels * share, wide), jnp.float32),
                pltpu.VMEM((levels * share, wide), jnp.float32),
                pltpu.SemaphoreType.DMA((len(given),)),
            ],
            compiler_params=params,
        )(*[pltpu.with_memory_space_constraint(x, pltpu.HBM) for x in given])
    packed = exchange(packed)
    with jax.named_scope("layer"):
        images = pl.pallas_call(
            lambda *refs: layer_kernel(lon, merges, subwins, *refs),
            out_shape=jax.ShapeDtypeStruct((2 * levels * share * ROWS_OUT, LANES), jnp.float32),
            in_specs=[vmem],
            out_specs=vmem,
            compiler_params=params,
        )(packed)
    images = exchange(images)
    with jax.named_scope("finish"):
        x, r = pl.pallas_call(
            lambda *refs: finish_kernel(lon, merges, *refs),
            out_shape=[jax.ShapeDtypeStruct(state, jnp.float32)] * 2,
            in_specs=[vmem] * 2,
            out_specs=[hbm] * 2,
            scratch_shapes=[
                pltpu.VMEM(state, jnp.float32),
                pltpu.VMEM(state, jnp.float32),
                pltpu.VMEM((fields, levels * share, wide), jnp.float32),
                pltpu.VMEM((fields, levels * share, wide), jnp.float32),
                pltpu.SemaphoreType.DMA((2, FIELDS)),
            ],
            compiler_params=params,
        )(b, images)
    return x.reshape(right_side.shape), r.reshape(right_side.shape)


def fits_by_layer(mesh, shape):
    space, tm, ens = mesh.shape["space"], mesh.shape["tm"], mesh.shape["ens"]
    subwins, fields, levels, lats, lon = shape
    return (
        (ens, tm, space, fields, lats) == (2, 4, 4, FIELDS, ROWS)
        and subwins == ens * tm
        and levels == space * tm
        and lon == 720
    )


def extended_2(cells, sides, width):
    for axis, dim in sides:
        count = lax.axis_size(axis)
        ends = count - 1
        head = lax.slice_in_dim(cells, 0, width, axis=dim)
        tail = lax.slice_in_dim(cells, cells.shape[dim] - width, cells.shape[dim], axis=dim)
        cells = jnp.concatenate(
            [
                lax.ppermute(tail, axis, [(i, (i + 1) % count) for i in range(ends)]),
                cells,
                lax.ppermute(head, axis, [((i + 1) % count, i) for i in range(ends)]),
            ],
            axis=dim,
        )
    return cells


def shifted(value, axis, by):
    peers = lax.axis_size(axis)
    pairs = [(i, i + by) for i in range(peers) if 0 <= i + by < peers]
    return lax.ppermute(value, axis, pairs)


def along_x(field):
    return 0.5 * (jnp.roll(field, -1, axis=-1) - jnp.roll(field, 1, axis=-1))


def second_x(field):
    return jnp.roll(field, -1, axis=-1) + jnp.roll(field, 1, axis=-1) - 2.0 * field


def along_y(extended):
    return 0.5 * (extended[..., 2:, :] - extended[..., :-2, :])


def trimmed(field, count):
    if count == 0:
        return field
    return field[..., count : field.shape[-2] - count, :]


def row_valid(lat_rows):
    first_row = lax.axis_index("space") * lat_rows - 4
    row_total = lat_rows * lax.axis_size("space")
    global_rows = first_row + jnp.arange(lat_rows + 8, dtype=jnp.int32)
    inside = jnp.logical_and(global_rows >= 0, global_rows < row_total)
    return inside.astype(jnp.float32)[:, None]


def tangent_core(state, margin, coefs):
    speed_col, couple_col, winds, have, valid = coefs
    height, east, north, tracer = (state[:, 0], state[:, 1], state[:, 2], state[:, 3])
    east_mid = east - speed_col * along_x(height)
    north_mid = (trimmed(north, 1) - speed_col * along_y(height)) * trimmed(valid, 5 - margin)
    height_new = trimmed(height, 2) - speed_col * (
        along_x(trimmed(east_mid, 2)) + along_y(north_mid)
    )
    tracer_one = trimmed(tracer, 1)
    inner = trimmed(tracer, 2)
    tracer_lap = second_x(inner) + tracer_one[..., 2:, :] + tracer_one[..., :-2, :] - 2.0 * inner
    wind_east = trimmed(winds[0], have - margin + 2)
    wind_north = trimmed(winds[1], have - margin + 2)
    tracer_new = (
        inner
        - wind_east * along_x(inner)
        - wind_north * along_y(tracer_one)
        + diffusion * tracer_lap
        + couple_col * height_new
    )
    result = jnp.stack(
        [height_new, trimmed(east_mid, 2), trimmed(north_mid, 1), tracer_new], axis=1
    )
    return result * trimmed(valid, 6 - margin)


def adjoint_core(state, margin, coefs):
    speed_col, couple_col, winds, have, valid = coefs
    height, east, north, tracer = (state[:, 0], state[:, 1], state[:, 2], state[:, 3])
    height_mix = height + couple_col * tracer
    east_mid = east + speed_col * along_x(height_mix)
    north_mid = (trimmed(north, 1) + speed_col * along_y(height_mix)) * trimmed(valid, 5 - margin)
    height_new = trimmed(height_mix, 2) + speed_col * (
        along_x(trimmed(east_mid, 2)) + along_y(north_mid)
    )
    tracer_one = trimmed(tracer, 1)
    inner = trimmed(tracer, 2)
    tracer_lap = second_x(inner) + tracer_one[..., 2:, :] + tracer_one[..., :-2, :] - 2.0 * inner
    wind_east = trimmed(winds[0], have - margin + 2)
    wind_north = trimmed(winds[1], have - margin + 1)
    tracer_new = (
        inner
        + along_x(wind_east * inner)
        + along_y(wind_north * tracer_one)
        + diffusion * tracer_lap
    )
    result = jnp.stack(
        [height_new, trimmed(east_mid, 2), trimmed(north_mid, 1), tracer_new], axis=1
    )
    return result * trimmed(valid, 6 - margin)


def rebuild(state, sent):
    widths = [(0, 0)] * (state.ndim - 3) + [(2, 2), (0, 0)]
    east_wide = jnp.pad(state[:, 1], widths)
    return jnp.stack([sent[:, 0], east_wide, sent[:, 1], sent[:, 2]], axis=1)


def tangent_near(state):
    picked = jnp.stack([state[:, 0], state[:, 2], state[:, 3]], axis=1)
    sent = extended_2(picked, (("space", 3),), 2)
    return rebuild(state, sent)


def adjoint_near(state):
    picked = jnp.stack([state[:, 0], state[:, 2], state[:, 3]], axis=1)
    sent = extended_2(picked, (("space", 3),), 2)
    return rebuild(state, sent)


def propagate(fields, step_core, near_fn, coefs):
    current = fields
    for step in range(STEPS):
        current = step_core(near_fn(current), 2, coefs)
    return current


def operate(direction, error_precision, observed, coefs):
    moved = propagate(direction, tangent_core, tangent_near, coefs)
    incoming = shifted(moved, "tm", 1)
    previous = jnp.concatenate([incoming, moved[:-1]], axis=0)
    weighted = error_precision * (direction - previous)
    back = propagate(weighted, adjoint_core, adjoint_near, coefs)
    arriving = shifted(back, "tm", -1)
    following = jnp.concatenate([back[1:], arriving], axis=0)
    return weighted - following + observed * direction


def squares(residual):
    return lax.psum(jnp.sum(residual * residual), ("space", "tm"))


def on_device(right_side, error_precision, obs_count, background_wind, wave_speed, tracer_coupling):
    lat_rows = right_side.shape[3]
    valid = row_valid(lat_rows)
    winds = extended_2(background_wind, (("space", 2),), 1)
    have = 1
    coefs = (wave_speed[:, None, None], tracer_coupling[:, None, None], winds, have, valid)
    observed = obs_count.astype(jnp.float32)
    solution_field = jnp.zeros_like(right_side)
    residual = right_side
    direction = right_side
    norm_now = squares(residual)
    for step in range(ITERS):
        image = operate(direction, error_precision, observed, coefs)
        alpha = norm_now / lax.psum(jnp.sum(direction * image), ("space", "tm"))
        solution_field = solution_field + alpha * direction
        residual = residual - alpha * image
        norm_next = squares(residual)
        direction = residual + norm_next / norm_now * direction
        norm_now = norm_next
    return (solution_field, residual)


def solution(mesh):
    def run(right_side, *others):
        body = by_layer if fits_by_layer(mesh, right_side.shape) else on_device
        return jax.shard_map(
            body,
            mesh=mesh,
            in_specs=(
                P(("ens", "tm"), None, None, "space", None),
                P("tm", None, None, "space", None),
                P("tm", None, None, "space", None),
                P(None, None, "space", None),
                P(),
                P(),
            ),
            out_specs=(
                P(("ens", "tm"), None, None, "space", None),
                P(("ens", "tm"), None, None, "space", None),
            ),
            check_vma=False,
        )(right_side, *others)

    return run
```

```python
import jax
import jax.numpy as jnp
from jax import lax
from jax.experimental import pallas as pl
from jax.experimental.pallas import tpu as pltpu
from jax.sharding import PartitionSpec as P

STEPS = 2
ITERS = 2


diffusion = 0.1


LANES = 128
ROWS = 8
TILES = 3
REACH = 4
FIELDS = 4
SLOT = 2 * REACH
WINDS = LANES - FIELDS * SLOT
FREE = 6 * REACH
MIXED = 2 * FIELDS * TILES
ROWS_IN = MIXED + 1
THIRDS = 4 * FIELDS
ROWS_OUT = THIRDS + 2 * FIELDS - 1


def merge_lanes(lon):
    core = lon // 2
    return (core + 3 * REACH) % LANES, (core - 3 * REACH) % LANES


def pack_kernel(
    lon, merges, b_hbm, e_hbm, o_hbm, w_hbm, speed_hbm, couple_hbm, out_ref, b_row_ref,
    b_ref, e_ref, o_ref, w_ref, speed_ref, couple_ref, s_row_ref, w_row_ref, sems,
):
    _, levels, share, _ = b_ref.shape
    full = lon // LANES
    rest = lon - full * LANES
    member = lax.axis_index("ens")
    turn = lax.axis_index("tm") * 2 + member
    comp = jnp.where(turn < 2 * TILES, turn // TILES, turn - 2 * TILES)

    copy_b = pltpu.make_async_copy(b_hbm, b_ref, sems.at[0])
    copy_e = pltpu.make_async_copy(e_hbm, e_ref, sems.at[1])
    copy_o = pltpu.make_async_copy(o_hbm, o_ref, sems.at[2])
    others = (
        pltpu.make_async_copy(w_hbm.at[comp], w_ref, sems.at[3]),
        pltpu.make_async_copy(speed_hbm, speed_ref, sems.at[4]),
        pltpu.make_async_copy(couple_hbm, couple_ref, sems.at[5]),
    )
    copy_b.start()
    pl.when(member == 0)(copy_e.start)
    pl.when(member != 0)(copy_o.start)
    for copy in others:
        copy.start()
    lane = lax.broadcasted_iota(jnp.int32, (ROWS, LANES), 1)
    row = lax.broadcasted_iota(jnp.int32, (ROWS, LANES), 0)
    group = ROWS // share

    def stage(copy, ref, row_ref):
        copy.wait()
        for f in range(FIELDS):
            for level in range(levels):
                row_ref[f, pl.ds(level * share, share), pl.ds(0, lon)] = ref[f, level].astype(jnp.float32)

    def place(half, g, k):
        return pl.ds((half * levels + g * group) * share * ROWS_IN + k, ROWS, stride=ROWS_IN), slice(None)

    def windows(first, third, last):
        before = pltpu.roll(last, LANES - rest, 1)
        after = jnp.where(lane < rest, last, pltpu.roll(first, rest, 1))
        ends = ((third, before), (after, third))
        merged = [jnp.where(lane < m, x, y) for m, (x, y) in zip(merges, ends)]
        extra = [jnp.where(lane < m, y, x) for m, (x, y) in zip(merges, ends)]
        return merged, extra

    def put(g, k, row_ref, f):
        tiles = [row_ref[f, pl.ds(g * ROWS, ROWS), pl.ds(c * LANES, LANES)] for c in range(full + 1)]
        merged, extra = windows(tiles[0], tiles[2], tiles[5])
        for half in range(2):
            for c, value in enumerate(tiles[TILES * half : TILES * half + 2] + [merged[half]]):
                out_ref[place(half, g, k + c)] = value
        return extra

    def by_level(ref, g):
        value = jnp.full((ROWS, LANES), ref[g * group], jnp.float32)
        for i in range(1, group):
            value = jnp.where(row < i * share, value, ref[g * group + i])
        return value

    stage(copy_b, b_ref, b_row_ref)
    pl.when(member == 0)(lambda: stage(copy_e, e_ref, s_row_ref))
    pl.when(member != 0)(lambda: stage(copy_o, o_ref, s_row_ref))
    for copy in others:
        copy.wait()
    for level in range(levels):
        w_row_ref[pl.ds(level * share, share), pl.ds(0, lon)] = w_ref[level]
    for g in range(levels // group):
        mixed = [None, None]
        for f in range(FIELDS):
            extra = put(g, f * TILES, b_row_ref, f)
            for half, m in enumerate(merges):
                at = WINDS + f * SLOT
                moved = pltpu.roll(extra[half], (at - (m - REACH)) % LANES, 1)
                mixed[half] = moved if f == 0 else jnp.where(lane < at, mixed[half], moved)
        tiles = [w_row_ref[pl.ds(g * ROWS, ROWS), pl.ds(c * LANES, LANES)] for c in range(full + 1)]
        merged, extra = windows(tiles[0], tiles[2], tiles[5])
        speed, couple = by_level(speed_ref, g), by_level(couple_ref, g)
        for half, m in enumerate(merges):
            parts = tiles[TILES * half : TILES * half + 2] + [merged[half]]
            wind, left = parts[TILES - 1], pltpu.roll(parts[TILES - 1], LANES - SLOT * FIELDS, 1)
            for c in reversed(range(TILES - 1)):
                wind = jnp.where(jnp.logical_or(turn == c, turn == TILES + c), parts[c], wind)
                by = (c + 1) * SLOT * FIELDS
                left = jnp.where(lane < by, pltpu.roll(parts[c], by, 1), left)
            wind = jnp.where(turn < 2 * TILES, wind, left)
            value = jnp.where(lane < WINDS, wind, mixed[half])
            value = jnp.where(lane == WINDS + SLOT, speed, value)
            value = jnp.where(lane == WINDS + 2 * SLOT - 1, couple, value)
            ends = pltpu.roll(extra[half], LANES - 1 - m, 1)
            value = jnp.where(lane >= LANES - 2, ends, value)
            out_ref[place(half, g, MIXED)] = value

    for g in range(levels // group):
        for f in range(FIELDS):
            put(g, (FIELDS + f) * TILES, s_row_ref, f)


def layer_kernel(lon, merges, subwins, in_ref, out_ref):
    half = lax.axis_index("ens")
    lane = lax.broadcasted_iota(jnp.int32, (ROWS, LANES), 1)
    row = lax.broadcasted_iota(jnp.int32, (ROWS, LANES), 0)
    below = lane < jnp.where(half == 0, merges[0], merges[1])
    free_lo = jnp.where(half == 0, merges[0] - 3 * REACH, merges[1] - 3 * REACH)
    free = jnp.logical_and(lane >= free_lo, lane < free_lo + FREE)

    def load(member, t, k):
        return in_ref[pl.ds((member * subwins + t) * ROWS * ROWS_IN + k, ROWS, stride=ROWS_IN), :]

    def of_half(values):
        return jnp.where(half == 0, values[0] % LANES, values[1] % LANES)

    mixed = [[load(member, t, MIXED) for t in range(subwins)] for member in range(2)]
    speed_at, couple_at = WINDS + SLOT, WINDS + 2 * SLOT - 1
    speed = 0.5 * jnp.broadcast_to(mixed[0][0][:, speed_at : speed_at + 1], (ROWS, LANES))
    couple = jnp.broadcast_to(mixed[0][0][:, couple_at : couple_at + 1], (ROWS, LANES))

    def back(x, by):
        moved = [pltpu.roll(v, by, 1) for v in x]
        return [jnp.where(lane < by, moved[i - 1], v) for i, v in enumerate(moved)]

    def ahead(x, by):
        moved = [pltpu.roll(v, LANES - by, 1) for v in x]
        return [jnp.where(lane >= LANES - by, moved[(i + 1) % len(x)], v) for i, v in enumerate(moved)]

    def up(x, by):
        return [pltpu.roll(v, ROWS - by, 0) for v in x]

    def down(x, by):
        return [pltpu.roll(v, by, 0) for v in x]

    def staggered(f, x):
        if f == 1:
            return ahead(x, 1)
        if f == 2:
            return up(x, 1)
        return x

    def aligned(f, x):
        if f == 1:
            return back(x, 1)
        if f == 2:
            return down(x, 1)
        return x

    def widened(x, extra):
        return x[:2] + [jnp.where(below, x[2], extra), jnp.where(below, extra, x[2])]

    def narrowed(x):
        return x[:2] + [jnp.where(below, x[2], x[3])]

    def fields_of(member, t, at):
        return [[load(member, t, (at + f) * TILES + c) for c in range(TILES)] for f in range(FIELDS)]

    def extras_of(member, t):
        shifts = [of_half([m - REACH - WINDS - f * SLOT for m in merges]) for f in range(FIELDS)]
        return [pltpu.roll(mixed[member][t], by, 1) for by in shifts]

    def stag(state):
        return [staggered(f, x) for f, x in enumerate(state)]

    def wind(comp):
        sent = [mixed[turn % 2][turn // 2] for turn in range(2 * subwins)]
        left = sent[2 * TILES + comp]
        tiles = []
        for c in range(TILES):
            by = WINDS - c * SLOT * FIELDS
            tiles.append(jnp.where(lane < WINDS, sent[comp * TILES + c], pltpu.roll(left, by, 1)))
        return tiles, pltpu.roll(sent[comp * TILES], of_half([m + 1 - LANES for m in merges]), 1)

    stay = 1.0 - 4.0 * diffusion
    grad_p = jnp.where(row == ROWS - 2, 0.0, speed)
    grad_m = jnp.where(row == ROWS - 1, 0.0, speed)
    before_p = jnp.where(row == 0, 0.0, speed)
    before_m = jnp.where(row == 1, 0.0, speed)
    div_p = jnp.where(row == ROWS - 1, 0.0, speed)
    div_m = jnp.where(row == 0, 0.0, speed)

    def coefficients(east, north):
        return (
            [diffusion - 0.5 * v for v in east],
            [diffusion + 0.5 * v for v in east],
            [jnp.where(row == ROWS - 1, 0.0, diffusion - 0.5 * v) for v in north],
            [jnp.where(row == 0, 0.0, diffusion + 0.5 * v) for v in north],
        )

    (east, east_extra), (north, north_extra) = wind(0), wind(1)
    narrow = coefficients(east, north)
    wide = coefficients(widened(east, east_extra), widened(north, north_extra))

    here = 2.0 * speed * speed + (div_p * grad_m + div_m * before_p)
    along, north_of, south_of = speed * speed, div_p * grad_p, div_m * before_m

    def divergence(u, v):
        return [
            speed * (a - b) + (div_p * c - div_m * d) for a, b, c, d in zip(u, back(u, 2), v, down(v, 2))
        ]

    def spread(h):
        ahead_h, up_h = ahead(h, 2), up(h, 2)
        change = [
            (along * (n + m) + (north_of * p + south_of * q)) - here * a
            for a, n, m, p, q in zip(h, ahead_h, back(h, 2), up_h, down(h, 2))
        ]
        return change, ahead_h, up_h

    def gradients(h, ahead_h, up_h):
        east = [speed * (n - m) for n, m in zip(ahead_h, h)]
        north = [grad_p * n - grad_m * m for n, m in zip(up_h, h)]
        return east, north

    def tangent(state, coefs):
        h, u, v, q = state
        flow = divergence(u, v)
        for _ in range(STEPS):
            change, ahead_h, up_h = spread(h)
            east, north = gradients(h, ahead_h, up_h)
            u, v = [a - b for a, b in zip(u, east)], [a - b for a, b in zip(v, north)]
            flow = [a - b for a, b in zip(flow, change)]
            h = [a - b for a, b in zip(h, flow)]
            q = [
                stay * a + (em * e + ep * w) + (nm * n + np * s) + couple * p
                for a, em, e, ep, w, nm, n, np, s, p in zip(
                    q, coefs[0], ahead(q, 1), coefs[1], back(q, 1), coefs[2], up(q, 1), coefs[3], down(q, 1), h
                )
            ]
        return [h, u, v, q]

    def adjoint(state, coefs):
        h, u, v, q = state
        flow = divergence(u, v)
        for _ in range(STEPS):
            h = [a + couple * b for a, b in zip(h, q)]
            change, ahead_h, up_h = spread(h)
            east, north = gradients(h, ahead_h, up_h)
            u, v = [a + b for a, b in zip(u, east)], [a + b for a, b in zip(v, north)]
            flow = [a + b for a, b in zip(flow, change)]
            h = [a + b for a, b in zip(h, flow)]
            e = ahead([a * b for a, b in zip(coefs[1], q)], 1)
            w = back([a * b for a, b in zip(coefs[0], q)], 1)
            n = up([a * b for a, b in zip(coefs[3], q)], 1)
            s = down([a * b for a, b in zip(coefs[2], q)], 1)
            q = [stay * a + (b + c) + (d + f) for a, b, c, d, f in zip(q, e, w, n, s)]
        return [h, u, v, q]

    def each(fn, *states):
        return [[fn(*vals) for vals in zip(*xs)] for xs in zip(*states)]

    def operate(p, p_wide, precision, observed):
        weighted = []
        for t in range(subwins):
            change = p[t]
            if t > 0:
                moved = tangent(p[t - 1], narrow) if p_wide is None else tangent(p_wide[t - 1], wide)
                if p_wide is not None:
                    moved = [narrowed(x) for x in moved]
                change = each(lambda a, b: a - b, change, moved)
            weighted.append(each(lambda a, b: a * b, precision[t], change))
        image = []
        for t in range(subwins):
            out = each(lambda w, o, d: w + o * d, weighted[t], observed[t], p[t])
            if t + 1 < subwins:
                moved = adjoint(weighted[t + 1], narrow)
                out = each(lambda a, b: a - b, out, moved)
            image.append(out)
        return image

    def flat(x):
        return [(c, v) for state in x for field in state for c, v in enumerate(field)]

    def total(terms):
        inner, edge = None, None
        for c, v in terms:
            if c < TILES - 1:
                inner = v if inner is None else inner + v
            else:
                edge = v if edge is None else edge + v
        both = inner + jnp.where(free, 0.0, edge)
        return jnp.sum(both, axis=(0, 1), keepdims=True)

    def dot(x, y):
        return total([(c, v * w) for (c, v), (_, w) in zip(x, y)])

    precision = [stag(fields_of(0, t, FIELDS)) for t in range(subwins)]
    observed = [stag(fields_of(1, t, FIELDS)) for t in range(subwins)]
    for member in range(2):
        plain = [fields_of(member, t, 0) for t in range(subwins)]
        b_wide = [
            stag([widened(x, e) for x, e in zip(plain[t], extras_of(member, t))]) for t in range(subwins - 1)
        ]
        b = [[narrowed(x) for x in state] for state in b_wide] + [stag(plain[-1])]
        one = operate(b, b_wide, precision, observed)
        two = operate(one, None, precision, observed)
        one, two = [[[aligned(f, x) for f, x in enumerate(state)] for state in y] for y in (one, two)]
        f0, f1, f2 = flat(plain), flat(one), flat(two)
        s00, s01, s11, s02, s12 = dot(f0, f0), dot(f0, f1), dot(f1, f1), dot(f0, f2), dot(f1, f2)
        step = jnp.where(s11 > 0.0, s01 / jnp.where(s11 > 0.0, s11, 1.0), 0.0)
        more = 2.0 - jnp.where(s00 > 0.0, step * s01 / jnp.where(s00 > 0.0, s00, 1.0), 0.0)
        step_t = jnp.broadcast_to(step, (ROWS, LANES))
        more_t = jnp.broadcast_to(more, (ROWS, LANES))
        res = [(c, v - step_t * w) for (c, v), (_, w) in zip(f0, f1)]
        mov = [(c, more_t * v - step_t * w) for (c, v), (_, w) in zip(f0, f1)]
        img = [(c, more_t * v - step_t * w) for (c, v), (_, w) in zip(f1, f2)]
        sums = [step, more, s00, s01, s11, s02, s12, dot(res, res), dot(mov, img)]
        sums += [sums[-1]] * (-len(sums) % 6)
        for t in range(subwins):

            def put(k, value):
                start = (member * subwins + t) * ROWS * ROWS_OUT + k
                out_ref[pl.ds(start, ROWS, stride=ROWS_OUT), :] = value

            images = one[t] + two[t]
            last = images[-1][TILES - 1]
            for k, x in enumerate(images):
                put(2 * k, x[0])
                put(2 * k + 1, x[1])
                if k < 5:
                    put(THIRDS + k, jnp.where(free, pltpu.roll(last, (-(k + 1) * FREE) % LANES, 1), x[2]))
                elif k < 2 * FIELDS - 1:
                    rows = []
                    for i in (k - 5, k - 3):
                        value = sums[3 * i + 2]
                        for j in (1, 0):
                            value = jnp.where(lane < free_lo + (j + 1) * SLOT, sums[3 * i + j], value)
                        rows.append(value)
                    put(THIRDS + k, jnp.where(free, jnp.where(row % 2 == 0, rows[0], rows[1]), x[2]))


def finish_kernel(lon, merges, b_row_ref, in_ref, x_hbm, r_hbm, x_ref, r_ref, x_row_ref, r_row_ref, sems):
    _, levels, share, _ = x_ref.shape
    full = lon // LANES
    rest = lon - full * LANES
    size = share * ROWS_OUT
    apart = merges[0] - merges[1]
    at_lane = merges[0] - 3 * REACH
    group = ROWS // share

    slots = []
    for i in range(3):
        at = THIRDS + 5 + i % 2 + (i // 2) * ROWS_OUT
        halves = [in_ref[pl.ds(half * levels * size + at, levels, stride=size), :] for half in range(2)]
        slots.append(jnp.concatenate([halves[0], pltpu.roll(halves[1], apart, 1)], axis=0))

    def sums(i):
        value = slots[i // 3]
        return pltpu.roll(value, LANES - (i % 3) * SLOT, 1) if i % 3 else value

    step, more, s00, s01, s11, s02, s12, rr, mi = [sums(i) for i in range(9)]

    def total(x):
        return jnp.sum(x, axis=0, keepdims=True)

    norm_0 = total(s00)
    alpha_0 = norm_0 / total(s01)
    d = step - alpha_0
    norm_1 = total(rr + d * (2.0 * (s01 - step * s11) + d * s11))
    beta = norm_1 / norm_0
    g = (1.0 + beta) - more
    cross_d = more * (s02 + s11) - 2.0 * step * s12
    cross_g = 2.0 * more * s01 - step * (s11 + s02)
    curve = total(mi + d * (cross_d + d * s12 + g * (s11 + s02)) + g * (cross_g + g * s01))
    alpha_1 = norm_1 / curve
    first = alpha_0 + alpha_1 * (1.0 + beta)
    second = alpha_0 * alpha_1
    first = jnp.broadcast_to(first[:, at_lane : at_lane + 1], (ROWS, LANES))
    second = jnp.broadcast_to(second[:, at_lane : at_lane + 1], (ROWS, LANES))
    lane = lax.broadcasted_iota(jnp.int32, (ROWS, LANES), 1)

    def tiles_of(g, k):
        halves = []
        for half in range(2):
            start = (half * levels + g * group) * size

            def rows(j):
                return in_ref[pl.ds(start + j, ROWS, stride=ROWS_OUT), :]

            if k < 2 * FIELDS - 1:
                third = rows(THIRDS + k)
            else:
                third = None
                for i in range(5):
                    part = pltpu.roll(rows(THIRDS + i), (i + 1) * FREE % LANES, 1)
                    begin = (merges[half] - 3 * REACH + (i + 1) * FREE) % LANES
                    here = jnp.logical_and(lane >= begin, lane < begin + FREE)
                    third = part if third is None else jnp.where(here, part, third)
            halves.append([rows(2 * k), rows(2 * k + 1), third])
        middle = jnp.where(lane < at_lane, halves[0][2], halves[1][2])
        return halves[0][:2] + [middle] + halves[1]

    copies = []
    for f in range(FIELDS):
        for g in range(levels // group):
            for c, (one, two) in enumerate(zip(tiles_of(g, f), tiles_of(g, FIELDS + f))):
                at = f, pl.ds(g * ROWS, ROWS), pl.ds(c * LANES, LANES)
                b = b_row_ref[at]
                x_row_ref[at] = first * b - second * one
                r_row_ref[at] = b + (second * two - first * one)
            for level in range(g * group, (g + 1) * group):
                at = f, pl.ds(level * share, share), pl.ds(0, lon)
                x_ref[f, level] = x_row_ref[at]
                r_ref[f, level] = r_row_ref[at]
        for i, (src, dst) in enumerate(((x_ref, x_hbm), (r_ref, r_hbm))):
            copies.append(pltpu.make_async_copy(src.at[f], dst.at[f], sems.at[i, f]))
            copies[-1].start()
    for copy in copies:
        copy.wait()


def by_layer(right_side, error_precision, obs_count, background_wind, wave_speed, tracer_coupling):
    _, fields, levels, share, lon = right_side.shape
    subwins = lax.axis_size("tm")
    merges = merge_lanes(lon)
    vmem = pl.BlockSpec(memory_space=pltpu.VMEM)
    hbm = pl.BlockSpec(memory_space=pltpu.HBM)
    params = pltpu.CompilerParams(vmem_limit_bytes=48 * 1024 * 1024)
    state = (fields, levels, share, lon)
    wide = (lon // LANES + 1) * LANES

    def exchange(x):
        x = x.reshape(2 * levels, -1, 1, LANES)
        return lax.all_to_all(x, ("ens", "tm", "space"), 0, 0, tiled=True).reshape(-1, LANES)

    b = right_side.reshape(state)
    given = (b, error_precision.reshape(state), obs_count.reshape(state), background_wind, wave_speed, tracer_coupling)
    with jax.named_scope("pack"):
        packed, b_rows = pl.pallas_call(
            lambda *refs: pack_kernel(lon, merges, *refs),
            out_shape=[
                jax.ShapeDtypeStruct((2 * levels * share * ROWS_IN, LANES), jnp.float32),
                jax.ShapeDtypeStruct((fields, levels * share, wide), jnp.float32),
            ],
            in_specs=[hbm] * len(given),
            out_specs=[vmem] * 2,
            scratch_shapes=[
                pltpu.VMEM(state, jnp.float32),
                pltpu.VMEM(state, jnp.float32),
                pltpu.VMEM(state, jnp.int32),
                pltpu.VMEM(background_wind.shape[1:], jnp.float32),
                pltpu.SMEM(wave_speed.shape, jnp.float32),
                pltpu.SMEM(tracer_coupling.shape, jnp.float32),
                pltpu.VMEM((fields, levels * share, wide), jnp.float32),
                pltpu.VMEM((levels * share, wide), jnp.float32),
                pltpu.SemaphoreType.DMA((len(given),)),
            ],
            compiler_params=params,
        )(*[pltpu.with_memory_space_constraint(x, pltpu.HBM) for x in given])
    packed = exchange(packed)
    with jax.named_scope("layer"):
        images = pl.pallas_call(
            lambda *refs: layer_kernel(lon, merges, subwins, *refs),
            out_shape=jax.ShapeDtypeStruct((2 * levels * share * ROWS_OUT, LANES), jnp.float32),
            in_specs=[vmem],
            out_specs=vmem,
            compiler_params=params,
        )(packed)
    images = exchange(images)
    with jax.named_scope("finish"):
        x, r = pl.pallas_call(
            lambda *refs: finish_kernel(lon, merges, *refs),
            out_shape=[jax.ShapeDtypeStruct(state, jnp.float32)] * 2,
            in_specs=[vmem] * 2,
            out_specs=[hbm] * 2,
            scratch_shapes=[
                pltpu.VMEM(state, jnp.float32),
                pltpu.VMEM(state, jnp.float32),
                pltpu.VMEM((fields, levels * share, wide), jnp.float32),
                pltpu.VMEM((fields, levels * share, wide), jnp.float32),
                pltpu.SemaphoreType.DMA((2, FIELDS)),
            ],
            compiler_params=params,
        )(b_rows, images)
    return x.reshape(right_side.shape), r.reshape(right_side.shape)


def fits_by_layer(mesh, shape):
    space, tm, ens = mesh.shape["space"], mesh.shape["tm"], mesh.shape["ens"]
    subwins, fields, levels, lats, lon = shape
    return (
        (ens, tm, space, fields, lats) == (2, 4, 4, FIELDS, ROWS)
        and subwins == ens * tm
        and levels == space * tm
        and lon == 720
    )


def extended_2(cells, sides, width):
    for axis, dim in sides:
        count = lax.axis_size(axis)
        ends = count - 1
        head = lax.slice_in_dim(cells, 0, width, axis=dim)
        tail = lax.slice_in_dim(cells, cells.shape[dim] - width, cells.shape[dim], axis=dim)
        cells = jnp.concatenate(
            [
                lax.ppermute(tail, axis, [(i, (i + 1) % count) for i in range(ends)]),
                cells,
                lax.ppermute(head, axis, [((i + 1) % count, i) for i in range(ends)]),
            ],
            axis=dim,
        )
    return cells


def shifted(value, axis, by):
    peers = lax.axis_size(axis)
    pairs = [(i, i + by) for i in range(peers) if 0 <= i + by < peers]
    return lax.ppermute(value, axis, pairs)


def along_x(field):
    return 0.5 * (jnp.roll(field, -1, axis=-1) - jnp.roll(field, 1, axis=-1))


def second_x(field):
    return jnp.roll(field, -1, axis=-1) + jnp.roll(field, 1, axis=-1) - 2.0 * field


def along_y(extended):
    return 0.5 * (extended[..., 2:, :] - extended[..., :-2, :])


def trimmed(field, count):
    if count == 0:
        return field
    return field[..., count : field.shape[-2] - count, :]


def row_valid(lat_rows):
    first_row = lax.axis_index("space") * lat_rows - 4
    row_total = lat_rows * lax.axis_size("space")
    global_rows = first_row + jnp.arange(lat_rows + 8, dtype=jnp.int32)
    inside = jnp.logical_and(global_rows >= 0, global_rows < row_total)
    return inside.astype(jnp.float32)[:, None]


def tangent_core(state, margin, coefs):
    speed_col, couple_col, winds, have, valid = coefs
    height, east, north, tracer = (state[:, 0], state[:, 1], state[:, 2], state[:, 3])
    east_mid = east - speed_col * along_x(height)
    north_mid = (trimmed(north, 1) - speed_col * along_y(height)) * trimmed(valid, 5 - margin)
    height_new = trimmed(height, 2) - speed_col * (
        along_x(trimmed(east_mid, 2)) + along_y(north_mid)
    )
    tracer_one = trimmed(tracer, 1)
    inner = trimmed(tracer, 2)
    tracer_lap = second_x(inner) + tracer_one[..., 2:, :] + tracer_one[..., :-2, :] - 2.0 * inner
    wind_east = trimmed(winds[0], have - margin + 2)
    wind_north = trimmed(winds[1], have - margin + 2)
    tracer_new = (
        inner
        - wind_east * along_x(inner)
        - wind_north * along_y(tracer_one)
        + diffusion * tracer_lap
        + couple_col * height_new
    )
    result = jnp.stack(
        [height_new, trimmed(east_mid, 2), trimmed(north_mid, 1), tracer_new], axis=1
    )
    return result * trimmed(valid, 6 - margin)


def adjoint_core(state, margin, coefs):
    speed_col, couple_col, winds, have, valid = coefs
    height, east, north, tracer = (state[:, 0], state[:, 1], state[:, 2], state[:, 3])
    height_mix = height + couple_col * tracer
    east_mid = east + speed_col * along_x(height_mix)
    north_mid = (trimmed(north, 1) + speed_col * along_y(height_mix)) * trimmed(valid, 5 - margin)
    height_new = trimmed(height_mix, 2) + speed_col * (
        along_x(trimmed(east_mid, 2)) + along_y(north_mid)
    )
    tracer_one = trimmed(tracer, 1)
    inner = trimmed(tracer, 2)
    tracer_lap = second_x(inner) + tracer_one[..., 2:, :] + tracer_one[..., :-2, :] - 2.0 * inner
    wind_east = trimmed(winds[0], have - margin + 2)
    wind_north = trimmed(winds[1], have - margin + 1)
    tracer_new = (
        inner
        + along_x(wind_east * inner)
        + along_y(wind_north * tracer_one)
        + diffusion * tracer_lap
    )
    result = jnp.stack(
        [height_new, trimmed(east_mid, 2), trimmed(north_mid, 1), tracer_new], axis=1
    )
    return result * trimmed(valid, 6 - margin)


def rebuild(state, sent):
    widths = [(0, 0)] * (state.ndim - 3) + [(2, 2), (0, 0)]
    east_wide = jnp.pad(state[:, 1], widths)
    return jnp.stack([sent[:, 0], east_wide, sent[:, 1], sent[:, 2]], axis=1)


def tangent_near(state):
    picked = jnp.stack([state[:, 0], state[:, 2], state[:, 3]], axis=1)
    sent = extended_2(picked, (("space", 3),), 2)
    return rebuild(state, sent)


def adjoint_near(state):
    picked = jnp.stack([state[:, 0], state[:, 2], state[:, 3]], axis=1)
    sent = extended_2(picked, (("space", 3),), 2)
    return rebuild(state, sent)


def propagate(fields, step_core, near_fn, coefs):
    current = fields
    for step in range(STEPS):
        current = step_core(near_fn(current), 2, coefs)
    return current


def operate(direction, error_precision, observed, coefs):
    moved = propagate(direction, tangent_core, tangent_near, coefs)
    incoming = shifted(moved, "tm", 1)
    previous = jnp.concatenate([incoming, moved[:-1]], axis=0)
    weighted = error_precision * (direction - previous)
    back = propagate(weighted, adjoint_core, adjoint_near, coefs)
    arriving = shifted(back, "tm", -1)
    following = jnp.concatenate([back[1:], arriving], axis=0)
    return weighted - following + observed * direction


def squares(residual):
    return lax.psum(jnp.sum(residual * residual), ("space", "tm"))


def on_device(right_side, error_precision, obs_count, background_wind, wave_speed, tracer_coupling):
    lat_rows = right_side.shape[3]
    valid = row_valid(lat_rows)
    winds = extended_2(background_wind, (("space", 2),), 1)
    have = 1
    coefs = (wave_speed[:, None, None], tracer_coupling[:, None, None], winds, have, valid)
    observed = obs_count.astype(jnp.float32)
    solution_field = jnp.zeros_like(right_side)
    residual = right_side
    direction = right_side
    norm_now = squares(residual)
    for step in range(ITERS):
        image = operate(direction, error_precision, observed, coefs)
        alpha = norm_now / lax.psum(jnp.sum(direction * image), ("space", "tm"))
        solution_field = solution_field + alpha * direction
        residual = residual - alpha * image
        norm_next = squares(residual)
        direction = residual + norm_next / norm_now * direction
        norm_now = norm_next
    return (solution_field, residual)


def solution(mesh):
    def run(right_side, *others):
        body = by_layer if fits_by_layer(mesh, right_side.shape) else on_device
        return jax.shard_map(
            body,
            mesh=mesh,
            in_specs=(
                P(("ens", "tm"), None, None, "space", None),
                P("tm", None, None, "space", None),
                P("tm", None, None, "space", None),
                P(None, None, "space", None),
                P(),
                P(),
            ),
            out_specs=(
                P(("ens", "tm"), None, None, "space", None),
                P(("ens", "tm"), None, None, "space", None),
            ),
            check_vma=False,
        )(right_side, *others)

    return run
```

```python
import jax
import jax.numpy as jnp
from jax import lax
from jax.experimental import pallas as pl
from jax.experimental.pallas import tpu as pltpu
from jax.sharding import PartitionSpec as P

STEPS = 2
ITERS = 2


diffusion = 0.1


LANES = 128
ROWS = 8
TILES = 3
REACH = 4
FIELDS = 4
SLOT = 2 * REACH
WINDS = LANES - FIELDS * SLOT
FREE = 6 * REACH
MIXED = 2 * FIELDS * TILES
ROWS_IN = MIXED + 1
THIRDS = 4 * FIELDS
ROWS_OUT = THIRDS + 2 * FIELDS - 1


def merge_lanes(lon):
    core = lon // 2
    return (core + 3 * REACH) % LANES, (core - 3 * REACH) % LANES


def pack_kernel(
    lon, merges, b_hbm, e_hbm, o_hbm, w_hbm, speed_hbm, couple_hbm, out_ref, b_row_ref,
    b_ref, e_ref, o_ref, w_ref, speed_ref, couple_ref, s_row_ref, w_row_ref, sems,
):
    _, levels, share, _ = b_ref.shape
    full = lon // LANES
    rest = lon - full * LANES
    member = lax.axis_index("ens")
    turn = lax.axis_index("tm") * 2 + member
    comp = jnp.where(turn < 2 * TILES, turn // TILES, turn - 2 * TILES)

    copy_b = pltpu.make_async_copy(b_hbm, b_ref, sems.at[0])
    copy_e = pltpu.make_async_copy(e_hbm, e_ref, sems.at[1])
    copy_o = pltpu.make_async_copy(o_hbm, o_ref, sems.at[2])
    others = (
        pltpu.make_async_copy(w_hbm.at[comp], w_ref, sems.at[3]),
        pltpu.make_async_copy(speed_hbm, speed_ref, sems.at[4]),
        pltpu.make_async_copy(couple_hbm, couple_ref, sems.at[5]),
    )
    copy_b.start()
    pl.when(member == 0)(copy_e.start)
    pl.when(member != 0)(copy_o.start)
    for copy in others:
        copy.start()
    lane = lax.broadcasted_iota(jnp.int32, (ROWS, LANES), 1)
    row = lax.broadcasted_iota(jnp.int32, (ROWS, LANES), 0)
    group = ROWS // share

    def stage(copy, ref, row_ref):
        copy.wait()
        for f in range(FIELDS):
            for level in range(levels):
                row_ref[f, pl.ds(level * share, share), pl.ds(0, lon)] = ref[f, level].astype(jnp.float32)

    def place(half, g, k):
        return pl.ds((half * levels + g * group) * share * ROWS_IN + k, ROWS, stride=ROWS_IN), slice(None)

    def windows(first, third, last):
        before = pltpu.roll(last, LANES - rest, 1)
        after = jnp.where(lane < rest, last, pltpu.roll(first, rest, 1))
        ends = ((third, before), (after, third))
        merged = [jnp.where(lane < m, x, y) for m, (x, y) in zip(merges, ends)]
        extra = [jnp.where(lane < m, y, x) for m, (x, y) in zip(merges, ends)]
        return merged, extra

    def put(g, k, row_ref, f):
        tiles = [row_ref[f, pl.ds(g * ROWS, ROWS), pl.ds(c * LANES, LANES)] for c in range(full + 1)]
        merged, extra = windows(tiles[0], tiles[2], tiles[5])
        for half in range(2):
            for c, value in enumerate(tiles[TILES * half : TILES * half + 2] + [merged[half]]):
                out_ref[place(half, g, k + c)] = value
        return extra

    def by_level(ref, g):
        value = jnp.full((ROWS, LANES), ref[g * group], jnp.float32)
        for i in range(1, group):
            value = jnp.where(row < i * share, value, ref[g * group + i])
        return value

    stage(copy_b, b_ref, b_row_ref)
    pl.when(member == 0)(lambda: stage(copy_e, e_ref, s_row_ref))
    pl.when(member != 0)(lambda: stage(copy_o, o_ref, s_row_ref))
    for copy in others:
        copy.wait()
    for level in range(levels):
        w_row_ref[pl.ds(level * share, share), pl.ds(0, lon)] = w_ref[level]
    for g in range(levels // group):
        mixed = [None, None]
        for f in range(FIELDS):
            extra = put(g, f * TILES, b_row_ref, f)
            for half, m in enumerate(merges):
                at = WINDS + f * SLOT
                moved = pltpu.roll(extra[half], (at - (m - REACH)) % LANES, 1)
                mixed[half] = moved if f == 0 else jnp.where(lane < at, mixed[half], moved)
        tiles = [w_row_ref[pl.ds(g * ROWS, ROWS), pl.ds(c * LANES, LANES)] for c in range(full + 1)]
        merged, extra = windows(tiles[0], tiles[2], tiles[5])
        speed, couple = by_level(speed_ref, g), by_level(couple_ref, g)
        for half, m in enumerate(merges):
            parts = tiles[TILES * half : TILES * half + 2] + [merged[half]]
            wind, left = parts[TILES - 1], pltpu.roll(parts[TILES - 1], LANES - SLOT * FIELDS, 1)
            for c in reversed(range(TILES - 1)):
                wind = jnp.where(jnp.logical_or(turn == c, turn == TILES + c), parts[c], wind)
                by = (c + 1) * SLOT * FIELDS
                left = jnp.where(lane < by, pltpu.roll(parts[c], by, 1), left)
            wind = jnp.where(turn < 2 * TILES, wind, left)
            value = jnp.where(lane < WINDS, wind, mixed[half])
            value = jnp.where(lane == WINDS + SLOT, speed, value)
            value = jnp.where(lane == WINDS + 2 * SLOT - 1, couple, value)
            ends = pltpu.roll(extra[half], LANES - 1 - m, 1)
            value = jnp.where(lane >= LANES - 2, ends, value)
            out_ref[place(half, g, MIXED)] = value

    for g in range(levels // group):
        for f in range(FIELDS):
            put(g, (FIELDS + f) * TILES, s_row_ref, f)


def layer_kernel(lon, merges, subwins, in_ref, out_ref):
    half = lax.axis_index("ens")
    lane = lax.broadcasted_iota(jnp.int32, (ROWS, LANES), 1)
    row = lax.broadcasted_iota(jnp.int32, (ROWS, LANES), 0)
    below = lane < jnp.where(half == 0, merges[0], merges[1])
    free_lo = jnp.where(half == 0, merges[0] - 3 * REACH, merges[1] - 3 * REACH)
    free = jnp.logical_and(lane >= free_lo, lane < free_lo + FREE)

    def load(member, t, k):
        return in_ref[pl.ds((member * subwins + t) * ROWS * ROWS_IN + k, ROWS, stride=ROWS_IN), :]

    def of_half(values):
        return jnp.where(half == 0, values[0] % LANES, values[1] % LANES)

    mixed = [[load(member, t, MIXED) for t in range(subwins)] for member in range(2)]
    speed_at, couple_at = WINDS + SLOT, WINDS + 2 * SLOT - 1
    speed = 0.5 * jnp.broadcast_to(mixed[0][0][:, speed_at : speed_at + 1], (ROWS, LANES))
    couple = jnp.broadcast_to(mixed[0][0][:, couple_at : couple_at + 1], (ROWS, LANES))

    def back(x, by):
        moved = [pltpu.roll(v, by, 1) for v in x]
        return [jnp.where(lane < by, moved[i - 1], v) for i, v in enumerate(moved)]

    def ahead(x, by):
        moved = [pltpu.roll(v, LANES - by, 1) for v in x]
        return [jnp.where(lane >= LANES - by, moved[(i + 1) % len(x)], v) for i, v in enumerate(moved)]

    def up(x, by):
        return [pltpu.roll(v, ROWS - by, 0) for v in x]

    def down(x, by):
        return [pltpu.roll(v, by, 0) for v in x]

    def staggered(f, x):
        if f == 1:
            return ahead(x, 1)
        if f == 2:
            return up(x, 1)
        return x

    def aligned(f, x):
        if f == 1:
            return back(x, 1)
        if f == 2:
            return down(x, 1)
        return x

    def widened(x, extra):
        return x[:2] + [jnp.where(below, x[2], extra), jnp.where(below, extra, x[2])]

    def narrowed(x):
        return x[:2] + [jnp.where(below, x[2], x[3])]

    def fields_of(member, t, at):
        return [[load(member, t, (at + f) * TILES + c) for c in range(TILES)] for f in range(FIELDS)]

    def extras_of(member, t):
        shifts = [of_half([m - REACH - WINDS - f * SLOT for m in merges]) for f in range(FIELDS)]
        return [pltpu.roll(mixed[member][t], by, 1) for by in shifts]

    def stag(state):
        return [staggered(f, x) for f, x in enumerate(state)]

    def wind(comp):
        sent = [mixed[turn % 2][turn // 2] for turn in range(2 * subwins)]
        left = sent[2 * TILES + comp]
        tiles = []
        for c in range(TILES):
            by = WINDS - c * SLOT * FIELDS
            tiles.append(jnp.where(lane < WINDS, sent[comp * TILES + c], pltpu.roll(left, by, 1)))
        return tiles, pltpu.roll(sent[comp * TILES], of_half([m + 1 - LANES for m in merges]), 1)

    stay = 1.0 - 4.0 * diffusion
    grad_p = jnp.where(row == ROWS - 2, 0.0, speed)
    grad_m = jnp.where(row == ROWS - 1, 0.0, speed)
    before_p = jnp.where(row == 0, 0.0, speed)
    before_m = jnp.where(row == 1, 0.0, speed)
    div_p = jnp.where(row == ROWS - 1, 0.0, speed)
    div_m = jnp.where(row == 0, 0.0, speed)

    def coefficients(east, north):
        return (
            [diffusion - 0.5 * v for v in east],
            [diffusion + 0.5 * v for v in east],
            [jnp.where(row == ROWS - 1, 0.0, diffusion - 0.5 * v) for v in north],
            [jnp.where(row == 0, 0.0, diffusion + 0.5 * v) for v in north],
        )

    (east, east_extra), (north, north_extra) = wind(0), wind(1)
    narrow = coefficients(east, north)
    wide = coefficients(widened(east, east_extra), widened(north, north_extra))

    here = 2.0 * speed * speed + (div_p * grad_m + div_m * before_p)
    along, north_of, south_of = speed * speed, div_p * grad_p, div_m * before_m

    def divergence(u, v):
        return [
            speed * (a - b) + (div_p * c - div_m * d) for a, b, c, d in zip(u, back(u, 2), v, down(v, 2))
        ]

    def spread(h):
        ahead_h, up_h = ahead(h, 2), up(h, 2)
        change = [
            (along * (n + m) + (north_of * p + south_of * q)) - here * a
            for a, n, m, p, q in zip(h, ahead_h, back(h, 2), up_h, down(h, 2))
        ]
        return change, ahead_h, up_h

    def gradients(h, ahead_h, up_h):
        east = [speed * (n - m) for n, m in zip(ahead_h, h)]
        north = [grad_p * n - grad_m * m for n, m in zip(up_h, h)]
        return east, north

    def tangent(state, coefs):
        h, u, v, q = state
        flow = divergence(u, v)
        for _ in range(STEPS):
            change, ahead_h, up_h = spread(h)
            east, north = gradients(h, ahead_h, up_h)
            u, v = [a - b for a, b in zip(u, east)], [a - b for a, b in zip(v, north)]
            flow = [a - b for a, b in zip(flow, change)]
            h = [a - b for a, b in zip(h, flow)]
            q = [
                stay * a + (em * e + ep * w) + (nm * n + np * s) + couple * p
                for a, em, e, ep, w, nm, n, np, s, p in zip(
                    q, coefs[0], ahead(q, 1), coefs[1], back(q, 1), coefs[2], up(q, 1), coefs[3], down(q, 1), h
                )
            ]
        return [h, u, v, q]

    def adjoint(state, coefs):
        h, u, v, q = state
        flow = divergence(u, v)
        for _ in range(STEPS):
            h = [a + couple * b for a, b in zip(h, q)]
            change, ahead_h, up_h = spread(h)
            east, north = gradients(h, ahead_h, up_h)
            u, v = [a + b for a, b in zip(u, east)], [a + b for a, b in zip(v, north)]
            flow = [a + b for a, b in zip(flow, change)]
            h = [a + b for a, b in zip(h, flow)]
            e = ahead([a * b for a, b in zip(coefs[1], q)], 1)
            w = back([a * b for a, b in zip(coefs[0], q)], 1)
            n = up([a * b for a, b in zip(coefs[3], q)], 1)
            s = down([a * b for a, b in zip(coefs[2], q)], 1)
            q = [stay * a + (b + c) + (d + f) for a, b, c, d, f in zip(q, e, w, n, s)]
        return [h, u, v, q]

    def each(fn, *states):
        return [[fn(*vals) for vals in zip(*xs)] for xs in zip(*states)]

    def operate(p, p_wide, precision, observed):
        weighted = []
        for t in range(subwins):
            change = p[t]
            if t > 0:
                moved = tangent(p[t - 1], narrow) if p_wide is None else tangent(p_wide[t - 1], wide)
                if p_wide is not None:
                    moved = [narrowed(x) for x in moved]
                change = each(lambda a, b: a - b, change, moved)
            weighted.append(each(lambda a, b: a * b, precision[t], change))
        image = []
        for t in range(subwins):
            out = each(lambda w, o, d: w + o * d, weighted[t], observed[t], p[t])
            if t + 1 < subwins:
                moved = adjoint(weighted[t + 1], narrow)
                out = each(lambda a, b: a - b, out, moved)
            image.append(out)
        return image

    def flat(x):
        return [(c, v) for state in x for field in state for c, v in enumerate(field)]

    def total(terms):
        inner, edge = None, None
        for c, v in terms:
            if c < TILES - 1:
                inner = v if inner is None else inner + v
            else:
                edge = v if edge is None else edge + v
        both = inner + jnp.where(free, 0.0, edge)
        return jnp.sum(both, axis=(0, 1), keepdims=True)

    def dot(x, y):
        return total([(c, v * w) for (c, v), (_, w) in zip(x, y)])

    precision = [stag(fields_of(0, t, FIELDS)) for t in range(subwins)]
    observed = [stag(fields_of(1, t, FIELDS)) for t in range(subwins)]
    for member in range(2):
        plain = [fields_of(member, t, 0) for t in range(subwins)]
        b_wide = [
            stag([widened(x, e) for x, e in zip(plain[t], extras_of(member, t))]) for t in range(subwins - 1)
        ]
        b = [[narrowed(x) for x in state] for state in b_wide] + [stag(plain[-1])]
        one = operate(b, b_wide, precision, observed)
        two = operate(one, None, precision, observed)
        one, two = [[[aligned(f, x) for f, x in enumerate(state)] for state in y] for y in (one, two)]
        f0, f1, f2 = flat(plain), flat(one), flat(two)
        s00, s01, s11, s02, s12 = dot(f0, f0), dot(f0, f1), dot(f1, f1), dot(f0, f2), dot(f1, f2)
        step = jnp.where(s11 > 0.0, s01 / jnp.where(s11 > 0.0, s11, 1.0), 0.0)
        more = 2.0 - jnp.where(s00 > 0.0, step * s01 / jnp.where(s00 > 0.0, s00, 1.0), 0.0)
        step_t = jnp.broadcast_to(step, (ROWS, LANES))
        more_t = jnp.broadcast_to(more, (ROWS, LANES))
        res = [(c, v - step_t * w) for (c, v), (_, w) in zip(f0, f1)]
        mov = [(c, more_t * v - step_t * w) for (c, v), (_, w) in zip(f0, f1)]
        img = [(c, more_t * v - step_t * w) for (c, v), (_, w) in zip(f1, f2)]
        sums = [step, more, s00, s01, s11, s02, s12, dot(res, res), dot(mov, img)]
        sums += [sums[-1]] * (-len(sums) % 6)
        for t in range(subwins):

            def put(k, value):
                start = (member * subwins + t) * ROWS * ROWS_OUT + k
                out_ref[pl.ds(start, ROWS, stride=ROWS_OUT), :] = value

            images = one[t] + two[t]
            last = images[-1][TILES - 1]
            for k, x in enumerate(images):
                put(2 * k, x[0])
                put(2 * k + 1, x[1])
                if k < 5:
                    put(THIRDS + k, jnp.where(free, pltpu.roll(last, (-(k + 1) * FREE) % LANES, 1), x[2]))
                elif k < 2 * FIELDS - 1:
                    rows = []
                    for i in (k - 5, k - 3):
                        value = sums[3 * i + 2]
                        for j in (1, 0):
                            value = jnp.where(lane < free_lo + (j + 1) * SLOT, sums[3 * i + j], value)
                        rows.append(value)
                    put(THIRDS + k, jnp.where(free, jnp.where(row % 2 == 0, rows[0], rows[1]), x[2]))


def finish_kernel(lon, merges, b_row_ref, in_ref, x_hbm, r_hbm, x_ref, r_ref, x_row_ref, r_row_ref, sems):
    _, levels, share, _ = x_ref.shape
    full = lon // LANES
    rest = lon - full * LANES
    size = share * ROWS_OUT
    apart = merges[0] - merges[1]
    at_lane = merges[0] - 3 * REACH
    group = ROWS // share

    slots = []
    for i in range(3):
        at = THIRDS + 5 + i % 2 + (i // 2) * ROWS_OUT
        halves = [in_ref[pl.ds(half * levels * size + at, levels, stride=size), :] for half in range(2)]
        slots.append(jnp.concatenate([halves[0], pltpu.roll(halves[1], apart, 1)], axis=0))

    def sums(i):
        value = slots[i // 3]
        return pltpu.roll(value, LANES - (i % 3) * SLOT, 1) if i % 3 else value

    step, more, s00, s01, s11, s02, s12, rr, mi = [sums(i) for i in range(9)]

    def total(x):
        return jnp.sum(x, axis=0, keepdims=True)

    norm_0 = total(s00)
    alpha_0 = norm_0 / total(s01)
    d = step - alpha_0
    norm_1 = total(rr + d * (2.0 * (s01 - step * s11) + d * s11))
    beta = norm_1 / norm_0
    g = (1.0 + beta) - more
    cross_d = more * (s02 + s11) - 2.0 * step * s12
    cross_g = 2.0 * more * s01 - step * (s11 + s02)
    curve = total(mi + d * (cross_d + d * s12 + g * (s11 + s02)) + g * (cross_g + g * s01))
    alpha_1 = norm_1 / curve
    first = alpha_0 + alpha_1 * (1.0 + beta)
    second = alpha_0 * alpha_1
    first = jnp.broadcast_to(first[:, at_lane : at_lane + 1], (ROWS, LANES))
    second = jnp.broadcast_to(second[:, at_lane : at_lane + 1], (ROWS, LANES))
    lane = lax.broadcasted_iota(jnp.int32, (ROWS, LANES), 1)

    def tiles_of(g, k):
        halves = []
        for half in range(2):
            start = (half * levels + g * group) * size

            def rows(j):
                return in_ref[pl.ds(start + j, ROWS, stride=ROWS_OUT), :]

            if k < 2 * FIELDS - 1:
                third = rows(THIRDS + k)
            else:
                third = None
                for i in range(5):
                    part = pltpu.roll(rows(THIRDS + i), (i + 1) * FREE % LANES, 1)
                    begin = (merges[half] - 3 * REACH + (i + 1) * FREE) % LANES
                    here = jnp.logical_and(lane >= begin, lane < begin + FREE)
                    third = part if third is None else jnp.where(here, part, third)
            halves.append([rows(2 * k), rows(2 * k + 1), third])
        middle = jnp.where(lane < at_lane, halves[0][2], halves[1][2])
        return halves[0][:2] + [middle] + halves[1]

    copies = []

    def send(i, f, row_ref, ref, hbm):
        for level in range(levels):
            ref[f, level] = row_ref[f, pl.ds(level * share, share), pl.ds(0, lon)]
        copies.append(pltpu.make_async_copy(ref.at[f], hbm.at[f], sems.at[i, f]))
        copies[-1].start()

    for f in reversed(range(FIELDS)):
        for g in range(levels // group):
            for c, (one, two) in enumerate(zip(tiles_of(g, f), tiles_of(g, FIELDS + f))):
                at = f, pl.ds(g * ROWS, ROWS), pl.ds(c * LANES, LANES)
                b = b_row_ref[at]
                x_row_ref[at] = first * b - second * one
                r_row_ref[at] = b + (second * two - first * one)
        send(0, f, x_row_ref, x_ref, x_hbm)
        send(1, f, r_row_ref, r_ref, r_hbm)
    for copy in copies:
        copy.wait()


def by_layer(right_side, error_precision, obs_count, background_wind, wave_speed, tracer_coupling):
    _, fields, levels, share, lon = right_side.shape
    subwins = lax.axis_size("tm")
    merges = merge_lanes(lon)
    vmem = pl.BlockSpec(memory_space=pltpu.VMEM)
    hbm = pl.BlockSpec(memory_space=pltpu.HBM)
    params = pltpu.CompilerParams(vmem_limit_bytes=48 * 1024 * 1024)
    state = (fields, levels, share, lon)
    wide = (lon // LANES + 1) * LANES

    def exchange(x):
        x = x.reshape(2 * levels, -1, 1, LANES)
        return lax.all_to_all(x, ("ens", "tm", "space"), 0, 0, tiled=True).reshape(-1, LANES)

    b = right_side.reshape(state)
    given = (b, error_precision.reshape(state), obs_count.reshape(state), background_wind, wave_speed, tracer_coupling)
    with jax.named_scope("pack"):
        packed, b_rows = pl.pallas_call(
            lambda *refs: pack_kernel(lon, merges, *refs),
            out_shape=[
                jax.ShapeDtypeStruct((2 * levels * share * ROWS_IN, LANES), jnp.float32),
                jax.ShapeDtypeStruct((fields, levels * share, wide), jnp.float32),
            ],
            in_specs=[hbm] * len(given),
            out_specs=[vmem] * 2,
            scratch_shapes=[
                pltpu.VMEM(state, jnp.float32),
                pltpu.VMEM(state, jnp.float32),
                pltpu.VMEM(state, jnp.int32),
                pltpu.VMEM(background_wind.shape[1:], jnp.float32),
                pltpu.SMEM(wave_speed.shape, jnp.float32),
                pltpu.SMEM(tracer_coupling.shape, jnp.float32),
                pltpu.VMEM((fields, levels * share, wide), jnp.float32),
                pltpu.VMEM((levels * share, wide), jnp.float32),
                pltpu.SemaphoreType.DMA((len(given),)),
            ],
            compiler_params=params,
        )(*[pltpu.with_memory_space_constraint(x, pltpu.HBM) for x in given])
    packed = exchange(packed)
    with jax.named_scope("layer"):
        images = pl.pallas_call(
            lambda *refs: layer_kernel(lon, merges, subwins, *refs),
            out_shape=jax.ShapeDtypeStruct((2 * levels * share * ROWS_OUT, LANES), jnp.float32),
            in_specs=[vmem],
            out_specs=vmem,
            compiler_params=params,
        )(packed)
    images = exchange(images)
    with jax.named_scope("finish"):
        x, r = pl.pallas_call(
            lambda *refs: finish_kernel(lon, merges, *refs),
            out_shape=[jax.ShapeDtypeStruct(state, jnp.float32)] * 2,
            in_specs=[vmem] * 2,
            out_specs=[hbm] * 2,
            scratch_shapes=[
                pltpu.VMEM(state, jnp.float32),
                pltpu.VMEM(state, jnp.float32),
                pltpu.VMEM((fields, levels * share, wide), jnp.float32),
                pltpu.VMEM((fields, levels * share, wide), jnp.float32),
                pltpu.SemaphoreType.DMA((2, FIELDS)),
            ],
            compiler_params=params,
        )(b_rows, images)
    return x.reshape(right_side.shape), r.reshape(right_side.shape)


def fits_by_layer(mesh, shape):
    space, tm, ens = mesh.shape["space"], mesh.shape["tm"], mesh.shape["ens"]
    subwins, fields, levels, lats, lon = shape
    return (
        (ens, tm, space, fields, lats) == (2, 4, 4, FIELDS, ROWS)
        and subwins == ens * tm
        and levels == space * tm
        and lon == 720
    )


def extended_2(cells, sides, width):
    for axis, dim in sides:
        count = lax.axis_size(axis)
        ends = count - 1
        head = lax.slice_in_dim(cells, 0, width, axis=dim)
        tail = lax.slice_in_dim(cells, cells.shape[dim] - width, cells.shape[dim], axis=dim)
        cells = jnp.concatenate(
            [
                lax.ppermute(tail, axis, [(i, (i + 1) % count) for i in range(ends)]),
                cells,
                lax.ppermute(head, axis, [((i + 1) % count, i) for i in range(ends)]),
            ],
            axis=dim,
        )
    return cells


def shifted(value, axis, by):
    peers = lax.axis_size(axis)
    pairs = [(i, i + by) for i in range(peers) if 0 <= i + by < peers]
    return lax.ppermute(value, axis, pairs)


def along_x(field):
    return 0.5 * (jnp.roll(field, -1, axis=-1) - jnp.roll(field, 1, axis=-1))


def second_x(field):
    return jnp.roll(field, -1, axis=-1) + jnp.roll(field, 1, axis=-1) - 2.0 * field


def along_y(extended):
    return 0.5 * (extended[..., 2:, :] - extended[..., :-2, :])


def trimmed(field, count):
    if count == 0:
        return field
    return field[..., count : field.shape[-2] - count, :]


def row_valid(lat_rows):
    first_row = lax.axis_index("space") * lat_rows - 4
    row_total = lat_rows * lax.axis_size("space")
    global_rows = first_row + jnp.arange(lat_rows + 8, dtype=jnp.int32)
    inside = jnp.logical_and(global_rows >= 0, global_rows < row_total)
    return inside.astype(jnp.float32)[:, None]


def tangent_core(state, margin, coefs):
    speed_col, couple_col, winds, have, valid = coefs
    height, east, north, tracer = (state[:, 0], state[:, 1], state[:, 2], state[:, 3])
    east_mid = east - speed_col * along_x(height)
    north_mid = (trimmed(north, 1) - speed_col * along_y(height)) * trimmed(valid, 5 - margin)
    height_new = trimmed(height, 2) - speed_col * (
        along_x(trimmed(east_mid, 2)) + along_y(north_mid)
    )
    tracer_one = trimmed(tracer, 1)
    inner = trimmed(tracer, 2)
    tracer_lap = second_x(inner) + tracer_one[..., 2:, :] + tracer_one[..., :-2, :] - 2.0 * inner
    wind_east = trimmed(winds[0], have - margin + 2)
    wind_north = trimmed(winds[1], have - margin + 2)
    tracer_new = (
        inner
        - wind_east * along_x(inner)
        - wind_north * along_y(tracer_one)
        + diffusion * tracer_lap
        + couple_col * height_new
    )
    result = jnp.stack(
        [height_new, trimmed(east_mid, 2), trimmed(north_mid, 1), tracer_new], axis=1
    )
    return result * trimmed(valid, 6 - margin)


def adjoint_core(state, margin, coefs):
    speed_col, couple_col, winds, have, valid = coefs
    height, east, north, tracer = (state[:, 0], state[:, 1], state[:, 2], state[:, 3])
    height_mix = height + couple_col * tracer
    east_mid = east + speed_col * along_x(height_mix)
    north_mid = (trimmed(north, 1) + speed_col * along_y(height_mix)) * trimmed(valid, 5 - margin)
    height_new = trimmed(height_mix, 2) + speed_col * (
        along_x(trimmed(east_mid, 2)) + along_y(north_mid)
    )
    tracer_one = trimmed(tracer, 1)
    inner = trimmed(tracer, 2)
    tracer_lap = second_x(inner) + tracer_one[..., 2:, :] + tracer_one[..., :-2, :] - 2.0 * inner
    wind_east = trimmed(winds[0], have - margin + 2)
    wind_north = trimmed(winds[1], have - margin + 1)
    tracer_new = (
        inner
        + along_x(wind_east * inner)
        + along_y(wind_north * tracer_one)
        + diffusion * tracer_lap
    )
    result = jnp.stack(
        [height_new, trimmed(east_mid, 2), trimmed(north_mid, 1), tracer_new], axis=1
    )
    return result * trimmed(valid, 6 - margin)


def rebuild(state, sent):
    widths = [(0, 0)] * (state.ndim - 3) + [(2, 2), (0, 0)]
    east_wide = jnp.pad(state[:, 1], widths)
    return jnp.stack([sent[:, 0], east_wide, sent[:, 1], sent[:, 2]], axis=1)


def tangent_near(state):
    picked = jnp.stack([state[:, 0], state[:, 2], state[:, 3]], axis=1)
    sent = extended_2(picked, (("space", 3),), 2)
    return rebuild(state, sent)


def adjoint_near(state):
    picked = jnp.stack([state[:, 0], state[:, 2], state[:, 3]], axis=1)
    sent = extended_2(picked, (("space", 3),), 2)
    return rebuild(state, sent)


def propagate(fields, step_core, near_fn, coefs):
    current = fields
    for step in range(STEPS):
        current = step_core(near_fn(current), 2, coefs)
    return current


def operate(direction, error_precision, observed, coefs):
    moved = propagate(direction, tangent_core, tangent_near, coefs)
    incoming = shifted(moved, "tm", 1)
    previous = jnp.concatenate([incoming, moved[:-1]], axis=0)
    weighted = error_precision * (direction - previous)
    back = propagate(weighted, adjoint_core, adjoint_near, coefs)
    arriving = shifted(back, "tm", -1)
    following = jnp.concatenate([back[1:], arriving], axis=0)
    return weighted - following + observed * direction


def squares(residual):
    return lax.psum(jnp.sum(residual * residual), ("space", "tm"))


def on_device(right_side, error_precision, obs_count, background_wind, wave_speed, tracer_coupling):
    lat_rows = right_side.shape[3]
    valid = row_valid(lat_rows)
    winds = extended_2(background_wind, (("space", 2),), 1)
    have = 1
    coefs = (wave_speed[:, None, None], tracer_coupling[:, None, None], winds, have, valid)
    observed = obs_count.astype(jnp.float32)
    solution_field = jnp.zeros_like(right_side)
    residual = right_side
    direction = right_side
    norm_now = squares(residual)
    for step in range(ITERS):
        image = operate(direction, error_precision, observed, coefs)
        alpha = norm_now / lax.psum(jnp.sum(direction * image), ("space", "tm"))
        solution_field = solution_field + alpha * direction
        residual = residual - alpha * image
        norm_next = squares(residual)
        direction = residual + norm_next / norm_now * direction
        norm_now = norm_next
    return (solution_field, residual)


def solution(mesh):
    def run(right_side, *others):
        body = by_layer if fits_by_layer(mesh, right_side.shape) else on_device
        return jax.shard_map(
            body,
            mesh=mesh,
            in_specs=(
                P(("ens", "tm"), None, None, "space", None),
                P("tm", None, None, "space", None),
                P("tm", None, None, "space", None),
                P(None, None, "space", None),
                P(),
                P(),
            ),
            out_specs=(
                P(("ens", "tm"), None, None, "space", None),
                P(("ens", "tm"), None, None, "space", None),
            ),
            check_vma=False,
        )(right_side, *others)

    return run
```

```python
import jax
import jax.numpy as jnp
from jax import lax
from jax.experimental import pallas as pl
from jax.experimental.pallas import tpu as pltpu
from jax.sharding import PartitionSpec as P

STEPS = 2
ITERS = 2


diffusion = 0.1


LANES = 128
ROWS = 8
TILES = 3
REACH = 4
FIELDS = 4
SLOT = 2 * REACH
WINDS = LANES - FIELDS * SLOT
FREE = 6 * REACH
MIXED = 2 * FIELDS * TILES
ROWS_IN = MIXED + 1
THIRDS = 4 * FIELDS
ROWS_OUT = THIRDS + 2 * FIELDS - 1


def merge_lanes(lon):
    core = lon // 2
    return (core + 3 * REACH) % LANES, (core - 3 * REACH) % LANES


def pack_kernel(
    lon, merges, b_hbm, e_hbm, o_hbm, w_hbm, speed_hbm, couple_hbm, out_ref, b_row_ref,
    b_ref, e_ref, o_ref, w_ref, speed_ref, couple_ref, s_row_ref, w_row_ref, sems,
):
    _, levels, share, _ = b_ref.shape
    full = lon // LANES
    rest = lon - full * LANES
    member = lax.axis_index("ens")
    turn = lax.axis_index("tm") * 2 + member
    comp = jnp.where(turn < 2 * TILES, turn // TILES, turn - 2 * TILES)

    copy_b = pltpu.make_async_copy(b_hbm, b_ref, sems.at[0])
    copy_e = pltpu.make_async_copy(e_hbm, e_ref, sems.at[1])
    copy_o = pltpu.make_async_copy(o_hbm, o_ref, sems.at[2])
    others = (
        pltpu.make_async_copy(w_hbm.at[comp], w_ref, sems.at[3]),
        pltpu.make_async_copy(speed_hbm, speed_ref, sems.at[4]),
        pltpu.make_async_copy(couple_hbm, couple_ref, sems.at[5]),
    )
    copy_b.start()
    pl.when(member == 0)(copy_e.start)
    pl.when(member != 0)(copy_o.start)
    for copy in others:
        copy.start()
    lane = lax.broadcasted_iota(jnp.int32, (ROWS, LANES), 1)
    row = lax.broadcasted_iota(jnp.int32, (ROWS, LANES), 0)
    group = ROWS // share

    def stage(copy, ref, row_ref):
        copy.wait()
        for f in range(FIELDS):
            for level in range(levels):
                row_ref[f, pl.ds(level * share, share), pl.ds(0, lon)] = ref[f, level].astype(jnp.float32)

    def place(half, g, k):
        return pl.ds((half * levels + g * group) * share * ROWS_IN + k, ROWS, stride=ROWS_IN), slice(None)

    def windows(first, third, last):
        before = pltpu.roll(last, LANES - rest, 1)
        after = jnp.where(lane < rest, last, pltpu.roll(first, rest, 1))
        ends = ((third, before), (after, third))
        merged = [jnp.where(lane < m, x, y) for m, (x, y) in zip(merges, ends)]
        extra = [jnp.where(lane < m, y, x) for m, (x, y) in zip(merges, ends)]
        return merged, extra

    def put(g, k, row_ref, f):
        tiles = [row_ref[f, pl.ds(g * ROWS, ROWS), pl.ds(c * LANES, LANES)] for c in range(full + 1)]
        merged, extra = windows(tiles[0], tiles[2], tiles[5])
        for half in range(2):
            for c, value in enumerate(tiles[TILES * half : TILES * half + 2] + [merged[half]]):
                out_ref[place(half, g, k + c)] = value
        return extra

    def by_level(ref, g):
        value = jnp.full((ROWS, LANES), ref[g * group], jnp.float32)
        for i in range(1, group):
            value = jnp.where(row < i * share, value, ref[g * group + i])
        return value

    stage(copy_b, b_ref, b_row_ref)
    pl.when(member == 0)(lambda: stage(copy_e, e_ref, s_row_ref))
    pl.when(member != 0)(lambda: stage(copy_o, o_ref, s_row_ref))
    for copy in others:
        copy.wait()
    for level in range(levels):
        w_row_ref[pl.ds(level * share, share), pl.ds(0, lon)] = w_ref[level]
    for g in range(levels // group):
        mixed = [None, None]
        for f in range(FIELDS):
            extra = put(g, f * TILES, b_row_ref, f)
            for half, m in enumerate(merges):
                at = WINDS + f * SLOT
                moved = pltpu.roll(extra[half], (at - (m - REACH)) % LANES, 1)
                mixed[half] = moved if f == 0 else jnp.where(lane < at, mixed[half], moved)
        tiles = [w_row_ref[pl.ds(g * ROWS, ROWS), pl.ds(c * LANES, LANES)] for c in range(full + 1)]
        merged, extra = windows(tiles[0], tiles[2], tiles[5])
        speed, couple = by_level(speed_ref, g), by_level(couple_ref, g)
        for half, m in enumerate(merges):
            parts = tiles[TILES * half : TILES * half + 2] + [merged[half]]
            wind, left = parts[TILES - 1], pltpu.roll(parts[TILES - 1], LANES - SLOT * FIELDS, 1)
            for c in reversed(range(TILES - 1)):
                wind = jnp.where(jnp.logical_or(turn == c, turn == TILES + c), parts[c], wind)
                by = (c + 1) * SLOT * FIELDS
                left = jnp.where(lane < by, pltpu.roll(parts[c], by, 1), left)
            wind = jnp.where(turn < 2 * TILES, wind, left)
            value = jnp.where(lane < WINDS, wind, mixed[half])
            value = jnp.where(lane == WINDS + SLOT, speed, value)
            value = jnp.where(lane == WINDS + 2 * SLOT - 1, couple, value)
            ends = pltpu.roll(extra[half], LANES - 1 - m, 1)
            value = jnp.where(lane >= LANES - 2, ends, value)
            out_ref[place(half, g, MIXED)] = value

    for g in range(levels // group):
        for f in range(FIELDS):
            put(g, (FIELDS + f) * TILES, s_row_ref, f)


def layer_kernel(lon, merges, subwins, in_ref, out_ref):
    half = lax.axis_index("ens")
    lane = lax.broadcasted_iota(jnp.int32, (ROWS, LANES), 1)
    row = lax.broadcasted_iota(jnp.int32, (ROWS, LANES), 0)
    below = lane < jnp.where(half == 0, merges[0], merges[1])
    free_lo = jnp.where(half == 0, merges[0] - 3 * REACH, merges[1] - 3 * REACH)
    free = jnp.logical_and(lane >= free_lo, lane < free_lo + FREE)

    def load(member, t, k):
        return in_ref[pl.ds((member * subwins + t) * ROWS * ROWS_IN + k, ROWS, stride=ROWS_IN), :]

    def of_half(values):
        return jnp.where(half == 0, values[0] % LANES, values[1] % LANES)

    mixed = [[load(member, t, MIXED) for t in range(subwins)] for member in range(2)]
    speed_at, couple_at = WINDS + SLOT, WINDS + 2 * SLOT - 1
    speed = 0.5 * jnp.broadcast_to(mixed[0][0][:, speed_at : speed_at + 1], (ROWS, LANES))
    couple = jnp.broadcast_to(mixed[0][0][:, couple_at : couple_at + 1], (ROWS, LANES))

    def back(x, by):
        moved = [pltpu.roll(v, by, 1) for v in x]
        return [jnp.where(lane < by, moved[i - 1], v) for i, v in enumerate(moved)]

    def ahead(x, by):
        moved = [pltpu.roll(v, LANES - by, 1) for v in x]
        return [jnp.where(lane >= LANES - by, moved[(i + 1) % len(x)], v) for i, v in enumerate(moved)]

    def up(x, by):
        return [pltpu.roll(v, ROWS - by, 0) for v in x]

    def down(x, by):
        return [pltpu.roll(v, by, 0) for v in x]

    def staggered(f, x):
        if f == 1:
            return ahead(x, 1)
        if f == 2:
            return up(x, 1)
        return x

    def aligned(f, x):
        if f == 1:
            return back(x, 1)
        if f == 2:
            return down(x, 1)
        return x

    def widened(x, extra):
        return x[:2] + [jnp.where(below, x[2], extra), jnp.where(below, extra, x[2])]

    def narrowed(x):
        return x[:2] + [jnp.where(below, x[2], x[3])]

    def fields_of(member, t, at):
        return [[load(member, t, (at + f) * TILES + c) for c in range(TILES)] for f in range(FIELDS)]

    def extras_of(member, t):
        shifts = [of_half([m - REACH - WINDS - f * SLOT for m in merges]) for f in range(FIELDS)]
        return [pltpu.roll(mixed[member][t], by, 1) for by in shifts]

    def stag(state):
        return [staggered(f, x) for f, x in enumerate(state)]

    def wind(comp):
        sent = [mixed[turn % 2][turn // 2] for turn in range(2 * subwins)]
        left = sent[2 * TILES + comp]
        tiles = []
        for c in range(TILES):
            by = WINDS - c * SLOT * FIELDS
            tiles.append(jnp.where(lane < WINDS, sent[comp * TILES + c], pltpu.roll(left, by, 1)))
        return tiles, pltpu.roll(sent[comp * TILES], of_half([m + 1 - LANES for m in merges]), 1)

    stay = 1.0 - 4.0 * diffusion
    grad_p = jnp.where(row == ROWS - 2, 0.0, speed)
    grad_m = jnp.where(row == ROWS - 1, 0.0, speed)
    before_p = jnp.where(row == 0, 0.0, speed)
    before_m = jnp.where(row == 1, 0.0, speed)
    div_p = jnp.where(row == ROWS - 1, 0.0, speed)
    div_m = jnp.where(row == 0, 0.0, speed)

    def coefficients(east, north):
        return (
            [diffusion - 0.5 * v for v in east],
            [diffusion + 0.5 * v for v in east],
            [jnp.where(row == ROWS - 1, 0.0, diffusion - 0.5 * v) for v in north],
            [jnp.where(row == 0, 0.0, diffusion + 0.5 * v) for v in north],
        )

    (east, east_extra), (north, north_extra) = wind(0), wind(1)
    narrow = coefficients(east, north)
    wide = coefficients(widened(east, east_extra), widened(north, north_extra))

    here = 2.0 * speed * speed + (div_p * grad_m + div_m * before_p)
    along, north_of, south_of = speed * speed, div_p * grad_p, div_m * before_m

    def divergence(u, v):
        return [
            speed * (a - b) + (div_p * c - div_m * d) for a, b, c, d in zip(u, back(u, 2), v, down(v, 2))
        ]

    def spread(h):
        ahead_h, up_h = ahead(h, 2), up(h, 2)
        change = [
            (along * (n + m) + (north_of * p + south_of * q)) - here * a
            for a, n, m, p, q in zip(h, ahead_h, back(h, 2), up_h, down(h, 2))
        ]
        return change, ahead_h, up_h

    def gradients(h, ahead_h, up_h):
        east = [speed * (n - m) for n, m in zip(ahead_h, h)]
        north = [grad_p * n - grad_m * m for n, m in zip(up_h, h)]
        return east, north

    def tangent(state, coefs):
        h, u, v, q = state
        flow = divergence(u, v)
        for _ in range(STEPS):
            change, ahead_h, up_h = spread(h)
            east, north = gradients(h, ahead_h, up_h)
            u, v = [a - b for a, b in zip(u, east)], [a - b for a, b in zip(v, north)]
            flow = [a - b for a, b in zip(flow, change)]
            h = [a - b for a, b in zip(h, flow)]
            q = [
                stay * a + (em * e + ep * w) + (nm * n + np * s) + couple * p
                for a, em, e, ep, w, nm, n, np, s, p in zip(
                    q, coefs[0], ahead(q, 1), coefs[1], back(q, 1), coefs[2], up(q, 1), coefs[3], down(q, 1), h
                )
            ]
        return [h, u, v, q]

    def adjoint(state, coefs):
        h, u, v, q = state
        flow = divergence(u, v)
        for _ in range(STEPS):
            h = [a + couple * b for a, b in zip(h, q)]
            change, ahead_h, up_h = spread(h)
            east, north = gradients(h, ahead_h, up_h)
            u, v = [a + b for a, b in zip(u, east)], [a + b for a, b in zip(v, north)]
            flow = [a + b for a, b in zip(flow, change)]
            h = [a + b for a, b in zip(h, flow)]
            e = ahead([a * b for a, b in zip(coefs[1], q)], 1)
            w = back([a * b for a, b in zip(coefs[0], q)], 1)
            n = up([a * b for a, b in zip(coefs[3], q)], 1)
            s = down([a * b for a, b in zip(coefs[2], q)], 1)
            q = [stay * a + (b + c) + (d + f) for a, b, c, d, f in zip(q, e, w, n, s)]
        return [h, u, v, q]

    def each(fn, *states):
        return [[fn(*vals) for vals in zip(*xs)] for xs in zip(*states)]

    def operate(p, p_wide, precision, observed):
        image = []
        for t in range(subwins):
            change = p[t]
            if t > 0:
                moved = tangent(p[t - 1], narrow) if p_wide is None else tangent(p_wide[t - 1], wide)
                if p_wide is not None:
                    moved = [narrowed(x) for x in moved]
                change = each(lambda a, b: a - b, change, moved)
            weighted = each(lambda a, b: a * b, precision[t], change)
            if t > 0:
                image[-1] = each(lambda a, b: a - b, image[-1], adjoint(weighted, narrow))
            image.append(weighted)
        return [each(lambda w, o, d: w + o * d, *x) for x in zip(image, observed, p)]

    def flat(x):
        return [(c, v) for state in x for field in state for c, v in enumerate(field)]

    def total(terms):
        inner, edge = None, None
        for c, v in terms:
            if c < TILES - 1:
                inner = v if inner is None else inner + v
            else:
                edge = v if edge is None else edge + v
        both = inner + jnp.where(free, 0.0, edge)
        return jnp.sum(both, axis=(0, 1), keepdims=True)

    def dot(x, y):
        return total([(c, v * w) for (c, v), (_, w) in zip(x, y)])

    precision = [stag(fields_of(0, t, FIELDS)) for t in range(subwins)]
    observed = [stag(fields_of(1, t, FIELDS)) for t in range(subwins)]
    for member in range(2):
        plain = [fields_of(member, t, 0) for t in range(subwins)]
        b_wide = [
            stag([widened(x, e) for x, e in zip(plain[t], extras_of(member, t))]) for t in range(subwins - 1)
        ]
        b = [[narrowed(x) for x in state] for state in b_wide] + [stag(plain[-1])]
        one = operate(b, b_wide, precision, observed)
        two = operate(one, None, precision, observed)
        one, two = [[[aligned(f, x) for f, x in enumerate(state)] for state in y] for y in (one, two)]
        f0, f1, f2 = flat(plain), flat(one), flat(two)
        s00, s01, s11, s02, s12 = dot(f0, f0), dot(f0, f1), dot(f1, f1), dot(f0, f2), dot(f1, f2)
        step = jnp.where(s11 > 0.0, s01 / jnp.where(s11 > 0.0, s11, 1.0), 0.0)
        more = 2.0 - jnp.where(s00 > 0.0, step * s01 / jnp.where(s00 > 0.0, s00, 1.0), 0.0)
        step_t = jnp.broadcast_to(step, (ROWS, LANES))
        more_t = jnp.broadcast_to(more, (ROWS, LANES))
        res = [(c, v - step_t * w) for (c, v), (_, w) in zip(f0, f1)]
        mov = [(c, more_t * v - step_t * w) for (c, v), (_, w) in zip(f0, f1)]
        img = [(c, more_t * v - step_t * w) for (c, v), (_, w) in zip(f1, f2)]
        sums = [step, more, s00, s01, s11, s02, s12, dot(res, res), dot(mov, img)]
        sums += [sums[-1]] * (-len(sums) % 6)
        for t in range(subwins):

            def put(k, value):
                start = (member * subwins + t) * ROWS * ROWS_OUT + k
                out_ref[pl.ds(start, ROWS, stride=ROWS_OUT), :] = value

            images = one[t] + two[t]
            last = images[-1][TILES - 1]
            for k, x in enumerate(images):
                put(2 * k, x[0])
                put(2 * k + 1, x[1])
                if k < 5:
                    put(THIRDS + k, jnp.where(free, pltpu.roll(last, (-(k + 1) * FREE) % LANES, 1), x[2]))
                elif k < 2 * FIELDS - 1:
                    rows = []
                    for i in (k - 5, k - 3):
                        value = sums[3 * i + 2]
                        for j in (1, 0):
                            value = jnp.where(lane < free_lo + (j + 1) * SLOT, sums[3 * i + j], value)
                        rows.append(value)
                    put(THIRDS + k, jnp.where(free, jnp.where(row % 2 == 0, rows[0], rows[1]), x[2]))


def finish_kernel(lon, merges, b_row_ref, in_ref, x_hbm, r_hbm, x_ref, r_ref, x_row_ref, r_row_ref, sems):
    _, levels, share, _ = x_ref.shape
    full = lon // LANES
    rest = lon - full * LANES
    size = share * ROWS_OUT
    apart = merges[0] - merges[1]
    at_lane = merges[0] - 3 * REACH
    group = ROWS // share

    slots = []
    for i in range(3):
        at = THIRDS + 5 + i % 2 + (i // 2) * ROWS_OUT
        halves = [in_ref[pl.ds(half * levels * size + at, levels, stride=size), :] for half in range(2)]
        slots.append(jnp.concatenate([halves[0], pltpu.roll(halves[1], apart, 1)], axis=0))

    def sums(i):
        value = slots[i // 3]
        return pltpu.roll(value, LANES - (i % 3) * SLOT, 1) if i % 3 else value

    step, more, s00, s01, s11, s02, s12, rr, mi = [sums(i) for i in range(9)]

    def total(x):
        return jnp.sum(x, axis=0, keepdims=True)

    norm_0 = total(s00)
    alpha_0 = norm_0 / total(s01)
    d = step - alpha_0
    norm_1 = total(rr + d * (2.0 * (s01 - step * s11) + d * s11))
    beta = norm_1 / norm_0
    g = (1.0 + beta) - more
    cross_d = more * (s02 + s11) - 2.0 * step * s12
    cross_g = 2.0 * more * s01 - step * (s11 + s02)
    curve = total(mi + d * (cross_d + d * s12 + g * (s11 + s02)) + g * (cross_g + g * s01))
    alpha_1 = norm_1 / curve
    first = alpha_0 + alpha_1 * (1.0 + beta)
    second = alpha_0 * alpha_1
    first = jnp.broadcast_to(first[:, at_lane : at_lane + 1], (ROWS, LANES))
    second = jnp.broadcast_to(second[:, at_lane : at_lane + 1], (ROWS, LANES))
    lane = lax.broadcasted_iota(jnp.int32, (ROWS, LANES), 1)

    def tiles_of(g, k):
        halves = []
        for half in range(2):
            start = (half * levels + g * group) * size

            def rows(j):
                return in_ref[pl.ds(start + j, ROWS, stride=ROWS_OUT), :]

            if k < 2 * FIELDS - 1:
                third = rows(THIRDS + k)
            else:
                third = None
                for i in range(5):
                    part = pltpu.roll(rows(THIRDS + i), (i + 1) * FREE % LANES, 1)
                    begin = (merges[half] - 3 * REACH + (i + 1) * FREE) % LANES
                    here = jnp.logical_and(lane >= begin, lane < begin + FREE)
                    third = part if third is None else jnp.where(here, part, third)
            halves.append([rows(2 * k), rows(2 * k + 1), third])
        middle = jnp.where(lane < at_lane, halves[0][2], halves[1][2])
        return halves[0][:2] + [middle] + halves[1]

    copies = []
    for f in range(FIELDS):
        for g in range(levels // group):
            for c, (one, two) in enumerate(zip(tiles_of(g, f), tiles_of(g, FIELDS + f))):
                at = f, pl.ds(g * ROWS, ROWS), pl.ds(c * LANES, LANES)
                b = b_row_ref[at]
                x_row_ref[at] = first * b - second * one
                r_row_ref[at] = b + (second * two - first * one)
            for level in range(g * group, (g + 1) * group):
                at = f, pl.ds(level * share, share), pl.ds(0, lon)
                x_ref[f, level] = x_row_ref[at]
                r_ref[f, level] = r_row_ref[at]
        for i, (src, dst) in enumerate(((x_ref, x_hbm), (r_ref, r_hbm))):
            copies.append(pltpu.make_async_copy(src.at[f], dst.at[f], sems.at[i, f]))
            copies[-1].start()
    for copy in copies:
        copy.wait()


def by_layer(right_side, error_precision, obs_count, background_wind, wave_speed, tracer_coupling):
    _, fields, levels, share, lon = right_side.shape
    subwins = lax.axis_size("tm")
    merges = merge_lanes(lon)
    vmem = pl.BlockSpec(memory_space=pltpu.VMEM)
    hbm = pl.BlockSpec(memory_space=pltpu.HBM)
    params = pltpu.CompilerParams(vmem_limit_bytes=48 * 1024 * 1024)
    state = (fields, levels, share, lon)
    wide = (lon // LANES + 1) * LANES

    def exchange(x):
        x = x.reshape(2 * levels, -1, 1, LANES)
        return lax.all_to_all(x, ("ens", "tm", "space"), 0, 0, tiled=True).reshape(-1, LANES)

    b = right_side.reshape(state)
    given = (b, error_precision.reshape(state), obs_count.reshape(state), background_wind, wave_speed, tracer_coupling)
    with jax.named_scope("pack"):
        packed, b_rows = pl.pallas_call(
            lambda *refs: pack_kernel(lon, merges, *refs),
            out_shape=[
                jax.ShapeDtypeStruct((2 * levels * share * ROWS_IN, LANES), jnp.float32),
                jax.ShapeDtypeStruct((fields, levels * share, wide), jnp.float32),
            ],
            in_specs=[hbm] * len(given),
            out_specs=[vmem] * 2,
            scratch_shapes=[
                pltpu.VMEM(state, jnp.float32),
                pltpu.VMEM(state, jnp.float32),
                pltpu.VMEM(state, jnp.int32),
                pltpu.VMEM(background_wind.shape[1:], jnp.float32),
                pltpu.SMEM(wave_speed.shape, jnp.float32),
                pltpu.SMEM(tracer_coupling.shape, jnp.float32),
                pltpu.VMEM((fields, levels * share, wide), jnp.float32),
                pltpu.VMEM((levels * share, wide), jnp.float32),
                pltpu.SemaphoreType.DMA((len(given),)),
            ],
            compiler_params=params,
        )(*[pltpu.with_memory_space_constraint(x, pltpu.HBM) for x in given])
    packed = exchange(packed)
    with jax.named_scope("layer"):
        images = pl.pallas_call(
            lambda *refs: layer_kernel(lon, merges, subwins, *refs),
            out_shape=jax.ShapeDtypeStruct((2 * levels * share * ROWS_OUT, LANES), jnp.float32),
            in_specs=[vmem],
            out_specs=vmem,
            compiler_params=params,
        )(packed)
    images = exchange(images)
    with jax.named_scope("finish"):
        x, r = pl.pallas_call(
            lambda *refs: finish_kernel(lon, merges, *refs),
            out_shape=[jax.ShapeDtypeStruct(state, jnp.float32)] * 2,
            in_specs=[vmem] * 2,
            out_specs=[hbm] * 2,
            scratch_shapes=[
                pltpu.VMEM(state, jnp.float32),
                pltpu.VMEM(state, jnp.float32),
                pltpu.VMEM((fields, levels * share, wide), jnp.float32),
                pltpu.VMEM((fields, levels * share, wide), jnp.float32),
                pltpu.SemaphoreType.DMA((2, FIELDS)),
            ],
            compiler_params=params,
        )(b_rows, images)
    return x.reshape(right_side.shape), r.reshape(right_side.shape)


def fits_by_layer(mesh, shape):
    space, tm, ens = mesh.shape["space"], mesh.shape["tm"], mesh.shape["ens"]
    subwins, fields, levels, lats, lon = shape
    return (
        (ens, tm, space, fields, lats) == (2, 4, 4, FIELDS, ROWS)
        and subwins == ens * tm
        and levels == space * tm
        and lon == 720
    )


def extended_2(cells, sides, width):
    for axis, dim in sides:
        count = lax.axis_size(axis)
        ends = count - 1
        head = lax.slice_in_dim(cells, 0, width, axis=dim)
        tail = lax.slice_in_dim(cells, cells.shape[dim] - width, cells.shape[dim], axis=dim)
        cells = jnp.concatenate(
            [
                lax.ppermute(tail, axis, [(i, (i + 1) % count) for i in range(ends)]),
                cells,
                lax.ppermute(head, axis, [((i + 1) % count, i) for i in range(ends)]),
            ],
            axis=dim,
        )
    return cells


def shifted(value, axis, by):
    peers = lax.axis_size(axis)
    pairs = [(i, i + by) for i in range(peers) if 0 <= i + by < peers]
    return lax.ppermute(value, axis, pairs)


def along_x(field):
    return 0.5 * (jnp.roll(field, -1, axis=-1) - jnp.roll(field, 1, axis=-1))


def second_x(field):
    return jnp.roll(field, -1, axis=-1) + jnp.roll(field, 1, axis=-1) - 2.0 * field


def along_y(extended):
    return 0.5 * (extended[..., 2:, :] - extended[..., :-2, :])


def trimmed(field, count):
    if count == 0:
        return field
    return field[..., count : field.shape[-2] - count, :]


def row_valid(lat_rows):
    first_row = lax.axis_index("space") * lat_rows - 4
    row_total = lat_rows * lax.axis_size("space")
    global_rows = first_row + jnp.arange(lat_rows + 8, dtype=jnp.int32)
    inside = jnp.logical_and(global_rows >= 0, global_rows < row_total)
    return inside.astype(jnp.float32)[:, None]


def tangent_core(state, margin, coefs):
    speed_col, couple_col, winds, have, valid = coefs
    height, east, north, tracer = (state[:, 0], state[:, 1], state[:, 2], state[:, 3])
    east_mid = east - speed_col * along_x(height)
    north_mid = (trimmed(north, 1) - speed_col * along_y(height)) * trimmed(valid, 5 - margin)
    height_new = trimmed(height, 2) - speed_col * (
        along_x(trimmed(east_mid, 2)) + along_y(north_mid)
    )
    tracer_one = trimmed(tracer, 1)
    inner = trimmed(tracer, 2)
    tracer_lap = second_x(inner) + tracer_one[..., 2:, :] + tracer_one[..., :-2, :] - 2.0 * inner
    wind_east = trimmed(winds[0], have - margin + 2)
    wind_north = trimmed(winds[1], have - margin + 2)
    tracer_new = (
        inner
        - wind_east * along_x(inner)
        - wind_north * along_y(tracer_one)
        + diffusion * tracer_lap
        + couple_col * height_new
    )
    result = jnp.stack(
        [height_new, trimmed(east_mid, 2), trimmed(north_mid, 1), tracer_new], axis=1
    )
    return result * trimmed(valid, 6 - margin)


def adjoint_core(state, margin, coefs):
    speed_col, couple_col, winds, have, valid = coefs
    height, east, north, tracer = (state[:, 0], state[:, 1], state[:, 2], state[:, 3])
    height_mix = height + couple_col * tracer
    east_mid = east + speed_col * along_x(height_mix)
    north_mid = (trimmed(north, 1) + speed_col * along_y(height_mix)) * trimmed(valid, 5 - margin)
    height_new = trimmed(height_mix, 2) + speed_col * (
        along_x(trimmed(east_mid, 2)) + along_y(north_mid)
    )
    tracer_one = trimmed(tracer, 1)
    inner = trimmed(tracer, 2)
    tracer_lap = second_x(inner) + tracer_one[..., 2:, :] + tracer_one[..., :-2, :] - 2.0 * inner
    wind_east = trimmed(winds[0], have - margin + 2)
    wind_north = trimmed(winds[1], have - margin + 1)
    tracer_new = (
        inner
        + along_x(wind_east * inner)
        + along_y(wind_north * tracer_one)
        + diffusion * tracer_lap
    )
    result = jnp.stack(
        [height_new, trimmed(east_mid, 2), trimmed(north_mid, 1), tracer_new], axis=1
    )
    return result * trimmed(valid, 6 - margin)


def rebuild(state, sent):
    widths = [(0, 0)] * (state.ndim - 3) + [(2, 2), (0, 0)]
    east_wide = jnp.pad(state[:, 1], widths)
    return jnp.stack([sent[:, 0], east_wide, sent[:, 1], sent[:, 2]], axis=1)


def tangent_near(state):
    picked = jnp.stack([state[:, 0], state[:, 2], state[:, 3]], axis=1)
    sent = extended_2(picked, (("space", 3),), 2)
    return rebuild(state, sent)


def adjoint_near(state):
    picked = jnp.stack([state[:, 0], state[:, 2], state[:, 3]], axis=1)
    sent = extended_2(picked, (("space", 3),), 2)
    return rebuild(state, sent)


def propagate(fields, step_core, near_fn, coefs):
    current = fields
    for step in range(STEPS):
        current = step_core(near_fn(current), 2, coefs)
    return current


def operate(direction, error_precision, observed, coefs):
    moved = propagate(direction, tangent_core, tangent_near, coefs)
    incoming = shifted(moved, "tm", 1)
    previous = jnp.concatenate([incoming, moved[:-1]], axis=0)
    weighted = error_precision * (direction - previous)
    back = propagate(weighted, adjoint_core, adjoint_near, coefs)
    arriving = shifted(back, "tm", -1)
    following = jnp.concatenate([back[1:], arriving], axis=0)
    return weighted - following + observed * direction


def squares(residual):
    return lax.psum(jnp.sum(residual * residual), ("space", "tm"))


def on_device(right_side, error_precision, obs_count, background_wind, wave_speed, tracer_coupling):
    lat_rows = right_side.shape[3]
    valid = row_valid(lat_rows)
    winds = extended_2(background_wind, (("space", 2),), 1)
    have = 1
    coefs = (wave_speed[:, None, None], tracer_coupling[:, None, None], winds, have, valid)
    observed = obs_count.astype(jnp.float32)
    solution_field = jnp.zeros_like(right_side)
    residual = right_side
    direction = right_side
    norm_now = squares(residual)
    for step in range(ITERS):
        image = operate(direction, error_precision, observed, coefs)
        alpha = norm_now / lax.psum(jnp.sum(direction * image), ("space", "tm"))
        solution_field = solution_field + alpha * direction
        residual = residual - alpha * image
        norm_next = squares(residual)
        direction = residual + norm_next / norm_now * direction
        norm_now = norm_next
    return (solution_field, residual)


def solution(mesh):
    def run(right_side, *others):
        body = by_layer if fits_by_layer(mesh, right_side.shape) else on_device
        return jax.shard_map(
            body,
            mesh=mesh,
            in_specs=(
                P(("ens", "tm"), None, None, "space", None),
                P("tm", None, None, "space", None),
                P("tm", None, None, "space", None),
                P(None, None, "space", None),
                P(),
                P(),
            ),
            out_specs=(
                P(("ens", "tm"), None, None, "space", None),
                P(("ens", "tm"), None, None, "space", None),
            ),
            check_vma=False,
        )(right_side, *others)

    return run
```
